32 devices in a mesh: dom: 8 (over z, y), rep: 4 (over x, core).
Axes of the slice: x: 2, y: 2, z: 4, core: 2. Of those that a mesh axis runs over, the one named last changes fastest.
Arguments:
- features: bfloat16 [4, 16384, 602], P('rep', 'dom'), may hold values from -6 to 6
- nbr_index: int32 [4, 3, 16384, 25], P('rep', None, 'dom'), may hold values from 0 to 2303, as said below
- nbr_mask: int32 [4, 3, 16384, 25], P('rep', None, 'dom'), may hold values from 0 to 1, as said below
- send_rows: int32 [4, 8, 8, 32], P('rep', 'dom'), may hold values from 0 to 2047
- send_count: int32 [4, 8, 8], P('rep', 'dom'), may hold values from 0 to 32, as said below
- labels: int32 [4, 128], P('rep', 'dom'), may hold values from 0 to 40
- seed_mask: int32 [4, 128], P('rep', 'dom'), may hold values from 0 to 1
- w_first: float32 [1204, 256], replicated, may hold values from -0.15625 to 0.15625
- w_rest: float32 [2, 512, 256], replicated, may hold values from -6 to 6
- w_head: float32 [256, 41], replicated, may hold values from -6 to 6
- biases: float32 [809], replicated, may hold values from -3 to 3
- stat_big: float32 [1204, 1204], P('rep'), as said below
- root_big: float32 [1204, 1204], P('rep'), as said below
- stat_mid: float32 [2, 512, 512], P(None, 'rep'), as said below
- root_mid: float32 [2, 512, 512], P(None, 'rep'), as said below
- stat_sq: float32 [4, 256, 256], P(None, 'rep'), as said below
- root_sq: float32 [4, 256, 256], replicated, as said below
- stat_hr: float32 [41, 41], replicated, as said below
- root_hr: float32 [41, 41], replicated, as said below
- bias_m: float32 [809], replicated, may hold values from -7.6293945e-06 to 7.6293945e-06
- bias_v: float32 [809], replicated, may hold values from 2.7506863e-16 to 1.1002745e-15
Outputs:
- loss_sum: float32 [], replicated
- seed_total: float32 [], replicated
- grad_norm: float32 [], replicated
- grad_first: float32 [1204, 256], P('rep')
- grad_rest: float32 [2, 512, 256], P(None, 'rep')
- grad_head: float32 [256, 41], P('rep')
- new_bias_m: float32 [809], replicated
- new_bias_v: float32 [809], replicated
- new_stat_big: float32 [1204, 1204], P('rep')
- new_stat_mid: float32 [2, 512, 512], P(None, 'rep')
- new_stat_sq: float32 [4, 256, 256], P(None, 'rep')
- new_stat_hr: float32 [41, 41], replicated
- new_first: float32 [1204, 256], P('rep')
- new_rest: float32 [2, 512, 256], P(None, 'rep')
- new_head: float32 [256, 41], P('rep')
- new_biases: float32 [809], replicated
- first_low: bfloat16 [1204, 256], P('rep')
- rest_low: bfloat16 [2, 512, 256], P(None, 'rep')
- head_low: bfloat16 [256, 41], P('rep')
The draws below stay inside these ranges and needn't reach their ends.
Inputs may be any that keep to these rules, and one draw needn't show every extreme that they name: `nbr_index`: a slot refers to an own row or to a slot s < send_count[b, q, p] of a sending partition q. `nbr_mask`: in layer one only the first 25 slots, in layers two and three only the first 10 slots may be valid; some nodes have no valid slot. `send_count`: zero from a partition to itself. `stat_big`: symmetric. `stat_mid`: symmetric. `stat_sq`: symmetric. `stat_hr`: symmetric. `root_big`: symmetric. `root_mid`: symmetric. `root_sq`: symmetric. `root_hr`: symmetric.
All inputs are finite; a program needn't handle non-finite values.
Results may differ from the reference program's by a relative error of at most 0.013.
Values may be sent and summed in bfloat16 or wider, within the bound.
A program may use at most 192 MiB of HBM per device.

```python
import math
import jax
import jax.numpy as jnp
from jax import lax

FIN = 602
H = 256
C = 41
FAN_ONE = 25
FAN_REST = 10
ND = 2048
SD = 16
CAP = 32
STEP = 5
MB = 4
NODES = 16384
SEEDS = 128
BIAS = 809
PARAMS = 581673
N_DOM = 8


clip_limit = 0.0001


def link_counts(key):
    drawn = jax.random.randint(key, (MB, N_DOM, N_DOM), max(CAP // 2, 1), CAP + 1)
    span = jnp.arange(N_DOM)
    nxt = span[None, :] == (span[:, None] + 1) % N_DOM
    same = span[None, :] == span[:, None]
    drawn = jnp.where(nxt[None], CAP, drawn)
    return jnp.where(same[None], 0, drawn).astype(jnp.int32)


def draw_send_count(key, part):
    return link_counts(key)


def draw_nbr_index(key, part):
    counts = link_counts(key)
    key = jax.random.fold_in(key, 7)
    keys = jax.random.split(key, 4)
    shape = (MB, 3, NODES, FAN_ONE)
    local = jax.random.randint(keys[0], shape, 0, ND)
    peer = jax.random.randint(keys[1], shape, 0, N_DOM)
    batch_ids = jnp.arange(MB)[:, None, None, None]
    owner = (jnp.arange(NODES) // ND)[None, None, :, None]
    avail = counts[batch_ids, peer, owner]
    slot = jax.random.randint(keys[2], shape, 0, 1 << 20) % jnp.maximum(avail, 1)
    pick = (jax.random.randint(keys[3], shape, 0, 2) == 1) & (avail > 0)
    return jnp.where(pick, ND + peer * CAP + slot, local).astype(jnp.int32)


def draw_nbr_mask(key, part):
    key = jax.random.fold_in(key, 11)
    keys = jax.random.split(key, 2)
    shape = (MB, 3, NODES, FAN_ONE)
    slots = jnp.arange(FAN_ONE)[None, None, None, :]
    fan = jnp.where(jnp.arange(3) == 0, FAN_ONE, FAN_REST)[None, :, None, None]
    live = jax.random.randint(keys[0], shape, 0, 10) < 9
    empty = jax.random.randint(keys[1], (MB, 3, NODES, 1), 0, 40) == 0
    return ((slots < fan) & live & jnp.logical_not(empty)).astype(jnp.int32)


def draw_seed_mask(key, part):
    key = jax.random.fold_in(key, 13)
    dom_pos = (jnp.arange(SEEDS) // SD)[None, :] * 1000 // (N_DOM - 1)
    rep_pos = jnp.arange(MB)[:, None] * 1000 // max(MB - 1, 1)
    level = 300 + 3 * (dom_pos + rep_pos) // 10
    return (jax.random.randint(key, (MB, SEEDS), 0, 1000) < level).astype(jnp.int32)


def sym_matrix(key, size, scale):
    keys = jax.random.split(key, 2)
    diag = jnp.exp(jax.random.uniform(keys[0], (size,), jnp.float32, 0.0, jnp.log(4.0)))
    off = jax.random.normal(keys[1], (size, size), jnp.float32) * (0.5 / size ** 0.5)
    off = (off + off.T) * 0.7071
    eye = jnp.eye(size, dtype=jnp.float32)
    return scale * (eye * diag[:, None] + (1.0 - eye) * off)


def unit():
    return clip_limit / PARAMS ** 0.5


def draw_stat_big(key, part):
    key = jax.random.fold_in(key, 21)
    return sym_matrix(key, 2 * FIN, H * unit() ** 2)


def draw_root_big(key, part):
    key = jax.random.fold_in(key, 22)
    return sym_matrix(key, 2 * FIN, ((2 * FIN) ** (-0.5) / unit()) ** 0.5)


def draw_stat_mid(key, part):
    key = jax.random.fold_in(key, 23)
    keys = jax.random.split(key, 2)
    return jnp.stack([sym_matrix(keys[i], 2 * H, H * unit() ** 2) for i in range(2)])


def draw_root_mid(key, part):
    key = jax.random.fold_in(key, 24)
    keys = jax.random.split(key, 2)
    return jnp.stack([sym_matrix(keys[i], 2 * H, (0.7071 / unit()) ** 0.5) for i in range(2)])


def draw_stat_sq(key, part):
    key = jax.random.fold_in(key, 25)
    keys = jax.random.split(key, 4)
    scales = [2 * FIN, 2 * H, 2 * H, C]
    return jnp.stack([sym_matrix(keys[i], H, scales[i] * unit() ** 2) for i in range(4)])


def draw_root_sq(key, part):
    key = jax.random.fold_in(key, 26)
    keys = jax.random.split(key, 4)
    spreads = [(2 * FIN) ** (-0.5), 0.7071, 0.7071, 1.4142]
    return jnp.stack([sym_matrix(keys[i], H, (spreads[i] / unit()) ** 0.5) for i in range(4)])


def draw_stat_hr(key, part):
    key = jax.random.fold_in(key, 27)
    return sym_matrix(key, C, H * unit() ** 2)


def draw_root_hr(key, part):
    key = jax.random.fold_in(key, 28)
    return sym_matrix(key, C, (1.4142 / unit()) ** 0.5)


def set_ends(array, rng, smallest, largest):
    index_at = [jax.random.randint(jax.random.fold_in(rng, axis), (), 0, length) for axis, length in enumerate(array.shape)]
    widest = array.shape.index(max(array.shape))
    neighbour = index_at[:widest] + [(index_at[widest] + 1) % array.shape[widest]] + index_at[widest + 1:]
    return array.at[tuple(index_at)].set(smallest).at[tuple(neighbour)].set(largest)


def steps_of(key, extent, cuts, least, high):
    loudness = 1.0
    for position, shards_of in cuts:
        heights = jax.random.uniform(jax.random.fold_in(jax.random.fold_in(key, 6), position), (shards_of,), jnp.float32, least / len(cuts), high / len(cuts))
        loudness = loudness * jnp.repeat(jnp.exp(heights), extent[position] // shards_of).reshape((-1,) + (1,) * (len(extent) - 1 - position))
    return loudness


def bell_draw(own_key, dims, scale, limit, pieces=(), kind=jnp.bfloat16):
    entries = scale * jax.random.normal(own_key, dims, jnp.float32)
    if pieces:
        entries = entries * steps_of(own_key, dims, pieces, -0.22, 0.18)
    return jnp.clip(entries, -limit, limit).astype(kind)


def setup_inputs(seed: int = 0) -> dict:
    streams_of = jax.random.split(jax.random.key(seed), 22)
    return {
        "features": bell_draw(streams_of[0], (MB, NODES, FIN), 1.0, 6.0, ((0, 4), (1, 8))),
        "nbr_index": draw_nbr_index(jax.random.fold_in(streams_of[21], 71), 0),
        "nbr_mask": draw_nbr_mask(jax.random.fold_in(streams_of[21], 71), 0),
        "send_rows": set_ends(jax.random.randint(streams_of[3], (MB, N_DOM, N_DOM, CAP), 0, ND), jax.random.fold_in(streams_of[3], 1), 0, ND - 1).astype(jnp.int32),
        "send_count": draw_send_count(jax.random.fold_in(streams_of[21], 71), 0),
        "labels": set_ends(jax.random.randint(streams_of[5], (MB, SEEDS), 0, C), jax.random.fold_in(streams_of[5], 1), 0, C - 1).astype(jnp.int32),
        "seed_mask": draw_seed_mask(jax.random.fold_in(streams_of[21], 71), 0),
        "w_first": bell_draw(streams_of[7], (2 * FIN, H), (2 * FIN) ** -0.5, 0.15625, (), jnp.float32),
        "w_rest": bell_draw(streams_of[8], (2, 2 * H, H), 0.7071, 6.0, (), jnp.float32),
        "w_head": bell_draw(streams_of[9], (H, C), 1.4142, 6.0, (), jnp.float32),
        "biases": bell_draw(streams_of[10], (BIAS,), 0.2, 3.0, (), jnp.float32),
        "stat_big": draw_stat_big(jax.random.fold_in(streams_of[21], 71), 0),
        "root_big": draw_root_big(jax.random.fold_in(streams_of[21], 71), 0),
        "stat_mid": draw_stat_mid(jax.random.fold_in(streams_of[21], 71), 0),
        "root_mid": draw_root_mid(jax.random.fold_in(streams_of[21], 71), 0),
        "stat_sq": draw_stat_sq(jax.random.fold_in(streams_of[21], 71), 0),
        "root_sq": draw_root_sq(jax.random.fold_in(streams_of[21], 71), 0),
        "stat_hr": draw_stat_hr(jax.random.fold_in(streams_of[21], 71), 0),
        "root_hr": draw_root_hr(jax.random.fold_in(streams_of[21], 71), 0),
        "bias_m": bell_draw(streams_of[19], (BIAS,), (0.00045 / PARAMS ** 0.5), 7.62939453125e-06, (), jnp.float32),
        "bias_v": jnp.clip(jnp.exp(jax.random.uniform(streams_of[20], (BIAS,), jnp.float32, math.log(2.750686291951341e-16), math.log(1.1002745167805364e-15))), 2.750686291951341e-16, 1.1002745167805364e-15),
    }


@jax.custom_vjp
def low(v):
    return lax.optimization_barrier(v.astype(jnp.bfloat16)).astype(jnp.float32)

@jax.custom_vjp
def low_back(v):
    return v

def low_keep(v):
    return (low(v), None)

def low_pass(kept, grad):
    return (grad,)

def back_keep(v):
    return (v, None)

def back_low(kept, grad):
    return (low(grad),)
low.defvjp(low_keep, low_pass)
low_back.defvjp(back_keep, back_low)
clip_limit = 0.0001
decay = 0.5
shampoo_rate = 1.0
beta_one = 0.9
beta_two = 0.999
bias_rate = 0.05
weight_decay = 0.01
adam_eps = 1e-08
norm_eps = 1e-06
highest = lax.Precision.HIGHEST

def activate(z):
    act = jax.nn.gelu(z, approximate=True)
    return act * lax.rsqrt(lax.optimization_barrier(jnp.sum(act * act, axis=-1, keepdims=True)) + norm_eps)

def neighbour_sum(args):
    table, nbr, mask = args
    return lax.optimization_barrier(jnp.sum(table[nbr] * mask[..., None], axis=1))

def layer(h, weight, bias, nbr, mask, rows, valid):
    width = h.shape[-1]
    hb = low(h)
    outgoing = jax.vmap(lambda block, picks: jnp.take(block, picks.reshape(-1), axis=0))(hb, rows)
    outgoing = outgoing.reshape(N_DOM, N_DOM, CAP, width) * valid[..., None]
    incoming = low_back(jnp.swapaxes(outgoing, 0, 1).reshape(N_DOM, N_DOM * CAP, width))
    table = jnp.concatenate([hb, incoming], axis=1)
    maskf = mask.astype(jnp.float32)
    gathered = lax.map(jax.checkpoint(neighbour_sum), (table, nbr, maskf))
    degree = jnp.maximum(lax.optimization_barrier(jnp.sum(maskf, axis=-1)), 1.0)[..., None]
    agg = low(low_back(gathered) / degree)
    joined = jnp.concatenate([hb, agg], axis=-1)
    z = low_back(jnp.einsum('dnk,kh->dnh', joined, low(weight), precision=highest) + bias)
    return activate(z)

def forward(params, features, nbr, mask, rows, counts, labels, seed_mask, total):
    w_first, w_rest, w_head, biases = params
    h = features.astype(jnp.float32).reshape(N_DOM, ND, FIN)
    valid = (jnp.arange(CAP)[None, None, :] < counts[:, :, None]).astype(jnp.float32)
    weights = (w_first, w_rest[0], w_rest[1])
    for level in range(3):
        h = layer(h, weights[level], biases[level * H:(level + 1) * H], nbr[level], mask[level], rows, valid)
    top = low(h[:, :SD])
    logits = low_back(jnp.einsum('dsh,hc->dsc', top, low(w_head), precision=highest) + biases[3 * H:])
    lse = jax.nn.logsumexp(logits, axis=-1)
    picked = jnp.take_along_axis(logits, labels[..., None], axis=-1)[..., 0]
    ce_sum = jnp.sum((lse - picked) * seed_mask)
    return (ce_sum / total, ce_sum)

def shampoo(grad, weight, left, left_root, right, right_root):
    new_left = decay * left + (1.0 - decay) * jnp.dot(grad, grad.T, precision=highest)
    new_right = decay * right + (1.0 - decay) * jnp.dot(grad.T, grad, precision=highest)
    step = jnp.dot(jnp.dot(left_root, grad, precision=highest), right_root, precision=highest)
    return (new_left, new_right, weight - shampoo_rate * step)

def reference(features, nbr_index, nbr_mask, send_rows, send_count, labels, seed_mask, w_first, w_rest, w_head, biases, stat_big, root_big, stat_mid, root_mid, stat_sq, root_sq, stat_hr, root_hr, bias_m, bias_v):
    params = (w_first, w_rest, w_head, biases)
    maskf = seed_mask.astype(jnp.float32)
    total = jnp.sum(maskf)
    grads = jax.tree.map(jnp.zeros_like, params)
    loss_sum = jnp.zeros((), jnp.float32)
    for batch in range(MB):
        nbr = nbr_index[batch].reshape(3, N_DOM, ND, FAN_ONE)
        mask = nbr_mask[batch].reshape(3, N_DOM, ND, FAN_ONE)
        lab = labels[batch].reshape(N_DOM, SD)
        smask = maskf[batch].reshape(N_DOM, SD)

        def objective(p):
            return forward(p, features[batch], nbr, mask, send_rows[batch], send_count[batch], lab, smask, total)
        value, pull, ce_sum = jax.vjp(objective, params, has_aux=True)
        part = pull(jnp.ones_like(value))[0]
        grads = jax.tree.map(lambda a, b: a + b, grads, part)
        loss_sum = loss_sum + ce_sum
    squares = sum((jnp.sum(g * g) for g in jax.tree.leaves(grads)))
    grad_norm = jnp.sqrt(squares)
    factor = clip_limit / jnp.maximum(grad_norm, clip_limit)
    g_first, g_rest, g_head, g_bias = jax.tree.map(lambda g: g * factor, grads)
    l_first, r_first, n_first = shampoo(g_first, w_first, stat_big, root_big, stat_sq[0], root_sq[0])
    l_mid0, r_mid0, n_mid0 = shampoo(g_rest[0], w_rest[0], stat_mid[0], root_mid[0], stat_sq[1], root_sq[1])
    l_mid1, r_mid1, n_mid1 = shampoo(g_rest[1], w_rest[1], stat_mid[1], root_mid[1], stat_sq[2], root_sq[2])
    l_head, r_head, n_head = shampoo(g_head, w_head, stat_sq[3], root_sq[3], stat_hr, root_hr)
    new_m = beta_one * bias_m + (1.0 - beta_one) * g_bias
    new_v = beta_two * bias_v + (1.0 - beta_two) * g_bias * g_bias
    m_hat = new_m / (1.0 - beta_one ** STEP)
    v_hat = new_v / (1.0 - beta_two ** STEP)
    new_b = biases - bias_rate * (m_hat / (jnp.sqrt(v_hat) + adam_eps) + weight_decay * biases)
    new_rest = jnp.stack([n_mid0, n_mid1])
    return (loss_sum, total, grad_norm, g_first, g_rest, g_head, new_m, new_v, l_first, jnp.stack([l_mid0, l_mid1]), jnp.stack([r_first, r_mid0, r_mid1, l_head]), r_head, n_first, new_rest, n_head, new_b, n_first.astype(jnp.bfloat16), new_rest.astype(jnp.bfloat16), n_head.astype(jnp.bfloat16))
```

```python
import functools

import jax
import jax.numpy as jnp
from jax import lax
from jax.experimental import pallas as pl
from jax.experimental.pallas import tpu as pltpu
from jax.sharding import PartitionSpec as P

STEP = 5
FAN_REST = 10

clip_limit = 0.0001
decay = 0.5
shampoo_rate = 1.0
beta_one = 0.9
beta_two = 0.999
bias_rate = 0.05
weight_decay = 0.01
adam_eps = 1e-08
norm_eps = 1e-06
MASKED = 8192

bf16 = jnp.bfloat16
f32 = jnp.float32
i32 = jnp.int32
MESH = pl.DeviceIdType.MESH


def nn(a, b):
    return jnp.dot(a, b, preferred_element_type=f32)


def nt(a, b):
    return lax.dot_general(a, b, (((1,), (1,)), ((), ())), preferred_element_type=f32)


def flip(a):
    return a.astype(f32).T.astype(a.dtype)


def round_up(a, b):
    return (a + b - 1) // b * b


def gelu_parts(z):
    scale = 0.7978845608028654
    square = z * z
    t = jnp.tanh(scale * (z + 0.044715 * (z * square)))
    half = 0.5 * (1.0 + t)
    act = z * half
    slope = half + 0.5 * z * (1.0 - t * t) * (scale * (1.0 + 3.0 * 0.044715 * square))
    root = lax.rsqrt(jnp.sum(act * act, axis=0, keepdims=True) + norm_eps)
    return act, slope, root


def pull_back(act, slope, root, grad):
    dot = jnp.sum(act * grad, axis=0, keepdims=True)
    return (slope * (root * grad - act * (root * root * root * dot))).astype(bf16)


def graph_kernel(
    peers, cap, seeds,
    c1, c2, c3, ids, col, lab, xt, w1, wr, wht, bias,
    g_out, s_out,
    joined, gathered, pick, chosen, far2, cblk, cinc, ctmp, crow, lrow, rdeg, lcode,
    w1t, act1, slope1, root1, h1t, ob0, ib0, obs, ibs, gl, rc, acc, sbuf, rx, ry, rz, gout,
    ssend, srecv, szv,
    send_sem, recv_sem, red_send, red_recv,
):
    fin, nodes = xt.shape
    hidden = w1.shape[1]
    finp = round_up(fin, 16)
    slots = peers * cap
    table = nodes + slots
    groups = table // 128
    span = ids.shape[1]
    local = span - slots
    me = lax.axis_index("dom")
    rep = lax.axis_index("rep")
    core = lax.rem(rep, 2)
    xpos = rep // 2
    ypos = lax.rem(me, 2)
    zpos = me // 2
    nz = peers // 2

    barrier = pltpu.get_barrier_semaphore()
    for off in range(1, peers):
        pl.semaphore_signal(barrier, inc=1, device_id={"dom": lax.rem(me + off, peers)}, device_id_type=MESH)
    mate_c = xpos * 2 + (1 - core)
    mate_x = (1 - xpos) * 2 + core
    for mate in (mate_c, mate_x):
        pl.semaphore_signal(barrier, inc=1, device_id={"rep": mate}, device_id_type=MESH)

    def exchange(stage, src, dst):
        copies = []
        for off in range(1, peers):
            peer = lax.rem(me + off, peers)
            copies.append(
                pltpu.make_async_remote_copy(
                    src_ref=src.at[pl.ds(pl.multiple_of(peer * cap, cap), cap)],
                    dst_ref=dst.at[pl.ds(pl.multiple_of(me * cap, cap), cap)],
                    send_sem=send_sem.at[stage, off - 1],
                    recv_sem=recv_sem.at[stage, off - 1],
                    device_id={"dom": peer},
                    device_id_type=MESH,
                )
            )
        for c in copies:
            c.start()
        return copies

    def finish(copies):
        for c in copies:
            c.wait()

    mine = pl.ds(pl.multiple_of(me * cap, cap), cap)

    pick[...] = jnp.where(
        col[...] == lax.broadcasted_iota(i32, (slots, nodes), 1), 1.0, 0.0
    ).astype(bf16)
    joined[finp - 16 : finp, :] = jnp.zeros((16, nodes), bf16)
    joined[0:fin, :] = xt[...]
    ob0[:, finp:] = jnp.zeros((slots, ob0.shape[1] - finp), bf16)
    ob0[:, 0:finp] = nt(pick[...], joined[0:finp, :]).astype(bf16)
    ib0[mine, :] = jnp.zeros((cap, ib0.shape[1]), bf16)
    for k in range(4):
        ibs[k, mine, :] = jnp.zeros((cap, hidden), bf16)
    pl.semaphore_wait(barrier, peers - 1 + 2)
    sent = exchange(0, ob0, ib0)

    wpad = jnp.concatenate(
        [w1[0:fin, :], jnp.zeros((finp - fin, hidden), f32), w1[fin : 2 * fin, :], jnp.zeros((finp - fin, hidden), f32)],
        axis=0,
    )
    w1t[...] = wpad.T.astype(bf16)
    w2 = wr[0].astype(bf16)
    w3 = wr[1].astype(bf16)
    bcol = bias[...].T

    def bias_col(level):
        return jnp.concatenate([bcol[:, 2 * level : 2 * level + 1], bcol[:, 2 * level + 1 : 2 * level + 2]], axis=0)

    pad = jnp.full((32 - c1.shape[0], 128), float(MASKED), f32)
    for c in range(nodes // 128):
        blk = jnp.concatenate([c1[:, c * 128 : (c + 1) * 128].astype(f32), pad], axis=0)
        ctmp[c * 128 : (c + 1) * 128, 0:32] = blk.T
    rdeg[0:1, :] = 1.0 / jnp.maximum(jnp.sum((c1[...] < MASKED).astype(f32), axis=0, keepdims=True), 1.0)
    ngroups = nodes // 8
    lane = lax.broadcasted_iota(i32, (ngroups, 256), 1)
    code = jnp.zeros((ngroups, 256), f32)
    for n in range(8):
        piece = ctmp[pl.ds(n, ngroups, stride=8), :]
        piece = jnp.concatenate([piece, piece], axis=1)
        piece = pltpu.roll(piece, n * 32, 1) if n else piece
        code = jnp.where((lane >> 5) == n, piece, code)
    code = code.astype(i32)
    crow[...] = ((code >> 7) * 8 + (lane >> 5)).astype(f32)
    lrow[...] = (code & 127).astype(f32)

    list_row = ids[0:1, :].astype(f32)

    def one_hot_rows(b, _):
        start = pl.multiple_of(b * 256, 256)
        row = (lax.broadcasted_iota(i32, (256, span), 0) + b * 256).astype(f32)
        chosen[pl.ds(start, 256), 0:span] = jnp.where(row == list_row, 1.0, 0.0).astype(bf16)
        return 0

    lax.fori_loop(0, nodes // 256, one_hot_rows, 0)
    code2 = c2[...]
    parts = jnp.concatenate([(code2 >> 7), (code2 & 127)], axis=0).astype(f32).astype(bf16)
    found = nn(parts, chosen[:, 0:span])
    lcode[...] = found[0:16] * 128.0 + found[16:32]
    live = (lcode[0:FAN_REST, :] < float(MASKED)).astype(f32)
    rdeg2 = 1.0 / jnp.maximum(jnp.sum(live, axis=0, keepdims=True), 1.0)

    rows_a = lax.broadcasted_iota(i32, (groups * 8, 256), 0).astype(f32)
    rows_b = lax.broadcasted_iota(i32, (128, 256), 0).astype(f32)

    def list_counts(first, size):
        row = (lax.broadcasted_iota(i32, (size, span), 0) + first).astype(f32)
        total = jnp.where(row == lcode[0:1, :], 1.0, 0.0)
        for k in range(1, FAN_REST):
            total = total + jnp.where(row == lcode[k : k + 1, :], 1.0, 0.0)
        return total.astype(bf16)

    def own_block(b, _):
        start = pl.multiple_of(b * 256, 256)
        for p in range(16):
            pair = []
            for half in range(2):
                g = b * 32 + p * 2 + half
                left = jnp.where(rows_a == crow[pl.ds(g, 1), :], 1.0, 0.0).astype(bf16)
                right = jnp.where(rows_b == lrow[pl.ds(g, 1), :], 1.0, 0.0).astype(bf16)
                pair.append(nt(left, right))
            for a in range(groups):
                tile = jnp.concatenate([pair[0][a * 8 : (a + 1) * 8], pair[1][a * 8 : (a + 1) * 8]], axis=0)
                cblk[p * 16 : (p + 1) * 16, a * 128 : (a + 1) * 128] = tile.astype(bf16)
        cinc[pl.ds(start, 256), :] = cblk[:, nodes:]
        gathered[:, pl.ds(start, 256)] = nt(joined[0:finp, :], cblk[:, 0:nodes])
        for q in range(8):
            chosen[pl.ds(pl.multiple_of(start + q * 32, 32), 32), span:] = list_counts(start + q * 32, 32)
        return 0

    lax.fori_loop(0, nodes // 256, own_block, 0)
    for q in range(slots // 32):
        far2[q * 32 : (q + 1) * 32, :] = list_counts(nodes + q * 32, 32)
    code3 = c3[...].astype(f32)
    row3 = (lax.broadcasted_iota(i32, (slots, 128), 0) + nodes).astype(f32)
    far3 = jnp.zeros((slots, 128), f32)
    for k in range(FAN_REST):
        far3 = far3 + jnp.where(row3 == code3[k : k + 1, :], 1.0, 0.0)
    far3 = far3.astype(bf16)
    rdeg3 = 1.0 / jnp.maximum(jnp.sum((code3[0:FAN_REST] < float(MASKED)).astype(f32), axis=0, keepdims=True), 1.0)
    r_id = lax.broadcasted_iota(i32, (local, 256), 0)
    l_id = lax.broadcasted_iota(i32, (local, 256), 1)
    is_self = (l_id < seeds) & (r_id == l_id + FAN_REST * seeds)
    is_nbr = (l_id >= 128) & (l_id < 128 + seeds) & (r_id < FAN_REST * seeds) & (lax.rem(r_id, seeds) == l_id - 128)
    spread = jnp.where(is_self | is_nbr, 1.0, 0.0).astype(bf16)
    keep_row = ids[1:2, :].astype(f32)

    finish(sent)
    ibt = flip(ib0[...])[0:finp, :]
    b1 = bias_col(0)

    def layer_one(b, _):
        blk = pl.ds(pl.multiple_of(b * 256, 256), 256)
        total = gathered[:, blk] + nt(ibt, cinc[blk, :])
        joined[finp:, blk] = (total * rdeg[0:1, blk]).astype(bf16)
        z = nn(w1t[...], joined[:, blk]) + b1
        act, slope, root = gelu_parts(z)
        act1[:, blk] = act
        slope1[:, blk] = slope
        root1[0:1, blk] = root
        h1t[:, blk] = (act * root).astype(bf16)
        return 0

    lax.fori_loop(0, nodes // 256, layer_one, 0)
    obs[0] = nt(pick[...], h1t[...]).astype(bf16)
    sent = exchange(1, obs.at[0], ibs.at[0])

    own2 = nn(h1t[...], chosen[...])
    w2t = flip(w2)
    finish(sent)
    agg2 = (own2[:, span:] + nn(flip(ibs[0]), far2[...])) * rdeg2
    joined2 = jnp.concatenate([own2[:, 0:span].astype(bf16), agg2.astype(bf16)], axis=0)
    act2, slope2, root2 = gelu_parts(nn(w2t, joined2) + bias_col(1))
    h2 = act2 * root2 * keep_row
    obs[1] = h2[:, 0:slots].T.astype(bf16)
    sent = exchange(2, obs.at[1], ibs.at[1])

    near3 = nn(h2[:, slots:].astype(bf16), spread)
    w3t = flip(w3)
    finish(sent)
    agg3 = (near3[:, 128:] + nn(flip(ibs[1]), far3)) * rdeg3
    joined3 = jnp.concatenate([near3[:, 0:128].astype(bf16), agg3.astype(bf16)], axis=0)
    act3, slope3, root3 = gelu_parts(nn(w3t, joined3) + bias_col(2))
    top = (act3 * root3).astype(bf16)

    classes = wht.shape[0]
    classp = round_up(classes, 16)
    wht_low = jnp.concatenate([wht[...], jnp.zeros((classp - classes, hidden), f32)], axis=0).astype(bf16)
    class_id = lax.broadcasted_iota(i32, (classp, 128), 0)
    seed_lane = lax.broadcasted_iota(i32, (1, 128), 1) < seeds
    weight = jnp.where(seed_lane, lab[1:2, :].astype(f32), 0.0)
    logits = nn(wht_low, top) + bcol[0:classp, 6:7]
    logits = jnp.where(class_id < classes, logits, -1e30)
    peak = jnp.max(logits, axis=0, keepdims=True)
    lse = peak + jnp.log(jnp.sum(jnp.exp(logits - peak), axis=0, keepdims=True))
    hot = jnp.where(class_id == lab[0:1, :], 1.0, 0.0)
    picked = jnp.sum(logits * hot, axis=0, keepdims=True)
    loss = jnp.sum((lse - picked) * weight, axis=1, keepdims=True)
    total = jnp.sum(weight, axis=1, keepdims=True)
    dlog = ((jnp.exp(logits - lse) - hot) * weight).astype(bf16)
    sc_lane = lax.broadcasted_iota(i32, (8, 128), 1)
    ssend[0] = jnp.where(sc_lane == 0, loss, jnp.where(sc_lane == 1, total, 0.0))

    seg_b = 0
    seg_a = 4 * hidden
    row_head = seg_a + 2 * finp
    row_bias = row_head + classp

    def put(row, value):
        size = value.shape[0]
        gl[0, row : row + size, :] = value[:, 0:128].astype(bf16)
        gl[1, row : row + size, :] = value[:, 128:].astype(bf16)

    ones = jnp.ones((16, 128), bf16)
    put(row_head, nt(dlog, top))
    bias_h = jnp.concatenate([nt(ones, dlog), jnp.zeros((16, hidden - classp), f32)], axis=1)
    dtop = nn(wht_low.astype(f32).T.astype(bf16), dlog)

    dz3 = pull_back(act3, slope3, root3, dtop)
    dj3 = nn(w3, dz3)
    dg3 = (dj3[hidden:] * rdeg3).astype(bf16)
    obs[2] = nt(far3, dg3).astype(bf16)
    sent = exchange(3, obs.at[2], ibs.at[2])
    dloc = nt(jnp.concatenate([dj3[0:hidden].astype(bf16), dg3], axis=1), spread)
    put(seg_b + 2 * hidden, nt(joined3, dz3))
    bias_3 = nt(ones, dz3)
    finish(sent)
    dh2 = jnp.concatenate([ibs[2].astype(f32).T, dloc], axis=1) * keep_row

    dz2 = pull_back(act2, slope2, root2, dh2)
    dj2 = nn(w2, dz2)
    dg2 = (dj2[hidden:] * rdeg2).astype(bf16)
    obs[3] = nt(far2[...], dg2).astype(bf16)
    sent = exchange(4, obs.at[3], ibs.at[3])
    put(seg_b, nt(joined2, dz2))
    bias_2 = nt(jnp.ones((16, span), bf16), dz2)
    both = jnp.concatenate([dj2[0:hidden].astype(bf16), dg2], axis=1)
    gathered[0:hidden, :] = nt(both, chosen[...])
    finish(sent)
    back = flip(ibs[3])

    def layer_one_back(b, _):
        blk = pl.ds(pl.multiple_of(b * 256, 256), 256)
        grad = gathered[0:hidden, blk] + nn(back, pick[:, blk])
        h1t[:, blk] = pull_back(act1[:, blk], slope1[:, blk], root1[0:1, blk], grad)
        return 0

    lax.fori_loop(0, nodes // 256, layer_one_back, 0)
    step_rows = finp // 2

    def first_grad(b, _):
        start = pl.multiple_of(b * step_rows, 16)
        value = nt(joined[pl.ds(start, step_rows), :], h1t[...])
        to = pl.multiple_of(seg_a + b * step_rows, 16)
        gl[0, pl.ds(to, step_rows), :] = value[:, 0:128].astype(bf16)
        gl[1, pl.ds(to, step_rows), :] = value[:, 128:].astype(bf16)
        return 0

    lax.fori_loop(0, 4, first_grad, 0)
    bias_1 = nt(jnp.ones((16, nodes), bf16), h1t[...])
    line = lax.broadcasted_iota(i32, (16, hidden), 0)
    put(
        row_bias,
        jnp.where(line == 0, bias_1, 0.0)
        + jnp.where(line == 1, bias_2, 0.0)
        + jnp.where(line == 2, bias_3, 0.0)
        + jnp.where(line == 3, bias_h, 0.0),
    )

    used = []

    def hop(src, dst, axis, who):
        used.append(0)
        k = len(used) - 1
        return pltpu.make_async_remote_copy(
            src_ref=src, dst_ref=dst, send_sem=red_send.at[k], recv_sem=red_recv.at[k],
            device_id={axis: who}, device_id_type=MESH,
        )

    mate_y = zpos * 2 + (1 - ypos)

    def z_mate(off):
        return lax.rem(zpos + off, nz) * 2 + ypos

    def go(*copies):
        for c in copies:
            c.start()
        for c in copies:
            c.wait()

    def rows_of(start, size):
        return pl.ds(pl.multiple_of(start, 16), size)

    rows = gl.shape[1]
    segments = ((seg_b, seg_a), (seg_a, rows - seg_a))

    go(
        hop(gl.at[1 - core], rc, "rep", mate_c),
        hop(ssend.at[0], srecv.at[0], "rep", mate_c),
    )
    acc[...] = gl[core].astype(f32) + rc[...].astype(f32)
    ssend[1] = ssend[0] + srecv[0]

    copies = [hop(ssend.at[1], srecv.at[1], "rep", mate_x)]
    for k, (base, size) in enumerate(segments):
        half = size // 2
        give = rows_of(base + (1 - xpos) * half, half)
        at = slice(base // 2, base // 2 + half)
        sbuf[at, :] = acc[give, :].astype(bf16)
        copies.append(hop(sbuf.at[at], rx.at[at], "rep", mate_x))
    go(*copies)
    ssend[2] = ssend[1] + srecv[1]
    copies = [hop(ssend.at[2], srecv.at[2], "dom", mate_y)]
    for k, (base, size) in enumerate(segments):
        half, quarter = size // 2, size // 4
        keep = rows_of(base + xpos * half, half)
        acc[keep, :] = acc[keep, :] + rx[base // 2 : base // 2 + half, :].astype(f32)
        give = rows_of(base + xpos * half + (1 - ypos) * quarter, quarter)
        at = slice(base // 4, base // 4 + quarter)
        sbuf[at, :] = acc[give, :].astype(bf16)
        copies.append(hop(sbuf.at[at], ry.at[at], "dom", mate_y))
    go(*copies)
    ssend[3] = ssend[2] + srecv[2]
    szv[zpos] = ssend[3]
    copies = []
    for k, (base, size) in enumerate(segments):
        half, quarter, piece = size // 2, size // 4, size // (4 * nz)
        keep = rows_of(base + xpos * half + ypos * quarter, quarter)
        acc[keep, :] = acc[keep, :] + ry[base // 4 : base // 4 + quarter, :].astype(f32)
        at = slice(base // 4, base // 4 + quarter)
        sbuf[at, :] = acc[keep, :].astype(bf16)
        for off in range(1, nz):
            to = lax.rem(zpos + off, nz)
            copies.append(
                hop(
                    sbuf.at[rows_of(base // 4 + to * piece, piece)],
                    rz.at[off - 1, base // (4 * nz) : base // (4 * nz) + piece],
                    "dom",
                    z_mate(off),
                )
            )
    for off in range(1, nz):
        copies.append(hop(ssend.at[3], szv.at[zpos], "dom", z_mate(off)))
    go(*copies)
    s_out[...] = szv[0] + szv[1] + szv[2] + szv[3]
    copies = []
    for k, (base, size) in enumerate(segments):
        half, quarter, piece = size // 2, size // 4, size // (4 * nz)
        here = rows_of(base + xpos * half + ypos * quarter + zpos * piece, piece)
        got = slice(base // (4 * nz), base // (4 * nz) + piece)
        value = acc[here, :]
        for off in range(1, nz):
            value = value + rz[off - 1, got, :].astype(f32)
        gout[core, here, :] = value.astype(bf16)
        for off in range(1, nz):
            copies.append(
                hop(gout.at[core, here], gout.at[core, here], "dom", z_mate(off))
            )
    go(*copies)
    copies = []
    for k, (base, size) in enumerate(segments):
        half, quarter = size // 2, size // 4
        part = gout.at[core, rows_of(base + xpos * half + ypos * quarter, quarter)]
        copies.append(hop(part, part, "dom", mate_y))
    go(*copies)
    copies = []
    for k, (base, size) in enumerate(segments):
        half = size // 2
        part = gout.at[core, rows_of(base + xpos * half, half)]
        copies.append(hop(part, part, "rep", mate_x))
    go(*copies)
    go(hop(gout.at[core], gout.at[core], "rep", mate_c))
    g_out[:, 0:128] = gout[0]
    g_out[:, 128:] = gout[1]


def summed_gradients(peers, cap, seeds, c1, c2, c3, ids, col, lab, xt, w1, wr, wht, bias):
    fin, nodes = xt.shape
    hidden = w1.shape[1]
    finp = round_up(fin, 16)
    wide = round_up(fin, 128)
    slots = peers * cap
    span = ids.shape[1]
    classp = round_up(wht.shape[0], 16)
    rows = 4 * hidden + 2 * finp + classp + 16
    nz = peers // 2
    vmem = pltpu.VMEM
    scratch = [
        vmem((2 * finp, nodes), bf16),
        vmem((finp, nodes), f32),
        vmem((slots, nodes), bf16),
        vmem((nodes, 2 * span), bf16),
        vmem((slots, span), bf16),
        vmem((256, nodes + slots), bf16),
        vmem((nodes, slots), bf16),
        vmem((nodes, 128), f32),
        vmem((nodes // 8, 256), f32),
        vmem((nodes // 8, 256), f32),
        vmem((8, nodes), f32),
        vmem((16, span), f32),
        vmem((hidden, 2 * finp), bf16),
        vmem((hidden, nodes), f32),
        vmem((hidden, nodes), f32),
        vmem((8, nodes), f32),
        vmem((hidden, nodes), bf16),
        vmem((slots, wide), bf16),
        vmem((slots, wide), bf16),
        vmem((4, slots, hidden), bf16),
        vmem((4, slots, hidden), bf16),
        vmem((2, rows, 128), bf16),
        vmem((rows, 128), bf16),
        vmem((rows, 128), f32),
        vmem((rows // 2, 128), bf16),
        vmem((rows // 2, 128), bf16),
        vmem((rows // 4, 128), bf16),
        vmem((nz - 1, rows // (4 * nz), 128), bf16),
        vmem((2, rows, 128), bf16),
        vmem((4, 8, 128), f32),
        vmem((3, 8, 128), f32),
        vmem((nz, 8, 128), f32),
        pltpu.SemaphoreType.DMA((5, peers - 1)),
        pltpu.SemaphoreType.DMA((5, peers - 1)),
        pltpu.SemaphoreType.DMA((28,)),
        pltpu.SemaphoreType.DMA((28,)),
    ]
    return pl.pallas_call(
        functools.partial(graph_kernel, peers, cap, seeds),
        out_shape=(
            jax.ShapeDtypeStruct((rows, hidden), bf16),
            jax.ShapeDtypeStruct((8, 128), f32),
        ),
        in_specs=[pl.BlockSpec(memory_space=vmem)] * 11,
        out_specs=(pl.BlockSpec(memory_space=vmem), pl.BlockSpec(memory_space=vmem)),
        scratch_shapes=scratch,
        compiler_params=pltpu.CompilerParams(
            collective_id=0, has_side_effects=True, vmem_limit_bytes=56 * 2**20
        ),
        name="graph_step",
    )(c1, c2, c3, ids, col, lab, xt, w1, wr, wht, bias)


def shampoo(grad, scale, weight, left, left_root, right, right_root, part, right_split):
    high = lax.Precision.HIGH
    count = left.shape[0]
    grad_rows = lax.dynamic_slice_in_dim(grad, part * count, count, 0)
    weight_rows = lax.dynamic_slice_in_dim(weight, part * count, count, 0)
    square = (1.0 - decay) * scale * scale
    new_left = decay * left + square * lax.dot_general(
        grad_rows, grad, (((1,), (1,)), ((), ())), preferred_element_type=f32
    )
    if right_split:
        cols = right.shape[0]
        grad_cols = lax.dynamic_slice_in_dim(grad, part * cols, cols, 1)
    else:
        grad_cols = grad
    new_right = decay * right + square * lax.dot_general(
        grad_cols, grad, (((0,), (0,)), ((), ())), preferred_element_type=f32
    )
    step = jnp.dot(
        jnp.dot(left_root, grad.astype(f32), precision=high), right_root, precision=high
    )
    return (
        grad_rows.astype(f32) * scale,
        new_left,
        new_right,
        weight_rows - (shampoo_rate * scale) * step,
    )


def shards(
    features, nbr_index, nbr_mask, send_rows, send_count, labels, seed_mask,
    w_first, w_rest, w_head, biases,
    stat_big, root_big, stat_mid, root_mid, stat_sq, root_sq, stat_hr, root_hr, bias_m, bias_v,
):
    hidden = w_rest.shape[2]
    peers = send_rows.shape[2]
    cap = send_rows.shape[3]
    nodes, fin = features.shape[1], features.shape[2]
    seeds = labels.shape[1]
    classes = w_head.shape[1]
    slots = peers * cap
    finp = round_up(fin, 16)
    classp = round_up(classes, 16)

    codes = jnp.where(nbr_mask[0] == 1, nbr_index[0], MASKED)
    codes = jnp.swapaxes(codes, 1, 2)
    c1 = codes[0]
    c2 = codes[1, 0:16]
    c3 = codes[2, 0:16, 0:128]
    valid = jnp.arange(cap)[None, :] < send_count.reshape(peers, 1)
    send = send_rows.reshape(peers, cap)
    col = jnp.where(valid, send, -1).reshape(slots, 1)
    around = c3[0:FAN_REST, 0:seeds].reshape(-1)
    own = around < nodes
    local = round_up(seeds * (FAN_REST + 1), 256)
    fill = local - seeds * (FAN_REST + 1)
    ids = jnp.stack(
        [
            jnp.concatenate(
                [
                    send.reshape(-1),
                    jnp.where(own, around, -1),
                    jnp.arange(seeds, dtype=i32),
                    jnp.full((fill,), -1, i32),
                ]
            ),
            jnp.concatenate(
                [
                    valid.reshape(-1).astype(i32),
                    own.astype(i32),
                    jnp.ones((seeds,), i32),
                    jnp.zeros((fill,), i32),
                ]
            ),
        ]
    )
    lab = jnp.pad(jnp.stack([labels[0], seed_mask[0]]), ((0, 0), (0, 128 - seeds)))
    xt = jnp.swapaxes(features[0], 0, 1)
    bias = jnp.pad(biases, (0, 1024 - biases.shape[0])).reshape(8, 128)
    g_all, scalars = summed_gradients(
        peers, cap, seeds, c1, c2, c3, ids, col, lab, xt, w_first, w_rest, w_head.T, bias
    )
    loss_sum, seed_total = scalars[0, 0], scalars[0, 1]
    rest = 4 * hidden
    g_two, g_three = g_all[0 : 2 * hidden], g_all[2 * hidden : rest]
    g_one = jnp.concatenate([g_all[rest : rest + fin], g_all[rest + finp : rest + finp + fin]])
    at = rest + 2 * finp
    g_top = g_all[at : at + classes].T
    at = at + classp
    g_bias = jnp.concatenate([g_all[at : at + 3].reshape(-1), g_all[at + 3, 0:classes]]).astype(f32)
    wide = g_all.astype(f32)
    grad_norm = jnp.sqrt(jnp.sum(wide * wide)) / seed_total
    scale = clip_limit / jnp.maximum(grad_norm, clip_limit) / seed_total
    grad_bias = g_bias * scale
    part = lax.axis_index("rep")
    head_rows = stat_sq.shape[1]
    head_root_rows = lax.dynamic_slice_in_dim(root_sq[3], part * head_rows, head_rows, 0)
    g_first, l_first, r_first, n_first = shampoo(
        g_one, scale, w_first, stat_big, root_big, stat_sq[0], root_sq[0], part, True
    )
    g_mid0, l_mid0, r_mid0, n_mid0 = shampoo(
        g_two, scale, w_rest[0], stat_mid[0], root_mid[0], stat_sq[1], root_sq[1], part, True
    )
    g_mid1, l_mid1, r_mid1, n_mid1 = shampoo(
        g_three, scale, w_rest[1], stat_mid[1], root_mid[1], stat_sq[2], root_sq[2], part, True
    )
    g_head, l_head, r_head, n_head = shampoo(
        g_top, scale, w_head, stat_sq[3], head_root_rows, stat_hr, root_hr, part, False
    )
    new_m = beta_one * bias_m + (1.0 - beta_one) * grad_bias
    new_v = beta_two * bias_v + (1.0 - beta_two) * grad_bias * grad_bias
    m_hat = new_m / (1.0 - beta_one**STEP)
    v_hat = new_v / (1.0 - beta_two**STEP)
    new_b = biases - bias_rate * (m_hat / (jnp.sqrt(v_hat) + adam_eps) + weight_decay * biases)
    new_rest = jnp.stack([n_mid0, n_mid1])
    return (
        loss_sum, seed_total, grad_norm,
        g_first, jnp.stack([g_mid0, g_mid1]), g_head,
        new_m, new_v,
        l_first, jnp.stack([l_mid0, l_mid1]), jnp.stack([r_first, r_mid0, r_mid1, l_head]), r_head,
        n_first, new_rest, n_head, new_b,
        n_first.astype(bf16), new_rest.astype(bf16), n_head.astype(bf16),
    )


highest = lax.Precision.HIGHEST


def plain_activate(z):
    act = jax.nn.gelu(z, approximate=True)
    return act * lax.rsqrt(jnp.sum(act * act, axis=-1, keepdims=True) + norm_eps)


def plain_counts(nbr, mask, columns):
    nodes, slots = nbr.shape
    column_ids = jnp.arange(columns, dtype=jnp.int32)[None, :]
    mask_low = mask.astype(jnp.bfloat16)

    def add_slot(slot, total):
        picks = lax.dynamic_slice_in_dim(nbr, slot, 1, 1)
        weight = lax.dynamic_slice_in_dim(mask_low, slot, 1, 1)
        return total + (picks == column_ids).astype(jnp.bfloat16) * weight

    return lax.fori_loop(0, slots, add_slot, jnp.zeros((nodes, columns), jnp.bfloat16))


def plain_forward(h, weight, bias, nbr, mask, send_list, valid):
    nodes, width = h.shape
    hb = h.astype(jnp.bfloat16)
    outgoing = (
        jnp.take(hb, send_list, axis=0).reshape(valid.shape[0], valid.shape[1], width)
        * valid[:, :, None]
    )
    incoming = lax.all_to_all(outgoing, "dom", split_axis=0, concat_axis=0, tiled=True)
    table = jnp.concatenate([hb, incoming.reshape(-1, width)], axis=0)
    counts = plain_counts(nbr, mask, table.shape[0])
    degree = jnp.maximum(jnp.sum(mask, axis=1), 1).astype(jnp.float32)[:, None]
    gathered = jnp.dot(counts, table, preferred_element_type=jnp.float32)
    joined = jnp.concatenate([hb, (gathered / degree).astype(jnp.bfloat16)], axis=1)
    z = jnp.dot(joined, weight.astype(jnp.bfloat16), preferred_element_type=jnp.float32) + bias
    return (plain_activate(z), (joined, counts, degree, z))


def plain_backward(grad_out, weight, kept, send_list, valid, need_input):
    joined, counts, degree, z = kept
    nodes = joined.shape[0]
    width = joined.shape[1] // 2
    grad_z = jax.vjp(plain_activate, z)[1](grad_out)[0].astype(jnp.bfloat16)
    grad_w = jnp.einsum("nk,nh->kh", joined, grad_z, preferred_element_type=jnp.float32)
    grad_b = jnp.sum(grad_z.astype(jnp.float32), axis=0)
    if not need_input:
        return (grad_w, grad_b, None)
    grad_joined = jnp.einsum(
        "nh,kh->nk", grad_z, weight.astype(jnp.bfloat16), preferred_element_type=jnp.float32
    )
    grad_gathered = (grad_joined[:, width:] / degree).astype(jnp.bfloat16)
    grad_table = jnp.einsum("nj,nw->jw", counts, grad_gathered, preferred_element_type=jnp.float32)
    returned = (
        grad_table[nodes:].reshape(valid.shape[0], valid.shape[1], width).astype(jnp.bfloat16)
    )
    returned = lax.all_to_all(returned, "dom", split_axis=0, concat_axis=0, tiled=True)
    sent_back = (returned * valid[:, :, None]).reshape(-1, width)
    placement = (send_list[:, None] == jnp.arange(nodes, dtype=jnp.int32)[None, :]).astype(
        jnp.bfloat16
    )
    scattered = jnp.einsum("sn,sw->nw", placement, sent_back, preferred_element_type=jnp.float32)
    return (grad_w, grad_b, grad_joined[:, :width] + grad_table[:nodes] + scattered)


def plain_shampoo(grad, weight, left, left_root, right, right_root, part, right_split):
    count = left.shape[0]
    grad_rows = lax.dynamic_slice_in_dim(grad, part * count, count, 0)
    weight_rows = lax.dynamic_slice_in_dim(weight, part * count, count, 0)
    new_left = decay * left + (1.0 - decay) * jnp.dot(grad_rows, grad.T, precision=highest)
    if right_split:
        cols = right.shape[0]
        grad_cols = lax.dynamic_slice_in_dim(grad, part * cols, cols, 1)
        new_right = decay * right + (1.0 - decay) * jnp.dot(grad_cols.T, grad, precision=highest)
    else:
        new_right = decay * right + (1.0 - decay) * jnp.dot(grad.T, grad, precision=highest)
    step = jnp.dot(jnp.dot(left_root, grad, precision=highest), right_root, precision=highest)
    return (grad_rows, new_left, new_right, weight_rows - shampoo_rate * step)


def plain_shards(
    features,
    nbr_index,
    nbr_mask,
    send_rows,
    send_count,
    labels,
    seed_mask,
    w_first,
    w_rest,
    w_head,
    biases,
    stat_big,
    root_big,
    stat_mid,
    root_mid,
    stat_sq,
    root_sq,
    stat_hr,
    root_hr,
    bias_m,
    bias_v,
):
    hidden = w_rest.shape[2]
    peers = send_rows.shape[2]
    cap = send_rows.shape[3]
    send_list = send_rows.reshape(-1)
    valid = (jnp.arange(cap)[None, :] < send_count.reshape(peers, 1)).astype(jnp.bfloat16)
    weights = [w_first, w_rest[0], w_rest[1]]
    state = features[0].astype(jnp.float32)
    kept = []
    for level in range(3):
        state, saved = plain_forward(
            state,
            weights[level],
            biases[level * hidden : (level + 1) * hidden],
            nbr_index[0, level],
            nbr_mask[0, level],
            send_list,
            valid,
        )
        kept.append(saved)
    seeds = labels.shape[1]
    top = state[:seeds].astype(jnp.bfloat16)
    head_low_w = w_head.astype(jnp.bfloat16)
    logits = jnp.dot(top, head_low_w, preferred_element_type=jnp.float32) + biases[3 * hidden :]
    lse = jax.nn.logsumexp(logits, axis=1)
    onehot = (labels[0][:, None] == jnp.arange(logits.shape[1])[None, :]).astype(jnp.float32)
    picked = jnp.sum(logits * onehot, axis=1)
    seed_weight = seed_mask[0].astype(jnp.float32)
    loss_sum, seed_total = lax.psum(
        (jnp.sum((lse - picked) * seed_weight), jnp.sum(seed_weight)), ("dom", "rep")
    )
    grad_logits = (
        (jnp.exp(logits - lse[:, None]) - onehot) * (seed_weight / seed_total)[:, None]
    ).astype(jnp.bfloat16)
    grad_head = jnp.einsum("sh,sc->hc", top, grad_logits, preferred_element_type=jnp.float32)
    grad_hbias = jnp.sum(grad_logits.astype(jnp.float32), axis=0)
    grad_head, grad_hbias = (grad_head, grad_hbias)
    grad_top = jnp.einsum("sc,hc->sh", grad_logits, head_low_w, preferred_element_type=jnp.float32)
    grad_state = jnp.zeros(state.shape, jnp.float32).at[:seeds].set(grad_top)
    results = [None, None, None]
    for level in (2, 1, 0):
        grad_w, grad_b, grad_state = plain_backward(
            grad_state, weights[level], kept[level], send_list, valid, level > 0
        )
        results[level] = (grad_w, grad_b)
    grad_bias = jnp.concatenate([results[0][1], results[1][1], results[2][1], grad_hbias])
    grad_one, grad_two, grad_three = (results[0][0], results[1][0], results[2][0])
    grad_one, grad_two, grad_three, grad_head, grad_bias = lax.psum(
        (grad_one, grad_two, grad_three, grad_head, grad_bias), ("dom", "rep")
    )
    everything = (grad_one, grad_two, grad_three, grad_head, grad_bias)
    grad_norm = jnp.sqrt(sum((jnp.sum(g * g) for g in everything)))
    factor = clip_limit / jnp.maximum(grad_norm, clip_limit)
    grad_one, grad_two, grad_three, grad_head, grad_bias = [g * factor for g in everything]
    part = lax.axis_index("rep")
    head_rows = stat_sq.shape[1]
    head_root_rows = lax.dynamic_slice_in_dim(root_sq[3], part * head_rows, head_rows, 0)
    g_first, l_first, r_first, n_first = plain_shampoo(
        grad_one, w_first, stat_big, root_big, stat_sq[0], root_sq[0], part, True
    )
    g_mid0, l_mid0, r_mid0, n_mid0 = plain_shampoo(
        grad_two, w_rest[0], stat_mid[0], root_mid[0], stat_sq[1], root_sq[1], part, True
    )
    g_mid1, l_mid1, r_mid1, n_mid1 = plain_shampoo(
        grad_three, w_rest[1], stat_mid[1], root_mid[1], stat_sq[2], root_sq[2], part, True
    )
    g_head, l_head, r_head, n_head = plain_shampoo(
        grad_head, w_head, stat_sq[3], head_root_rows, stat_hr, root_hr, part, False
    )
    new_m = beta_one * bias_m + (1.0 - beta_one) * grad_bias
    new_v = beta_two * bias_v + (1.0 - beta_two) * grad_bias * grad_bias
    m_hat = new_m / (1.0 - beta_one**STEP)
    v_hat = new_v / (1.0 - beta_two**STEP)
    new_b = biases - bias_rate * (m_hat / (jnp.sqrt(v_hat) + adam_eps) + weight_decay * biases)
    new_rest = jnp.stack([n_mid0, n_mid1])
    return (
        loss_sum,
        seed_total,
        grad_norm,
        g_first,
        jnp.stack([g_mid0, g_mid1]),
        g_head,
        new_m,
        new_v,
        l_first,
        jnp.stack([l_mid0, l_mid1]),
        jnp.stack([r_first, r_mid0, r_mid1, l_head]),
        r_head,
        n_first,
        new_rest,
        n_head,
        new_b,
        n_first.astype(jnp.bfloat16),
        new_rest.astype(jnp.bfloat16),
        n_head.astype(jnp.bfloat16),
    )


def solution(mesh):
    placed = (
        P("rep", "dom", None),
        P("rep", None, "dom", None),
        P("rep", None, "dom", None),
        P("rep", "dom", None, None),
        P("rep", "dom", None),
        P("rep", "dom"),
        P("rep", "dom"),
        P(), P(), P(), P(),
        P("rep", None),
        P("rep", None),
        P(None, "rep", None),
        P(None, "rep", None),
        P(None, "rep", None),
        P(), P(), P(), P(), P(),
    )
    small = mesh.shape["rep"] == 4 and mesh.shape["dom"] == 8
    return jax.shard_map(
        shards if small else plain_shards,
        mesh=mesh,
        in_specs=placed,
        out_specs=(
            P(), P(), P(),
            P("rep", None), P(None, "rep", None), P("rep", None),
            P(), P(),
            P("rep", None), P(None, "rep", None), P(None, "rep", None), P(),
            P("rep", None), P(None, "rep", None), P("rep", None), P(),
            P("rep", None), P(None, "rep", None), P("rep", None),
        ),
        check_vma=False,
    )
```

```python
import functools

import jax
import jax.numpy as jnp
from jax import lax
from jax.experimental import pallas as pl
from jax.experimental.pallas import tpu as pltpu
from jax.sharding import PartitionSpec as P

STEP = 5
FAN_REST = 10

clip_limit = 0.0001
decay = 0.5
shampoo_rate = 1.0
beta_one = 0.9
beta_two = 0.999
bias_rate = 0.05
weight_decay = 0.01
adam_eps = 1e-08
norm_eps = 1e-06
MASKED = 8192

bf16 = jnp.bfloat16
f32 = jnp.float32
i32 = jnp.int32
MESH = pl.DeviceIdType.MESH


def nn(a, b):
    return jnp.dot(a, b, preferred_element_type=f32)


def nt(a, b):
    return lax.dot_general(a, b, (((1,), (1,)), ((), ())), preferred_element_type=f32)


def flip(a):
    return a.astype(f32).T.astype(a.dtype)


def round_up(a, b):
    return (a + b - 1) // b * b


def gelu(z):
    scale = 0.7978845608028654
    return z * (0.5 + 0.5 * jnp.tanh(z * (scale + (0.044715 * scale) * (z * z))))


def gelu_slope(z):
    scale = 0.7978845608028654
    square = z * z
    half = 0.5 + 0.5 * jnp.tanh(z * (scale + (0.044715 * scale) * square))
    return half + (half - half * half) * (z * (2.0 * scale + (6.0 * 0.044715 * scale) * square))


def norm_root(act):
    return lax.rsqrt(jnp.sum(act * act, axis=0, keepdims=True) + norm_eps)


def pull_back(act, slope, root, grad):
    dot = jnp.sum(act * grad, axis=0, keepdims=True)
    return (slope * (root * grad - act * (root * root * root * dot))).astype(bf16)


def as_column(row):
    return jnp.broadcast_to(row, (8, row.shape[1])).T[:, 0:1]


def widen(row, width, value=0):
    return jnp.concatenate([row, jnp.full((1, width - row.shape[1]), value, row.dtype)], axis=1)


def graph_kernel(
    peers, cap, seeds, fan,
    code_ref, srow, scnt, lab, smask, xt, w1_hbm, wr_hbm, wht, bias,
    g_out, s_out,
    joined, gathered, pick, chosen, far2, cblk_a, cblk_b, cinc, ctmp, crow, lrow, rdeg, part2, lcode,
    w1, wr, w1t, act1, z1, root1, h1t, ob0, ib0, obs, ibs,
    gl, acc, rc, sb1, rb1, sb2, rb2, sbz, rbz, gout, ssend, srecv, szv,
    load_sem, send_sem, recv_sem, red_send, red_recv,
):
    fin, nodes = xt.shape
    hidden = w1.shape[1]
    finp = round_up(fin, 16)
    slots = peers * cap
    table = nodes + slots
    groups = table // 128
    chunks = nodes // 128
    span = far2.shape[1]
    local = span - slots
    me = lax.axis_index("dom")
    rep = lax.axis_index("rep")
    core = lax.rem(rep, 2)
    xpos = rep // 2
    ypos = lax.rem(me, 2)
    zpos = me // 2
    nz = peers // 2
    mate_c = xpos * 2 + (1 - core)
    mate_x = (1 - xpos) * 2 + core
    mate_y = zpos * 2 + (1 - ypos)

    bias = bias[...].reshape(1, bias.shape[0])
    load1 = pltpu.make_async_copy(w1_hbm, w1, load_sem.at[0])
    load2 = pltpu.make_async_copy(wr_hbm, wr, load_sem.at[1])
    load1.start()
    load2.start()
    barrier = pltpu.get_barrier_semaphore()
    for off in range(1, peers):
        pl.semaphore_signal(barrier, inc=1, device_id={"dom": lax.rem(me + off, peers)}, device_id_type=MESH)
    for mate in (mate_c, mate_x):
        pl.semaphore_signal(barrier, inc=1, device_id={"rep": mate}, device_id_type=MESH)

    def exchange(stage, src, dst):
        copies = []
        for off in range(1, peers):
            peer = lax.rem(me + off, peers)
            copies.append(
                pltpu.make_async_remote_copy(
                    src_ref=src.at[pl.ds(pl.multiple_of(peer * cap, cap), cap)],
                    dst_ref=dst.at[pl.ds(pl.multiple_of(me * cap, cap), cap)],
                    send_sem=send_sem.at[stage, off - 1],
                    recv_sem=recv_sem.at[stage, off - 1],
                    device_id={"dom": peer},
                    device_id_type=MESH,
                )
            )
        for c in copies:
            c.start()
        return copies

    def finish(copies):
        for c in copies:
            c.wait()

    mine = pl.ds(pl.multiple_of(me * cap, cap), cap)

    count = jnp.broadcast_to(scnt[...], (peers, peers))
    count = jnp.where(
        lax.broadcasted_iota(i32, (peers, peers), 0) == lax.broadcasted_iota(i32, (peers, peers), 1), count, 0
    )
    count = jnp.sum(count.astype(f32), axis=1, keepdims=True)
    in_use = lax.broadcasted_iota(i32, (peers, cap), 1).astype(f32) < count
    slot = jnp.where(in_use, srow[...].astype(f32), -1.0)
    per = 128 // cap
    slot = jnp.concatenate([slot] * per, axis=1)
    owner = lax.broadcasted_iota(i32, (peers, 128), 0)
    place = lax.broadcasted_iota(i32, (peers, 128), 1) // cap
    send_row = jnp.concatenate(
        [
            jnp.sum(jnp.where(owner == place + t * per, slot, 0.0), axis=0, keepdims=True)
            for t in range(slots // 128)
        ],
        axis=1,
    )
    send_col = as_column(send_row)
    pick[...] = jnp.where(
        send_col == lax.broadcasted_iota(i32, (slots, nodes), 1).astype(f32), 1.0, 0.0
    ).astype(bf16)
    joined[finp - 16 : finp, :] = jnp.zeros((16, nodes), bf16)
    joined[0:fin, :] = xt[...]
    ob0[:, finp:] = jnp.zeros((slots, ob0.shape[1] - finp), bf16)
    ob0[:, 0:finp] = nt(pick[...], joined[0:finp, :]).astype(bf16)
    ib0[mine, :] = jnp.zeros((cap, ib0.shape[1]), bf16)
    for k in range(4):
        ibs[k, mine, :] = jnp.zeros((cap, hidden), bf16)
    pl.semaphore_wait(barrier, peers - 1 + 2)
    sent = exchange(0, ob0, ib0)

    def codes(level, c, size):
        return code_ref[level, 0:size, c * 128 : (c + 1) * 128]

    fill = jnp.full((32 - fan, 128), float(MASKED), f32)
    fill2 = jnp.full((16 - FAN_REST, 128), float(MASKED), f32)
    for c in range(chunks):
        here = slice(c * 128, (c + 1) * 128)
        code = codes(0, c, fan)
        degree = jnp.sum((code < MASKED).astype(f32), axis=0, keepdims=True)
        rdeg[0:1, here] = 1.0 / jnp.maximum(degree, 1.0)
        ctmp[here, 0:32] = jnp.concatenate([code, fill], axis=0).T
        code = jnp.concatenate([codes(1, c, FAN_REST), fill2], axis=0).astype(i32)
        part2[0:16, here] = (code >> 7).astype(f32).astype(bf16)
        part2[16:32, here] = (code & 127).astype(f32).astype(bf16)

    ngroups = nodes // 8
    lane = lax.broadcasted_iota(i32, (ngroups, 256), 1)
    code = jnp.zeros((ngroups, 256), f32)
    for n in range(8):
        piece = ctmp[pl.ds(n, ngroups, stride=8), :]
        piece = jnp.concatenate([piece, piece], axis=1)
        piece = pltpu.roll(piece, n * 32, 1) if n else piece
        code = jnp.where((lane >> 5) == n, piece, code)
    code = code.astype(i32)
    crow[...] = ((code >> 7) * 8 + (lane >> 5)).astype(f32)
    lrow[...] = (code & 127).astype(f32)

    code3 = codes(2, 0, FAN_REST)
    lane = lax.broadcasted_iota(i32, (1, 128), 1)
    fits = 128 // seeds
    tiles, keeps = [], []
    for t in range(local // 128):
        tile = jnp.full((1, 128), -1.0, f32)
        for j in range(fits):
            k = t * fits + j
            here = lane // seeds == j
            if k < FAN_REST:
                piece = code3[k : k + 1, :]
                piece = pltpu.roll(piece, j * seeds, 1) if j else piece
                tile = jnp.where(here & (piece < nodes), piece, tile)
            elif k == FAN_REST:
                tile = jnp.where(here, (lane - j * seeds).astype(f32), tile)
        tiles.append(tile)
    list_row = jnp.concatenate([send_row] + tiles, axis=1)
    keep_row = jnp.where(list_row >= 0.0, 1.0, 0.0)

    def one_hot_rows(b, _):
        start = pl.multiple_of(b * 256, 256)
        row = (lax.broadcasted_iota(i32, (256, span), 0) + b * 256).astype(f32)
        chosen[pl.ds(start, 256), 0:span] = jnp.where(row == list_row, 1.0, 0.0).astype(bf16)
        return 0

    lax.fori_loop(0, nodes // 256, one_hot_rows, 0)
    found = nn(part2[...], chosen[:, 0:span])
    lcode[...] = found[0:16] * 128.0 + found[16:32]
    live = (lcode[0:FAN_REST, :] < float(MASKED)).astype(f32)
    rdeg2 = 1.0 / jnp.maximum(jnp.sum(live, axis=0, keepdims=True), 1.0)

    rows_a = lax.broadcasted_iota(i32, (groups * 8, 256), 0).astype(f32)
    rows_b = lax.broadcasted_iota(i32, (128, 256), 0).astype(f32)

    def list_counts(first, size):
        row = (lax.broadcasted_iota(i32, (size, span), 0) + first).astype(f32)
        total = jnp.where(row == lcode[0:1, :], 1.0, 0.0)
        for k in range(1, FAN_REST):
            total = total + jnp.where(row == lcode[k : k + 1, :], 1.0, 0.0)
        return total.astype(bf16)

    def build(b, cblk):
        start = b * 256
        for p in range(16):
            pair = []
            for half in range(2):
                g = b * 32 + p * 2 + half
                left = jnp.where(rows_a == crow[pl.ds(g, 1), :], 1.0, 0.0).astype(bf16)
                right = jnp.where(rows_b == lrow[pl.ds(g, 1), :], 1.0, 0.0).astype(bf16)
                pair.append(nt(left, right))
            for a in range(groups):
                tile = jnp.concatenate([pair[0][a * 8 : (a + 1) * 8], pair[1][a * 8 : (a + 1) * 8]], axis=0)
                if a < chunks:
                    cblk[p * 16 : (p + 1) * 16, a * 128 : (a + 1) * 128] = tile.astype(bf16)
                else:
                    at = pl.ds(pl.multiple_of(start + p * 16, 16), 16)
                    cinc[at, (a - chunks) * 128 : (a - chunks + 1) * 128] = tile.astype(bf16)
        for q in range(8):
            at = pl.ds(pl.multiple_of(start + q * 32, 32), 32)
            chosen[at, span:] = list_counts(start + q * 32, 32)

    def multiply(b, cblk):
        blk = pl.ds(pl.multiple_of(b * 256, 256), 256)
        gathered[:, blk] = nt(joined[0:finp, :], cblk[...])

    build(0, cblk_a)

    def own_blocks(i, _):
        multiply(2 * i, cblk_a)
        build(2 * i + 1, cblk_b)
        multiply(2 * i + 1, cblk_b)
        build(2 * i + 2, cblk_a)
        return 0

    last = nodes // 256 - 1
    lax.fori_loop(0, (last - 1) // 2, own_blocks, 0)
    multiply(last - 1, cblk_a)
    build(last, cblk_b)
    multiply(last, cblk_b)

    load1.wait()
    load2.wait()
    wpad = jnp.concatenate(
        [w1[0:fin, :], jnp.zeros((finp - fin, hidden), f32), w1[fin : 2 * fin, :], jnp.zeros((finp - fin, hidden), f32)],
        axis=0,
    )
    w1t[...] = wpad.T.astype(bf16)
    w2 = wr[0].astype(bf16)
    w3 = wr[1].astype(bf16)

    def bias_col(level):
        return as_column(bias[0:1, level * hidden : (level + 1) * hidden])

    finish(sent)
    ibt = flip(ib0[...])[0:finp, :]
    b1 = bias_col(0)

    def layer_one(b, _):
        blk = pl.ds(pl.multiple_of(b * 256, 256), 256)
        total = gathered[:, blk] + nt(ibt, cinc[blk, :])
        joined[finp:, blk] = (total * rdeg[0:1, blk]).astype(bf16)
        z = nn(w1t[...], joined[:, blk]) + b1
        z1[:, blk] = z
        act = gelu(z)
        root = norm_root(act)
        act1[:, blk] = act
        root1[0:1, blk] = root
        h1t[:, blk] = (act * root).astype(bf16)
        return 0

    lax.fori_loop(0, nodes // 256, layer_one, 0)
    obs[0] = nt(pick[...], h1t[...]).astype(bf16)
    sent = exchange(1, obs.at[0], ibs.at[0])

    own2 = nn(h1t[...], chosen[...])
    w2t = flip(w2)
    for q in range(slots // 32):
        far2[q * 32 : (q + 1) * 32, :] = list_counts(nodes + q * 32, 32)

    def slopes(b, _):
        blk = pl.ds(pl.multiple_of(b * 256, 256), 256)
        z1[:, blk] = gelu_slope(z1[:, blk])
        return 0

    lax.fori_loop(0, nodes // 256, slopes, 0)
    b2 = bias_col(1)
    finish(sent)
    agg2 = (own2[:, span:] + nn(flip(ibs[0]), far2[...])) * rdeg2
    joined2 = jnp.concatenate([own2[:, 0:span].astype(bf16), agg2.astype(bf16)], axis=0)
    z2 = nn(w2t, joined2) + b2
    act2 = gelu(z2)
    root2 = norm_root(act2)
    h2 = act2 * root2 * keep_row
    obs[1] = h2[:, 0:slots].T.astype(bf16)
    sent = exchange(2, obs.at[1], ibs.at[1])

    r_id = lax.broadcasted_iota(i32, (local, 256), 0)
    l_id = lax.broadcasted_iota(i32, (local, 256), 1)
    is_self = (l_id < seeds) & (r_id == l_id + FAN_REST * seeds)
    is_nbr = (l_id >= 128) & (l_id < 128 + seeds) & (r_id < FAN_REST * seeds) & (lax.rem(r_id, seeds) == l_id - 128)
    spread = jnp.where(is_self | is_nbr, 1.0, 0.0).astype(bf16)
    near3 = nn(h2[:, slots:].astype(bf16), spread)
    row3 = (lax.broadcasted_iota(i32, (slots, 128), 0) + nodes).astype(f32)
    far3 = jnp.zeros((slots, 128), f32)
    for k in range(FAN_REST):
        far3 = far3 + jnp.where(row3 == code3[k : k + 1, :], 1.0, 0.0)
    far3 = far3.astype(bf16)
    rdeg3 = 1.0 / jnp.maximum(jnp.sum((code3 < float(MASKED)).astype(f32), axis=0, keepdims=True), 1.0)
    slope2 = gelu_slope(z2)
    w3t = flip(w3)
    classes = wht.shape[0]
    classp = round_up(classes, 16)
    wht_low = jnp.concatenate([wht[...], jnp.zeros((classp - classes, hidden), f32)], axis=0)
    wh_low = wht_low.T.astype(bf16)
    wht_low = wht_low.astype(bf16)
    b3 = bias_col(2)
    bh = as_column(widen(bias[0:1, 3 * hidden : 3 * hidden + classes], 128))[0:classp]
    class_id = lax.broadcasted_iota(i32, (classp, 128), 0)
    hot = jnp.where(class_id == widen(lab[...], 128), 1.0, 0.0)
    weight = widen(smask[...].astype(f32), 128)
    finish(sent)
    agg3 = (near3[:, 128:] + nn(flip(ibs[1]), far3)) * rdeg3
    joined3 = jnp.concatenate([near3[:, 0:128].astype(bf16), agg3.astype(bf16)], axis=0)
    z3 = nn(w3t, joined3) + b3
    act3 = gelu(z3)
    slope3 = gelu_slope(z3)
    root3 = norm_root(act3)
    top = (act3 * root3).astype(bf16)

    logits = nn(wht_low, top) + bh
    logits = jnp.where(class_id < classes, logits, -1e30)
    peak = jnp.max(logits, axis=0, keepdims=True)
    lse = peak + jnp.log(jnp.sum(jnp.exp(logits - peak), axis=0, keepdims=True))
    dlog = ((jnp.exp(logits - lse) - hot) * weight).astype(bf16)
    dtop = nn(wh_low, dlog)

    dz3 = pull_back(act3, slope3, root3, dtop)
    dj3 = nn(w3, dz3)
    dg3 = (dj3[hidden:] * rdeg3).astype(bf16)
    obs[2] = nt(far3, dg3).astype(bf16)
    sent = exchange(3, obs.at[2], ibs.at[2])
    dloc = nt(jnp.concatenate([dj3[0:hidden].astype(bf16), dg3], axis=1), spread)

    seg_a = 4 * hidden
    row_head = seg_a + 2 * finp
    row_bias = row_head + classp
    rows = gl.shape[1]

    def put(row, value):
        size = value.shape[0]
        gl[0, row : row + size, :] = value[:, 0:128].astype(bf16)
        gl[1, row : row + size, :] = value[:, 128:].astype(bf16)

    picked = jnp.sum(logits * hot, axis=0, keepdims=True)
    loss = jnp.sum((lse - picked) * weight, axis=1, keepdims=True)
    total = jnp.sum(weight, axis=1, keepdims=True)
    sc_lane = lax.broadcasted_iota(i32, (8, 128), 1)
    ssend[0] = jnp.where(sc_lane == 0, loss, jnp.where(sc_lane == 1, total, 0.0))
    ones = jnp.ones((16, 128), bf16)
    put(row_head, nt(dlog, top))
    bias_h = jnp.concatenate([nt(ones, dlog), jnp.zeros((16, hidden - classp), f32)], axis=1)
    put(2 * hidden, nt(joined3, dz3))
    bias_3 = nt(ones, dz3)
    finish(sent)
    dh2 = jnp.concatenate([ibs[2].astype(f32).T, dloc], axis=1) * keep_row

    dz2 = pull_back(act2, slope2, root2, dh2)
    dj2 = nn(w2, dz2)
    dg2 = (dj2[hidden:] * rdeg2).astype(bf16)
    obs[3] = nt(far2[...], dg2).astype(bf16)
    sent = exchange(4, obs.at[3], ibs.at[3])
    put(0, nt(joined2, dz2))

    used = []

    def hop(src, dst, axis, who):
        used.append(0)
        k = len(used) - 1
        copy = pltpu.make_async_remote_copy(
            src_ref=src, dst_ref=dst, send_sem=red_send.at[k], recv_sem=red_recv.at[k],
            device_id={axis: who}, device_id_type=MESH,
        )
        copy.start()
        return copy

    def z_mate(off):
        return lax.rem(zpos + off, nz) * 2 + ypos

    def rows_of(start, size):
        return pl.ds(pl.multiple_of(start, 16), size)

    ways = ((xpos, "rep", mate_x), (ypos, "dom", mate_y))

    def parts_of(segment):
        return [(base, size, ways[order], ways[1 - order]) for base, size, order in segment]

    def core_start(segment):
        base, size = segment[0][0], sum(p[1] for p in segment)
        at = slice(base, base + size)
        return [hop(gl.at[1 - core, at], rc.at[at], "rep", mate_c)]

    def core_done(segment):
        base, size = segment[0][0], sum(p[1] for p in segment)
        at = slice(base, base + size)
        acc[at, :] = gl[core, at, :].astype(f32) + rc[at, :].astype(f32)

    def one_start(segment):
        copies = []
        for base, size, (pos, axis, mate), _ in parts_of(segment):
            half = size // 2
            at = slice(base // 2, base // 2 + half)
            sb1[at, :] = acc[rows_of(base + (1 - pos) * half, half), :].astype(bf16)
            copies.append(hop(sb1.at[at], rb1.at[at], axis, mate))
        return copies

    def one_done(segment):
        for base, size, (pos, _, _), _ in parts_of(segment):
            half = size // 2
            keep = rows_of(base + pos * half, half)
            acc[keep, :] = acc[keep, :] + rb1[base // 2 : base // 2 + half, :].astype(f32)

    def two_start(segment):
        copies = []
        for base, size, (pos, _, _), (pos2, axis, mate) in parts_of(segment):
            half, quarter = size // 2, size // 4
            at = slice(base // 4, base // 4 + quarter)
            sb2[at, :] = acc[rows_of(base + pos * half + (1 - pos2) * quarter, quarter), :].astype(bf16)
            copies.append(hop(sb2.at[at], rb2.at[at], axis, mate))
        return copies

    def two_done(segment):
        for base, size, (pos, _, _), (pos2, _, _) in parts_of(segment):
            half, quarter = size // 2, size // 4
            keep = rows_of(base + pos * half + pos2 * quarter, quarter)
            acc[keep, :] = acc[keep, :] + rb2[base // 4 : base // 4 + quarter, :].astype(f32)

    def z_start(segment):
        copies = []
        for base, size, (pos, _, _), (pos2, _, _) in parts_of(segment):
            half, quarter, piece = size // 2, size // 4, size // (4 * nz)
            at = slice(base // 4, base // 4 + quarter)
            sbz[at, :] = acc[rows_of(base + pos * half + pos2 * quarter, quarter), :].astype(bf16)
            low = base // (4 * nz)
            for off in range(1, nz):
                to = lax.rem(zpos + off, nz)
                copies.append(
                    hop(
                        sbz.at[rows_of(base // 4 + to * piece, piece)],
                        rbz.at[off - 1, low : low + piece],
                        "dom",
                        z_mate(off),
                    )
                )
        return copies

    def z_done_and_spread(segment):
        copies = []
        for base, size, (pos, _, _), (pos2, _, _) in parts_of(segment):
            half, quarter, piece = size // 2, size // 4, size // (4 * nz)
            here = rows_of(base + pos * half + pos2 * quarter + zpos * piece, piece)
            low = base // (4 * nz)
            value = acc[here, :]
            for off in range(1, nz):
                value = value + rbz[off - 1, low : low + piece, :].astype(f32)
            gout[core, here, :] = value.astype(bf16)
            part = gout.at[core, here]
            for off in range(1, nz):
                copies.append(hop(part, part, "dom", z_mate(off)))
        return copies

    def spread_two(segment):
        copies = []
        for base, size, (pos, _, _), (pos2, axis, mate) in parts_of(segment):
            half, quarter = size // 2, size // 4
            part = gout.at[core, rows_of(base + pos * half + pos2 * quarter, quarter)]
            copies += [hop(part, part, axis, mate), hop(part, part, "rep", mate_c)]
        return copies

    def spread_one(segment):
        copies = []
        for base, size, (pos, axis, mate), (pos2, _, _) in parts_of(segment):
            half, quarter = size // 2, size // 4
            part = gout.at[core, rows_of(base + pos * half, half)]
            copies.append(hop(part, part, axis, mate))
            part = gout.at[core, rows_of(base + pos * half + (1 - pos2) * quarter, quarter)]
            copies.append(hop(part, part, "rep", mate_c))
        return copies

    def spread_core(segment):
        copies = []
        for base, size, (pos, _, _), _ in parts_of(segment):
            half = size // 2
            part = gout.at[core, rows_of(base + (1 - pos) * half, half)]
            copies.append(hop(part, part, "rep", mate_c))
        return copies

    rest = ((0, 2 * hidden, 0), (2 * hidden, 2 * hidden, 1))
    first = ((seg_a, 3 * hidden, 0), (seg_a + 3 * hidden, rows - seg_a - 3 * hidden, 1))
    sums = core_start(rest) + [hop(ssend.at[0], srecv.at[0], "rep", mate_c)]

    bias_2 = nt(jnp.ones((16, span), bf16), dz2)
    both = jnp.concatenate([dj2[0:hidden].astype(bf16), dg2], axis=1)
    gathered[0:hidden, :] = nt(both, chosen[...])
    finish(sums)
    core_done(rest)
    ssend[1] = ssend[0] + srecv[0]
    sums = one_start(rest) + [hop(ssend.at[1], srecv.at[1], "rep", mate_x)]
    finish(sent)
    back = flip(ibs[3])

    def layer_one_back(b, _):
        blk = pl.ds(pl.multiple_of(b * 256, 256), 256)
        grad = gathered[0:hidden, blk] + nn(back, pick[:, blk])
        h1t[:, blk] = pull_back(act1[:, blk], z1[:, blk], root1[0:1, blk], grad)
        return 0

    lax.fori_loop(0, nodes // 256, layer_one_back, 0)
    finish(sums)
    one_done(rest)
    ssend[2] = ssend[1] + srecv[1]
    sums = two_start(rest) + [hop(ssend.at[2], srecv.at[2], "dom", mate_y)]
    step_rows = finp // 2

    def first_grad(b, _):
        start = pl.multiple_of(b * step_rows, 16)
        value = nt(joined[pl.ds(start, step_rows), :], h1t[...])
        to = pl.multiple_of(seg_a + b * step_rows, 16)
        gl[0, pl.ds(to, step_rows), :] = value[:, 0:128].astype(bf16)
        gl[1, pl.ds(to, step_rows), :] = value[:, 128:].astype(bf16)
        return 0

    lax.fori_loop(0, 4, first_grad, 0)
    bias_1 = nt(jnp.ones((16, nodes), bf16), h1t[...])
    line = lax.broadcasted_iota(i32, (16, hidden), 0)
    put(
        row_bias,
        jnp.where(line == 0, bias_1, 0.0)
        + jnp.where(line == 1, bias_2, 0.0)
        + jnp.where(line == 2, bias_3, 0.0)
        + jnp.where(line == 3, bias_h, 0.0),
    )
    now = core_start(first)
    finish(sums)
    two_done(rest)
    ssend[3] = ssend[2] + srecv[2]
    szv[zpos] = ssend[3]
    sums = z_start(rest)
    for off in range(1, nz):
        sums.append(hop(ssend.at[3], szv.at[zpos], "dom", z_mate(off)))
    finish(now)
    core_done(first)
    now = one_start(first)
    finish(sums)
    sums = z_done_and_spread(rest)
    s_out[...] = szv[0] + szv[1] + szv[2] + szv[3]
    finish(now)
    one_done(first)
    now = two_start(first)
    finish(sums)
    sums = spread_two(rest)
    finish(now)
    two_done(first)
    now = z_start(first)
    finish(sums)
    sums = spread_one(rest)
    finish(now)
    now = z_done_and_spread(first)
    finish(sums)
    sums = spread_core(rest)
    finish(now)
    now = spread_two(first)
    finish(sums)
    finish(now)
    now = spread_one(first)
    finish(now)
    now = spread_core(first)
    finish(now)
    out = pltpu.make_async_copy(gout, g_out, load_sem.at[0])
    out.start()
    out.wait()


def summed_gradients(peers, cap, seeds, fan, codes, srow, scnt, lab, smask, xt, w1, wr, wht, bias):
    fin, nodes = xt.shape
    hidden = w1.shape[1]
    finp = round_up(fin, 16)
    wide = round_up(fin, 128)
    slots = peers * cap
    span = slots + round_up(seeds * (FAN_REST + 1), 128)
    classp = round_up(wht.shape[0], 16)
    rows = 4 * hidden + 2 * finp + classp + 16
    nz = peers // 2
    vmem = pltpu.VMEM
    sems = 60
    scratch = [
        vmem((2 * finp, nodes), bf16),
        vmem((finp, nodes), f32),
        vmem((slots, nodes), bf16),
        vmem((nodes, 2 * span), bf16),
        vmem((slots, span), bf16),
        vmem((256, nodes), bf16),
        vmem((256, nodes), bf16),
        vmem((nodes, slots), bf16),
        vmem((nodes, 128), f32),
        vmem((nodes // 8, 256), f32),
        vmem((nodes // 8, 256), f32),
        vmem((8, nodes), f32),
        vmem((32, nodes), bf16),
        vmem((16, span), f32),
        vmem(w1.shape, f32),
        vmem(wr.shape, f32),
        vmem((hidden, 2 * finp), bf16),
        vmem((hidden, nodes), f32),
        vmem((hidden, nodes), f32),
        vmem((8, nodes), f32),
        vmem((hidden, nodes), bf16),
        vmem((slots, wide), bf16),
        vmem((slots, wide), bf16),
        vmem((4, slots, hidden), bf16),
        vmem((4, slots, hidden), bf16),
        vmem((2, rows, 128), bf16),
        vmem((rows, 128), f32),
        vmem((rows, 128), bf16),
        vmem((rows // 2, 128), bf16),
        vmem((rows // 2, 128), bf16),
        vmem((rows // 4, 128), bf16),
        vmem((rows // 4, 128), bf16),
        vmem((rows // 4, 128), bf16),
        vmem((nz - 1, rows // (4 * nz), 128), bf16),
        vmem((2, rows, 128), bf16),
        vmem((4, 8, 128), f32),
        vmem((3, 8, 128), f32),
        vmem((nz, 8, 128), f32),
        pltpu.SemaphoreType.DMA((2,)),
        pltpu.SemaphoreType.DMA((5, peers - 1)),
        pltpu.SemaphoreType.DMA((5, peers - 1)),
        pltpu.SemaphoreType.DMA((sems,)),
        pltpu.SemaphoreType.DMA((sems,)),
    ]
    inside = pl.BlockSpec(memory_space=vmem)
    outside = pl.BlockSpec(memory_space=pl.ANY)
    return pl.pallas_call(
        functools.partial(graph_kernel, peers, cap, seeds, fan),
        out_shape=(
            jax.ShapeDtypeStruct((2, rows, 128), bf16),
            jax.ShapeDtypeStruct((8, 128), f32),
        ),
        in_specs=[inside] * 6 + [outside] * 2 + [inside] * 2,
        out_specs=(outside, inside),
        scratch_shapes=scratch,
        compiler_params=pltpu.CompilerParams(
            collective_id=0, has_side_effects=True, vmem_limit_bytes=48 * 2**20
        ),
        name="graph_step",
    )(codes, srow, scnt, lab, smask, xt, w1, wr, wht, bias)


def split_dot(a, b):
    high = a.astype(bf16)
    low = (a - high.astype(f32)).astype(bf16)
    return nn(high, b) + nn(low, b)


def three_dot(a, b):
    high = b.astype(bf16)
    low = (b - high.astype(f32)).astype(bf16)
    return split_dot(a, high) + nn(a.astype(bf16), low)


def update_kernel(
    fin,
    g_all, scalars, w1, wr, wht, bias, st1, rt1, stm, rtm, sts, rts, sth, rth, bm, bv,
    loss_o, total_o, norm_o, g1_o, gr_o, gh_o, m_o, v_o, l1_o, lm_o, ls_o, lh_o, n1_o, nr_o, nh_o, nb_o,
    n1_low, nr_low, nh_low,
    g1, g_mine, w_mine, full, gb,
):
    hidden = w1.shape[1]
    classes = wht.shape[0]
    classp = round_up(classes, 16)
    finp = round_up(fin, 16)
    seg_a = 4 * hidden
    part = lax.axis_index("rep")

    def grads(start, size):
        return jnp.concatenate(
            [g_all[0, start : start + size, :], g_all[1, start : start + size, :]], axis=1
        )

    total = scalars[0:1, 1:2]
    square = jnp.zeros((16, hidden), f32)
    for r in range(0, g_all.shape[1], 16):
        g = grads(r, 16).astype(f32)
        square = square + g * g
    square = jnp.sum(jnp.sum(square, axis=0, keepdims=True), axis=1, keepdims=True)
    norm = jnp.sqrt(square) / total
    scale = clip_limit / jnp.maximum(norm, clip_limit) / total
    loss_o[...] = scalars[0:1, 0:1]
    total_o[...] = total
    norm_o[...] = norm
    lift = (1.0 - decay) * scale * scale
    move = shampoo_rate * scale

    g1[0:fin, :] = grads(seg_a, finp)[0:fin].astype(f32)
    g1[fin : 2 * fin, :] = grads(seg_a + finp, finp)[0:fin].astype(f32)
    count = st1.shape[0]
    for i in range(2 * fin // count):

        @pl.when(part == i)
        def _():
            g_mine[...] = g1[i * count : (i + 1) * count, :]
            w_mine[...] = w1[i * count : (i + 1) * count, :]

    g_rows = g_mine[...]
    g_low = g1[...].astype(bf16)
    g1_o[...] = g_rows * scale
    l1_o[...] = decay * st1[...] + lift * nt(g_rows.astype(bf16), g_low)
    full[0] = nn(g1[...].T.astype(bf16), g_low)
    step = three_dot(split_dot(rt1[...], g_low), rts[0])
    fresh = w_mine[...] - move * step
    n1_o[...] = fresh
    n1_low[...] = fresh.astype(bf16)

    for i in range(2):
        g = grads(i * 2 * hidden, 2 * hidden)
        count = stm.shape[1]
        at = pl.ds(pl.multiple_of(part * count, count), count)
        base = pl.ds(pl.multiple_of(i * 2 * hidden + part * count, 16), count)
        g_rows = jnp.concatenate([g_all[0, base, :], g_all[1, base, :]], axis=1)
        gr_o[i] = g_rows.astype(f32) * scale
        lm_o[i] = decay * stm[i] + lift * nt(g_rows, g)
        full[1 + i] = nn(flip(g), g)
        step = three_dot(split_dot(rtm[i], g), rts[1 + i])
        fresh = wr[i, at, :] - move * step
        nr_o[i] = fresh
        nr_low[i] = fresh.astype(bf16)

    gt = grads(seg_a + 2 * finp, classp)
    full[3] = nn(flip(gt), gt)
    count = sts.shape[1]
    mine = pl.ds(pl.multiple_of(part * count, count), count)
    for i in range(4):
        ls_o[i] = decay * sts[i] + lift * full[i, mine, :]
    lh_o[...] = decay * sth[...] + lift * nt(gt, gt)[0:classes, 0:classes]
    root = rts[3, mine, :]
    high = root.astype(bf16)
    low = (root - high.astype(f32)).astype(bf16)
    left = (nt(gt, high) + nt(gt, low))[0:classes]
    step = three_dot(rth[...], left)
    gt_mine = jnp.zeros((classes, count), f32)
    wt_mine = jnp.zeros((classes, count), f32)
    gt_wide = gt.astype(f32)
    for i in range(hidden // count):
        here = slice(i * count, (i + 1) * count)
        gt_mine = jnp.where(part == i, gt_wide[0:classes, here], gt_mine)
        wt_mine = jnp.where(part == i, wht[:, here], wt_mine)
    gh_o[...] = gt_mine * scale
    fresh = wt_mine - move * step
    nh_o[...] = fresh
    nh_low[...] = fresh.astype(bf16)

    lines = grads(seg_a + 2 * finp + classp, 16).astype(f32)
    for i in range(4):
        gb[0:1, i * hidden : (i + 1) * hidden] = lines[i : i + 1, :]
    size = bias.shape[0]
    g = gb[0:1, 0:size] * scale
    bias = bias[...].reshape(1, size)
    new_m = beta_one * bm[...].reshape(1, size) + (1.0 - beta_one) * g
    new_v = beta_two * bv[...].reshape(1, size) + (1.0 - beta_two) * g * g
    m_hat = new_m / (1.0 - beta_one**STEP)
    v_hat = new_v / (1.0 - beta_two**STEP)
    m_o[...] = new_m.reshape(size)
    v_o[...] = new_v.reshape(size)
    fresh = bias - bias_rate * (m_hat / (jnp.sqrt(v_hat) + adam_eps) + weight_decay * bias)
    nb_o[...] = fresh.reshape(size)


def updates(fin, *args):
    g_all, scalars, w1, wr, wht, bias, st1, rt1, stm, rtm, sts, rts, sth, rth, bm, bv = args
    hidden = w1.shape[1]
    classes = wht.shape[0]
    count = sts.shape[1]
    n1 = (st1.shape[0], hidden)
    nr = (2, stm.shape[1], hidden)
    nh = (classes, count)

    def of(shape, kind=f32):
        return jax.ShapeDtypeStruct(shape, kind)

    one = of((1, 1))
    line = of(bias.shape)
    shapes = (
        one, one, one, of(n1), of(nr), of(nh), line, line,
        of(st1.shape), of(stm.shape), of(sts.shape), of(sth.shape),
        of(n1), of(nr), of(nh), line, of(n1, bf16), of(nr, bf16), of(nh, bf16),
    )
    inside = pl.BlockSpec(memory_space=pltpu.VMEM)
    return pl.pallas_call(
        functools.partial(update_kernel, fin),
        out_shape=shapes,
        in_specs=[inside] * len(args),
        out_specs=(inside,) * len(shapes),
        scratch_shapes=[
            pltpu.VMEM((2 * fin, hidden), f32),
            pltpu.VMEM(n1, f32),
            pltpu.VMEM(n1, f32),
            pltpu.VMEM((4, hidden, hidden), f32),
            pltpu.VMEM((1, 4 * hidden), f32),
        ],
        compiler_params=pltpu.CompilerParams(vmem_limit_bytes=40 * 2**20),
        name="update_step",
    )(*args)


def shards(
    features, nbr_index, nbr_mask, send_rows, send_count, labels, seed_mask,
    w_first, w_rest, w_head, biases,
    stat_big, root_big, stat_mid, root_mid, stat_sq, root_sq, stat_hr, root_hr, bias_m, bias_v,
):
    peers = send_rows.shape[2]
    cap = send_rows.shape[3]
    fin = features.shape[2]
    fan = nbr_index.shape[3]
    seeds = labels.shape[1]

    codes = jnp.where(nbr_mask[0] == 1, nbr_index[0], MASKED).astype(f32)

    g_all, scalars = summed_gradients(
        peers, cap, seeds, fan,
        jnp.swapaxes(codes, 1, 2),
        send_rows[0, 0], send_count[0], labels, seed_mask,
        jnp.swapaxes(features[0], 0, 1), w_first, w_rest, w_head.T, biases,
    )
    out = list(
        updates(
            fin, g_all, scalars, w_first, w_rest, w_head.T, biases,
            stat_big, root_big, stat_mid, root_mid, stat_sq, root_sq, stat_hr, root_hr,
            bias_m, bias_v,
        )
    )
    for i in (0, 1, 2):
        out[i] = out[i].reshape(())
    for i in (5, 14, 18):
        out[i] = out[i].T
    return tuple(out)


highest = lax.Precision.HIGHEST


def plain_activate(z):
    act = jax.nn.gelu(z, approximate=True)
    return act * lax.rsqrt(jnp.sum(act * act, axis=-1, keepdims=True) + norm_eps)


def plain_counts(nbr, mask, columns):
    nodes, slots = nbr.shape
    column_ids = jnp.arange(columns, dtype=jnp.int32)[None, :]
    mask_low = mask.astype(jnp.bfloat16)

    def add_slot(slot, total):
        picks = lax.dynamic_slice_in_dim(nbr, slot, 1, 1)
        weight = lax.dynamic_slice_in_dim(mask_low, slot, 1, 1)
        return total + (picks == column_ids).astype(jnp.bfloat16) * weight

    return lax.fori_loop(0, slots, add_slot, jnp.zeros((nodes, columns), jnp.bfloat16))


def plain_forward(h, weight, bias, nbr, mask, send_list, valid):
    nodes, width = h.shape
    hb = h.astype(jnp.bfloat16)
    outgoing = (
        jnp.take(hb, send_list, axis=0).reshape(valid.shape[0], valid.shape[1], width)
        * valid[:, :, None]
    )
    incoming = lax.all_to_all(outgoing, "dom", split_axis=0, concat_axis=0, tiled=True)
    table = jnp.concatenate([hb, incoming.reshape(-1, width)], axis=0)
    counts = plain_counts(nbr, mask, table.shape[0])
    degree = jnp.maximum(jnp.sum(mask, axis=1), 1).astype(jnp.float32)[:, None]
    gathered = jnp.dot(counts, table, preferred_element_type=jnp.float32)
    joined = jnp.concatenate([hb, (gathered / degree).astype(jnp.bfloat16)], axis=1)
    z = jnp.dot(joined, weight.astype(jnp.bfloat16), preferred_element_type=jnp.float32) + bias
    return (plain_activate(z), (joined, counts, degree, z))


def plain_backward(grad_out, weight, kept, send_list, valid, need_input):
    joined, counts, degree, z = kept
    nodes = joined.shape[0]
    width = joined.shape[1] // 2
    grad_z = jax.vjp(plain_activate, z)[1](grad_out)[0].astype(jnp.bfloat16)
    grad_w = jnp.einsum("nk,nh->kh", joined, grad_z, preferred_element_type=jnp.float32)
    grad_b = jnp.sum(grad_z.astype(jnp.float32), axis=0)
    if not need_input:
        return (grad_w, grad_b, None)
    grad_joined = jnp.einsum(
        "nh,kh->nk", grad_z, weight.astype(jnp.bfloat16), preferred_element_type=jnp.float32
    )
    grad_gathered = (grad_joined[:, width:] / degree).astype(jnp.bfloat16)
    grad_table = jnp.einsum("nj,nw->jw", counts, grad_gathered, preferred_element_type=jnp.float32)
    returned = (
        grad_table[nodes:].reshape(valid.shape[0], valid.shape[1], width).astype(jnp.bfloat16)
    )
    returned = lax.all_to_all(returned, "dom", split_axis=0, concat_axis=0, tiled=True)
    sent_back = (returned * valid[:, :, None]).reshape(-1, width)
    placement = (send_list[:, None] == jnp.arange(nodes, dtype=jnp.int32)[None, :]).astype(
        jnp.bfloat16
    )
    scattered = jnp.einsum("sn,sw->nw", placement, sent_back, preferred_element_type=jnp.float32)
    return (grad_w, grad_b, grad_joined[:, :width] + grad_table[:nodes] + scattered)


def plain_shampoo(grad, weight, left, left_root, right, right_root, part, right_split):
    count = left.shape[0]
    grad_rows = lax.dynamic_slice_in_dim(grad, part * count, count, 0)
    weight_rows = lax.dynamic_slice_in_dim(weight, part * count, count, 0)
    new_left = decay * left + (1.0 - decay) * jnp.dot(grad_rows, grad.T, precision=highest)
    if right_split:
        cols = right.shape[0]
        grad_cols = lax.dynamic_slice_in_dim(grad, part * cols, cols, 1)
        new_right = decay * right + (1.0 - decay) * jnp.dot(grad_cols.T, grad, precision=highest)
    else:
        new_right = decay * right + (1.0 - decay) * jnp.dot(grad.T, grad, precision=highest)
    step = jnp.dot(jnp.dot(left_root, grad, precision=highest), right_root, precision=highest)
    return (grad_rows, new_left, new_right, weight_rows - shampoo_rate * step)


def plain_shards(
    features,
    nbr_index,
    nbr_mask,
    send_rows,
    send_count,
    labels,
    seed_mask,
    w_first,
    w_rest,
    w_head,
    biases,
    stat_big,
    root_big,
    stat_mid,
    root_mid,
    stat_sq,
    root_sq,
    stat_hr,
    root_hr,
    bias_m,
    bias_v,
):
    hidden = w_rest.shape[2]
    peers = send_rows.shape[2]
    cap = send_rows.shape[3]
    send_list = send_rows.reshape(-1)
    valid = (jnp.arange(cap)[None, :] < send_count.reshape(peers, 1)).astype(jnp.bfloat16)
    weights = [w_first, w_rest[0], w_rest[1]]
    state = features[0].astype(jnp.float32)
    kept = []
    for level in range(3):
        state, saved = plain_forward(
            state,
            weights[level],
            biases[level * hidden : (level + 1) * hidden],
            nbr_index[0, level],
            nbr_mask[0, level],
            send_list,
            valid,
        )
        kept.append(saved)
    seeds = labels.shape[1]
    top = state[:seeds].astype(jnp.bfloat16)
    head_low_w = w_head.astype(jnp.bfloat16)
    logits = jnp.dot(top, head_low_w, preferred_element_type=jnp.float32) + biases[3 * hidden :]
    lse = jax.nn.logsumexp(logits, axis=1)
    onehot = (labels[0][:, None] == jnp.arange(logits.shape[1])[None, :]).astype(jnp.float32)
    picked = jnp.sum(logits * onehot, axis=1)
    seed_weight = seed_mask[0].astype(jnp.float32)
    loss_sum, seed_total = lax.psum(
        (jnp.sum((lse - picked) * seed_weight), jnp.sum(seed_weight)), ("dom", "rep")
    )
    grad_logits = (
        (jnp.exp(logits - lse[:, None]) - onehot) * (seed_weight / seed_total)[:, None]
    ).astype(jnp.bfloat16)
    grad_head = jnp.einsum("sh,sc->hc", top, grad_logits, preferred_element_type=jnp.float32)
    grad_hbias = jnp.sum(grad_logits.astype(jnp.float32), axis=0)
    grad_head, grad_hbias = (grad_head, grad_hbias)
    grad_top = jnp.einsum("sc,hc->sh", grad_logits, head_low_w, preferred_element_type=jnp.float32)
    grad_state = jnp.zeros(state.shape, jnp.float32).at[:seeds].set(grad_top)
    results = [None, None, None]
    for level in (2, 1, 0):
        grad_w, grad_b, grad_state = plain_backward(
            grad_state, weights[level], kept[level], send_list, valid, level > 0
        )
        results[level] = (grad_w, grad_b)
    grad_bias = jnp.concatenate([results[0][1], results[1][1], results[2][1], grad_hbias])
    grad_one, grad_two, grad_three = (results[0][0], results[1][0], results[2][0])
    grad_one, grad_two, grad_three, grad_head, grad_bias = lax.psum(
        (grad_one, grad_two, grad_three, grad_head, grad_bias), ("dom", "rep")
    )
    everything = (grad_one, grad_two, grad_three, grad_head, grad_bias)
    grad_norm = jnp.sqrt(sum((jnp.sum(g * g) for g in everything)))
    factor = clip_limit / jnp.maximum(grad_norm, clip_limit)
    grad_one, grad_two, grad_three, grad_head, grad_bias = [g * factor for g in everything]
    part = lax.axis_index("rep")
    head_rows = stat_sq.shape[1]
    head_root_rows = lax.dynamic_slice_in_dim(root_sq[3], part * head_rows, head_rows, 0)
    g_first, l_first, r_first, n_first = plain_shampoo(
        grad_one, w_first, stat_big, root_big, stat_sq[0], root_sq[0], part, True
    )
    g_mid0, l_mid0, r_mid0, n_mid0 = plain_shampoo(
        grad_two, w_rest[0], stat_mid[0], root_mid[0], stat_sq[1], root_sq[1], part, True
    )
    g_mid1, l_mid1, r_mid1, n_mid1 = plain_shampoo(
        grad_three, w_rest[1], stat_mid[1], root_mid[1], stat_sq[2], root_sq[2], part, True
    )
    g_head, l_head, r_head, n_head = plain_shampoo(
        grad_head, w_head, stat_sq[3], head_root_rows, stat_hr, root_hr, part, False
    )
    new_m = beta_one * bias_m + (1.0 - beta_one) * grad_bias
    new_v = beta_two * bias_v + (1.0 - beta_two) * grad_bias * grad_bias
    m_hat = new_m / (1.0 - beta_one**STEP)
    v_hat = new_v / (1.0 - beta_two**STEP)
    new_b = biases - bias_rate * (m_hat / (jnp.sqrt(v_hat) + adam_eps) + weight_decay * biases)
    new_rest = jnp.stack([n_mid0, n_mid1])
    return (
        loss_sum,
        seed_total,
        grad_norm,
        g_first,
        jnp.stack([g_mid0, g_mid1]),
        g_head,
        new_m,
        new_v,
        l_first,
        jnp.stack([l_mid0, l_mid1]),
        jnp.stack([r_first, r_mid0, r_mid1, l_head]),
        r_head,
        n_first,
        new_rest,
        n_head,
        new_b,
        n_first.astype(jnp.bfloat16),
        new_rest.astype(jnp.bfloat16),
        n_head.astype(jnp.bfloat16),
    )


def solution(mesh):
    placed = (
        P("rep", "dom", None),
        P("rep", None, "dom", None),
        P("rep", None, "dom", None),
        P("rep", "dom", None, None),
        P("rep", "dom", None),
        P("rep", "dom"),
        P("rep", "dom"),
        P(), P(), P(), P(),
        P("rep", None),
        P("rep", None),
        P(None, "rep", None),
        P(None, "rep", None),
        P(None, "rep", None),
        P(), P(), P(), P(), P(),
    )
    small = mesh.shape["rep"] == 4 and mesh.shape["dom"] == 8
    return jax.shard_map(
        shards if small else plain_shards,
        mesh=mesh,
        in_specs=placed,
        out_specs=(
            P(), P(), P(),
            P("rep", None), P(None, "rep", None), P("rep", None),
            P(), P(),
            P("rep", None), P(None, "rep", None), P(None, "rep", None), P(),
            P("rep", None), P(None, "rep", None), P("rep", None), P(),
            P("rep", None), P(None, "rep", None), P("rep", None),
        ),
        check_vma=False,
    )
```

```python
import functools

import jax
import jax.numpy as jnp
from jax import lax
from jax.experimental import pallas as pl
from jax.experimental.pallas import tpu as pltpu
from jax.sharding import PartitionSpec as P

STEP = 5
FAN_REST = 10

clip_limit = 0.0001
decay = 0.5
shampoo_rate = 1.0
beta_one = 0.9
beta_two = 0.999
bias_rate = 0.05
weight_decay = 0.01
adam_eps = 1e-08
norm_eps = 1e-06
MASKED = 8192

bf16 = jnp.bfloat16
f32 = jnp.float32
i32 = jnp.int32
MESH = pl.DeviceIdType.MESH


def nn(a, b):
    return jnp.dot(a, b, preferred_element_type=f32)


def nt(a, b):
    return lax.dot_general(a, b, (((1,), (1,)), ((), ())), preferred_element_type=f32)


def flip(a):
    return a.astype(f32).T.astype(a.dtype)


def round_up(a, b):
    return (a + b - 1) // b * b


def gelu(z):
    scale = 0.7978845608028654
    return z * (0.5 + 0.5 * jnp.tanh(z * (scale + (0.044715 * scale) * (z * z))))


def gelu_slope(z):
    scale = 0.7978845608028654
    square = z * z
    half = 0.5 + 0.5 * jnp.tanh(z * (scale + (0.044715 * scale) * square))
    return half + (half - half * half) * (z * (2.0 * scale + (6.0 * 0.044715 * scale) * square))


def norm_root(act, axis):
    return lax.rsqrt(jnp.sum(act * act, axis=axis, keepdims=True) + norm_eps)


def pull_back(act, slope, root, grad, axis):
    dot = jnp.sum(act * grad, axis=axis, keepdims=True)
    return (slope * (root * grad - act * (root * root * root * dot))).astype(bf16)


def as_column(row):
    return jnp.broadcast_to(row, (8, row.shape[1])).T[:, 0:1]


def widen(row, width, value=0):
    return jnp.concatenate([row, jnp.full((1, width - row.shape[1]), value, row.dtype)], axis=1)


def graph_kernel(
    peers, cap, seeds, fan,
    nbr_hbm, msk_hbm, xt_hbm, w1_hbm, wr_hbm, srow_hbm, scnt_hbm, lab_hbm, smask_hbm, wht_hbm, bias_hbm,
    g_out, s_out,
    nbr, msk, xt, srow, scnt, lab, smask, wht, bias, joined, near, chosen, far2, far2t, grad1, ctmp, crow, lrow, lcode, crow2, lrow2, rdeg,
    w1, wr, w1t, act1, slope1, root1, h1t, ob0, ib0, ob1, ib1, ob2, ib2, ob3, ib3, ob4, ib4, ob5, ib5,
    gl, acc, rc, sbq, rbq, sbz, rbz, gout, ssend, srecv, sqv, szv,
    load_sem, send_sem, recv_sem, red_send, red_recv,
):
    fin, nodes = xt.shape
    hidden = w1.shape[1]
    finp = round_up(fin, 16)
    slots = peers * cap
    table = nodes + slots
    groups = table // 128
    chunks = nodes // 128
    blocks = nodes // 256
    span = far2.shape[0]
    local = span - slots
    me = lax.axis_index("dom")
    rep = lax.axis_index("rep")
    core = lax.rem(rep, 2)
    xpos = rep // 2
    ypos = lax.rem(me, 2)
    zpos = me // 2
    nz = peers // 2
    mate_c = xpos * 2 + (1 - core)
    mate_x = (1 - xpos) * 2 + core
    mate_y = zpos * 2 + (1 - ypos)

    loads = [
        pltpu.make_async_copy(src, dst, load_sem.at[k])
        for k, (src, dst) in enumerate(
            (
                (srow_hbm, srow), (scnt_hbm, scnt), (xt_hbm, xt), (nbr_hbm, nbr), (msk_hbm, msk),
                (w1_hbm, w1), (wr_hbm, wr), (lab_hbm, lab), (smask_hbm, smask), (wht_hbm, wht), (bias_hbm, bias),
            )
        )
    ]
    for load in loads:
        load.start()
    barrier = pltpu.get_barrier_semaphore()
    for off in range(1, peers):
        pl.semaphore_signal(barrier, inc=1, device_id={"dom": lax.rem(me + off, peers)}, device_id_type=MESH)
    for mate in (mate_c, mate_x):
        pl.semaphore_signal(barrier, inc=1, device_id={"rep": mate}, device_id_type=MESH)
    mate_xy = {"dom": mate_y, "rep": mate_x}
    pl.semaphore_signal(barrier, inc=1, device_id=mate_xy, device_id_type=MESH)

    def exchange(stage, src, dst, same=False):
        size = dst.shape[0] // peers
        copies = []
        for off in range(1, peers):
            peer = lax.rem(me + off, peers)
            copies.append(
                pltpu.make_async_remote_copy(
                    src_ref=src if same else src.at[pl.ds(pl.multiple_of(peer * size, 16), size)],
                    dst_ref=dst.at[pl.ds(pl.multiple_of(me * size, 16), size)],
                    send_sem=send_sem.at[stage, off - 1],
                    recv_sem=recv_sem.at[stage, off - 1],
                    device_id={"dom": peer},
                    device_id_type=MESH,
                )
            )
        for c in copies:
            c.start()
        return copies

    started = []

    def finish(copies):
        for c in copies:
            c.wait_recv()
        started.extend(copies)

    loads[0].wait()
    loads[1].wait()
    count = jnp.broadcast_to(scnt[...], (peers, peers))
    count = jnp.where(
        lax.broadcasted_iota(i32, (peers, peers), 0) == lax.broadcasted_iota(i32, (peers, peers), 1), count, 0
    )
    count = jnp.sum(count.astype(f32), axis=1, keepdims=True)
    in_use = lax.broadcasted_iota(i32, (peers, cap), 1).astype(f32) < count
    slot = jnp.where(in_use, srow[...].astype(f32), -1.0)
    per = 128 // cap
    slot = jnp.concatenate([slot] * per, axis=1)
    owner = lax.broadcasted_iota(i32, (peers, 128), 0)
    place = lax.broadcasted_iota(i32, (peers, 128), 1) // cap
    send_row = jnp.concatenate(
        [
            jnp.sum(jnp.where(owner == place + t * per, slot, 0.0), axis=0, keepdims=True)
            for t in range(slots // 128)
        ],
        axis=1,
    )
    node_id = lax.broadcasted_iota(i32, (256, nodes), 1).astype(f32)
    send_col = as_column(send_row)
    for r in range(0, slots, 256):
        chosen[r : r + 256, :] = jnp.where(send_col[r : r + 256] == node_id, 1.0, 0.0).astype(bf16)
    line = lax.broadcasted_iota(i32, (16, nodes), 0)
    joined[finp - 16 : finp, :] = jnp.where(line == 16 - (finp - fin), 1.0, 0.0).astype(bf16)
    r_id = lax.broadcasted_iota(i32, (2 * seeds, local), 0)
    l_id = lax.broadcasted_iota(i32, (2 * seeds, local), 1)
    is_self = (r_id < seeds) & (l_id == r_id + FAN_REST * seeds)
    is_nbr = (r_id >= seeds) & (l_id < FAN_REST * seeds) & (lax.rem(l_id, seeds) == r_id - seeds)
    spread = jnp.where(is_self | is_nbr, 1.0, 0.0)
    spread_t = spread.T.astype(bf16)
    spread = spread.astype(bf16)
    loads[2].wait()
    joined[0:fin, :] = xt[...]
    ob0[:, finp:] = jnp.zeros((slots, ob0.shape[1] - finp), bf16)
    ob0[:, 0:finp] = nt(chosen[0:slots, :], joined[0:finp, :]).astype(bf16)
    for buf in (ib0, ib1, ib2, ib3, ib4, ib5):
        size = buf.shape[0] // peers
        buf[pl.ds(pl.multiple_of(me * size, 16), size), :] = jnp.zeros((size, buf.shape[1]), bf16)
    pl.semaphore_wait(barrier, peers - 1 + 3)
    sent = exchange(0, ob0, ib0)

    loads[3].wait()
    loads[4].wait()

    def codes(level, size, here):
        at = slice(0, size)
        return jnp.where(msk[level, at, 0, here] == 1, nbr[level, at, 0, here], MASKED).astype(f32)

    code3 = codes(2, FAN_REST, slice(0, 128))
    code3t = jnp.concatenate([code3, jnp.full((16 - FAN_REST, 128), float(MASKED), f32)], axis=0).T[0:seeds]
    degree = jnp.sum(jnp.where(code3t < float(MASKED), 1.0, 0.0), axis=1, keepdims=True)
    rdeg3 = 1.0 / jnp.maximum(degree, 1.0)
    tiled = jnp.concatenate([code3t] * peers, axis=0)
    r_id = lax.broadcasted_iota(i32, (peers * seeds, 128), 0)
    l_id = lax.broadcasted_iota(i32, (peers * seeds, 128), 1)
    wanted = jnp.where(l_id < cap, nodes + (r_id // seeds) * cap + l_id, -1).astype(f32)
    far3 = jnp.zeros(wanted.shape, f32)
    for k in range(FAN_REST):
        far3 = far3 + jnp.where(wanted == tiled[:, k : k + 1], 1.0, 0.0)
    ob5[...] = far3.astype(bf16)
    sent_far = exchange(5, ob5, ib5)

    fill = jnp.full((32 - fan, 128), float(MASKED), f32)
    fill2 = jnp.full((16 - FAN_REST, 128), float(MASKED), f32)
    for c in range(chunks):
        here = slice(c * 128, (c + 1) * 128)
        code = codes(0, fan, here)
        degree = jnp.sum((code < MASKED).astype(f32), axis=0, keepdims=True)
        rdeg[0:1, here] = 1.0 / jnp.maximum(degree, 1.0)
        code2 = jnp.concatenate([codes(1, FAN_REST, here), fill2], axis=0).astype(i32)
        ctmp[here, 0:64] = jnp.concatenate(
            [code, fill, (code2 >> 7).astype(f32), (code2 & 127).astype(f32)], axis=0
        ).T

    def grouped(source, count, width):
        each = 256 // width
        lane = lax.broadcasted_iota(i32, (count, 256), 1) // width
        code = jnp.zeros((count, 256), f32)
        for n in range(each):
            piece = source[pl.ds(n, count, stride=each), :]
            piece = jnp.concatenate([piece, piece], axis=1)
            piece = pltpu.roll(piece, n * width, 1) if n else piece
            code = jnp.where(lane == n, piece, code)
        code = code.astype(i32)
        return ((code >> 7) * each + lane).astype(f32), (code & 127).astype(f32)

    crow[...], lrow[...] = grouped(ctmp, nodes // 8, 32)

    lane = lax.broadcasted_iota(i32, (1, 128), 1)
    fits = 128 // seeds
    tiles = []
    for t in range(local // 128):
        tile = jnp.full((1, 128), -1.0, f32)
        for j in range(fits):
            k = t * fits + j
            here = lane // seeds == j
            if k < FAN_REST:
                piece = code3[k : k + 1, :]
                piece = pltpu.roll(piece, j * seeds, 1) if j else piece
                tile = jnp.where(here & (piece < nodes), piece, tile)
            elif k == FAN_REST:
                tile = jnp.where(here, (lane - j * seeds).astype(f32), tile)
        tiles.append(tile)
    local_col = as_column(jnp.concatenate(tiles, axis=1))
    for r in range(0, local, 256):
        chosen[slots + r : slots + r + 256, :] = jnp.where(
            local_col[r : r + 256] == node_id, 1.0, 0.0
        ).astype(bf16)
    keep = jnp.where(jnp.concatenate([send_col, local_col], axis=0) >= 0.0, 1.0, 0.0)
    found = nn(chosen[0:span, :], ctmp[...].astype(bf16))
    lcode[...] = pltpu.roll(found, 96, 1) * 128.0 + pltpu.roll(found, 80, 1)
    lane = lax.broadcasted_iota(i32, (span, 128), 1)
    degree = jnp.sum(
        jnp.where((lcode[...] < float(MASKED)) & (lane < FAN_REST), 1.0, 0.0), axis=1, keepdims=True
    )
    rdeg2 = 1.0 / jnp.maximum(degree, 1.0)
    crow2[...], lrow2[...] = grouped(lcode, span // 16, 16)

    rows_a = lax.broadcasted_iota(i32, (groups * 8, 256), 0).astype(f32)
    rows_b = lax.broadcasted_iota(i32, (128, 256), 0).astype(f32)
    rows_c = lax.broadcasted_iota(i32, (groups * 16, 256), 0).astype(f32)

    def list_counts(b, _):
        for p in range(16):
            g = b * 16 + p
            left = jnp.where(rows_c == crow2[pl.ds(g, 1), :], 1.0, 0.0).astype(bf16)
            right = jnp.where(rows_b == lrow2[pl.ds(g, 1), :], 1.0, 0.0).astype(bf16)
            value = nt(left, right).astype(bf16)
            for a in range(groups):
                tile = value[a * 16 : (a + 1) * 16]
                if a < chunks:
                    chosen[pl.ds(pl.multiple_of(span + g * 16, 16), 16), a * 128 : (a + 1) * 128] = tile
                else:
                    at = pl.ds(pl.multiple_of(g * 16, 16), 16)
                    far2[at, (a - chunks) * 128 : (a - chunks + 1) * 128] = tile
        return 0

    lax.fori_loop(0, span // 256, list_counts, 0)

    def build(b, _):
        for p in range(16):
            pair = []
            for half in range(2):
                g = b * 32 + p * 2 + half
                left = jnp.where(rows_a == crow[pl.ds(g, 1), :], 1.0, 0.0).astype(bf16)
                right = jnp.where(rows_b == lrow[pl.ds(g, 1), :], 1.0, 0.0).astype(bf16)
                pair.append(nt(left, right))
            at = pl.ds(pl.multiple_of(b * 256 + p * 16, 16), 16)
            for a in range(groups):
                tile = jnp.concatenate([pair[0][a * 8 : (a + 1) * 8], pair[1][a * 8 : (a + 1) * 8]], axis=0)
                near[at, a * 128 : (a + 1) * 128] = tile.astype(bf16)
        return 0

    lax.fori_loop(0, blocks, build, 0)

    for load in loads[5:]:
        load.wait()
    bias = bias[...].reshape(1, bias.shape[0])
    wpad = jnp.concatenate(
        [w1[0:fin, :], jnp.zeros((finp - fin, hidden), f32), w1[fin : 2 * fin, :], jnp.zeros((finp - fin, hidden), f32)],
        axis=0,
    )
    w1t[...] = wpad.T.astype(bf16)
    b1 = as_column(bias[0:1, 0:hidden])

    finish(sent)
    ibt = flip(ib0[...])[0:finp, :]

    def block(b):
        return pl.ds(b * 256 if isinstance(b, int) else pl.multiple_of(b * 256, 256), 256)

    def gather(b):
        blk = block(b)
        total = nt(joined[0:finp, :], near[blk, 0:nodes]) + nt(ibt, near[blk, nodes:])
        joined[finp:, blk] = (total * rdeg[0:1, blk]).astype(bf16)

    def product(b):
        blk = block(b)
        grad1[:, blk] = nn(w1t[...], joined[:, blk]) + b1

    def activate(b):
        blk = block(b)
        z = grad1[:, blk]
        act = gelu(z)
        slope1[:, blk] = gelu_slope(z)
        root = norm_root(act, 0)
        act1[:, blk] = act
        root1[0:1, blk] = root
        h1t[:, blk] = (act * root).astype(bf16)

    gather(0)
    far2t[...] = flip(far2[...])
    w2 = wr[0].astype(bf16)
    w3 = wr[1].astype(bf16)
    product(0)
    gather(1)

    def layer_one(b, _):
        activate(b - 2)
        product(b - 1)
        gather(b)
        return 0

    lax.fori_loop(2, blocks, layer_one, 0)
    activate(blocks - 2)
    product(blocks - 1)
    activate(blocks - 1)
    sent_rows = nt(chosen[0:slots, :], h1t[...]).astype(bf16)
    ob1[...] = sent_rows
    sent = exchange(1, ob1, ib1)

    own2 = nt(chosen[slots:, :], h1t[...])
    finish(sent_far)
    far3r = ib5[...].astype(f32)[:, 0:cap]
    spots = peers * cap
    r_id = lax.broadcasted_iota(i32, (peers * seeds, spots), 0) // seeds
    l_id = lax.broadcasted_iota(i32, (peers * seeds, spots), 1) // cap
    collect = jnp.where(r_id == l_id, jnp.concatenate([far3r] * peers, axis=1), 0.0)
    scatter = collect.T.astype(bf16)
    collect = collect.astype(bf16)

    finish(sent)

    def rows_two(own_self, own_sum, at):
        agg = (own_sum + nn(far2[at, :], ib1[...])) * rdeg2[at]
        both = jnp.concatenate([own_self, agg.astype(bf16)], axis=1)
        z = nn(both, w2) + bias[0:1, hidden : 2 * hidden]
        act = gelu(z)
        root = norm_root(act, 1)
        return both, z, act, root, (act * (root * keep[at])).astype(bf16)

    out_at, in_at = slice(0, slots), slice(slots, span)
    joined2a, z2a, act2a, root2a, h2a = rows_two(sent_rows, own2[local:span], out_at)
    ob2[...] = nn(collect, h2a).astype(bf16)
    sent = exchange(2, ob2, ib2)

    joined2b, z2b, act2b, root2b, h2b = rows_two(own2[0:local].astype(bf16), own2[span:], in_at)
    near3 = nn(spread, h2b)
    slope2b = gelu_slope(z2b)
    classes = wht.shape[0]
    classp = round_up(classes, 16)
    wht_low = jnp.concatenate([wht[...], jnp.zeros((classp - classes, hidden), f32)], axis=0).astype(bf16)
    bh = widen(bias[0:1, 3 * hidden : 3 * hidden + classes], classp)
    class_id = lax.broadcasted_iota(i32, (seeds, classp), 1)
    label = as_column(widen(lab[...].astype(f32), 128))[0:seeds]
    hot = jnp.where(class_id.astype(f32) == label, 1.0, 0.0)
    weight = as_column(widen(smask[...].astype(f32), 128))[0:seeds]
    finish(sent)
    total = near3[seeds:]
    for q in range(peers):
        total = total + ib2[q * seeds : (q + 1) * seeds, :].astype(f32)
    joined3 = jnp.concatenate([near3[0:seeds].astype(bf16), (total * rdeg3).astype(bf16)], axis=1)
    z3 = nn(joined3, w3) + bias[0:1, 2 * hidden : 3 * hidden]
    act3 = gelu(z3)
    slope3 = gelu_slope(z3)
    root3 = norm_root(act3, 1)
    top = (act3 * root3).astype(bf16)

    logits = nt(top, wht_low) + bh
    logits = jnp.where(class_id < classes, logits, -1e30)
    peak = jnp.max(logits, axis=1, keepdims=True)
    lse = peak + jnp.log(jnp.sum(jnp.exp(logits - peak), axis=1, keepdims=True))
    dlog = ((jnp.exp(logits - lse) - hot) * weight).astype(bf16)
    dtop = nn(dlog, wht_low)

    dz3 = pull_back(act3, slope3, root3, dtop, 1)
    dj3 = nt(dz3, w3)
    dg3 = (dj3[:, hidden:] * rdeg3).astype(bf16)
    ob3[...] = dg3
    sent = exchange(3, ob3, ib3, same=True)
    dloc = nn(spread_t, jnp.concatenate([dj3[:, 0:hidden].astype(bf16), dg3], axis=0))

    seg_a = 4 * hidden
    row_head = seg_a + 2 * finp
    row_bias = row_head + classp
    rows = gl.shape[1]

    def put(row, value):
        size = value.shape[0]
        gl[0, row : row + size, :] = value[:, 0:128].astype(bf16)
        gl[1, row : row + size, :] = value[:, 128:].astype(bf16)

    picked = jnp.sum(logits * hot, axis=1, keepdims=True)
    loss = jnp.sum((lse - picked) * weight, axis=0, keepdims=True)
    total = jnp.sum(weight, axis=0, keepdims=True)
    sc_lane = lax.broadcasted_iota(i32, (8, 128), 1)
    ssend[0] = jnp.where(sc_lane == 0, loss, jnp.where(sc_lane == 1, total, 0.0))
    dz2b = pull_back(act2b, slope2b, root2b, dloc * keep[in_at], 1)
    dj2b = nt(dz2b, w2)
    dg2b = (dj2b[:, hidden:] * rdeg2[in_at]).astype(bf16)
    near_ret = nn(far2t[:, in_at], dg2b)
    slope2a = gelu_slope(z2a)
    put(row_head, nn(dlog.astype(f32).T.astype(bf16), top))
    put(2 * hidden, nn(joined3.astype(f32).T.astype(bf16), dz3))
    bias_3 = jnp.sum(dz3.astype(f32), axis=0, keepdims=True)
    bias_h = widen(jnp.sum(dlog.astype(f32), axis=0, keepdims=True), hidden)
    finish(sent)

    dh2a = nn(scatter, ib3[...]) * keep[out_at]
    dz2a = pull_back(act2a, slope2a, root2a, dh2a, 1)
    dj2a = nt(dz2a, w2)
    dg2a = (dj2a[:, hidden:] * rdeg2[out_at]).astype(bf16)
    ob4[...] = (near_ret + nn(far2t[:, out_at], dg2a)).astype(bf16)
    sent = exchange(4, ob4, ib4)
    put(0, nn(flip(joined2a), dz2a) + nn(flip(joined2b), dz2b))

    used = []

    def hop(src, dst, who):
        used.append(0)
        k = len(used) - 1
        copy = pltpu.make_async_remote_copy(
            src_ref=src, dst_ref=dst, send_sem=red_send.at[k], recv_sem=red_recv.at[k],
            device_id=who, device_id_type=MESH,
        )
        copy.start()
        return copy

    def rows_of(start, size):
        return pl.ds(pl.multiple_of(start, 16), size)

    to_core = {"rep": mate_c}
    plane = (
        xpos * 2 + ypos,
        (
            ((1 - xpos) * 2 + ypos, {"rep": mate_x}),
            (xpos * 2 + 1 - ypos, {"dom": mate_y}),
            ((1 - xpos) * 2 + 1 - ypos, mate_xy),
        ),
    )
    others = [lax.rem(zpos + off, nz) for off in range(1, nz)]
    column = (zpos, tuple((to, {"dom": to * 2 + ypos}) for to in others))

    def summing(start, size, out_sem, one, two):
        (mine1, group1), (mine2, group2) = one, two
        quarter = size // (len(group1) + 1)
        piece = quarter // (len(group2) + 1)
        whole = slice(start, start + size)
        at1, at2 = start // 4, start // (4 * nz)
        at1, at2 = slice(at1, at1 + quarter), slice(at2, at2 + piece)
        kept = rows_of(start + mine1 * quarter, quarter)
        here = rows_of(start + mine1 * quarter + mine2 * piece, piece)
        copies = [hop(gl.at[1 - core, whole], rc.at[whole], to_core)]
        yield
        finish(copies)
        value = gl[core, whole, :].astype(f32) + rc[whole, :].astype(f32)
        acc[whole, :] = value
        sbq[whole, :] = value.astype(bf16)
        copies = [
            hop(sbq.at[rows_of(start + to * quarter, quarter)], rbq.at[k, at1], who)
            for k, (to, who) in enumerate(group1)
        ]
        yield
        finish(copies)
        value = acc[kept, :]
        for k in range(len(group1)):
            value = value + rbq[k, at1, :].astype(f32)
        acc[kept, :] = value
        sbz[at1, :] = value.astype(bf16)
        copies = [
            hop(sbz.at[rows_of(start // 4 + to * piece, piece)], rbz.at[k, at2], who)
            for k, (to, who) in enumerate(group2)
        ]
        yield
        finish(copies)
        value = acc[here, :]
        for k in range(len(group2)):
            value = value + rbz[k, at2, :].astype(f32)
        gout[core, here, :] = value.astype(bf16)
        part = gout.at[core, here]
        copies = [hop(part, part, who) for _, who in group2]
        yield
        finish(copies)
        part = gout.at[core, kept]
        copies = [hop(part, part, who) for _, who in group1]
        copies.append(hop(part, part, to_core))
        yield
        finish(copies)
        copies = []
        for to, _ in group1:
            part = gout.at[core, rows_of(start + to * quarter, quarter)]
            copies.append(hop(part, part, to_core))
        yield
        finish(copies)
        out = [
            pltpu.make_async_copy(gout.at[h, whole], g_out.at[h, whole], load_sem.at[out_sem + h])
            for h in range(2)
        ]
        for c in out:
            c.start()
        yield
        for c in out:
            c.wait()

    def summing_scalars():
        copies = [hop(ssend.at[0], srecv.at[0], to_core)]
        yield
        finish(copies)
        ssend[1] = ssend[0] + srecv[0]
        mine = plane[0]
        sqv[mine] = ssend[1]
        copies = [hop(ssend.at[1], sqv.at[mine], who) for _, who in plane[1]]
        yield
        finish(copies)
        ssend[2] = sqv[0] + sqv[1] + sqv[2] + sqv[3]
        szv[zpos] = ssend[2]
        copies = [hop(ssend.at[2], szv.at[zpos], who) for _, who in column[1]]
        yield
        finish(copies)
        total = szv[0]
        for k in range(1, nz):
            total = total + szv[k]
        s_out[...] = total

    def go_on(*runs):
        for run in runs:
            next(run, None)

    cut = seg_a + 2 * (4 * nz * 16)
    rest = summing(0, seg_a, 4, plane, column)
    first = summing(seg_a, cut - seg_a, 0, column, plane)
    second = summing(cut, rows - cut, 2, plane, column)
    scalars = summing_scalars()
    go_on(rest, scalars)

    bias_2 = jnp.sum(dz2a.astype(f32), axis=0, keepdims=True) + jnp.sum(dz2b.astype(f32), axis=0, keepdims=True)
    line = lax.broadcasted_iota(i32, (16, hidden), 0)
    put(
        row_bias,
        jnp.where(line == 1, bias_2, 0.0) + jnp.where(line == 2, bias_3, 0.0) + jnp.where(line == 3, bias_h, 0.0),
    )
    both = flip(
        jnp.concatenate(
            [dj2a[:, 0:hidden].astype(bf16), dj2b[:, 0:hidden].astype(bf16), dg2a, dg2b], axis=0
        )
    )
    grad1[...] = nn(both, chosen[...])
    go_on(rest, scalars)
    finish(sent)
    back = flip(ib4[...])

    def layer_one_back(b, _):
        blk = block(b)
        grad = grad1[:, blk] + nn(back, chosen[0:slots, blk])
        h1t[:, blk] = pull_back(act1[:, blk], slope1[:, blk], root1[0:1, blk], grad, 0)
        return 0

    lax.fori_loop(0, blocks, layer_one_back, 0)
    size = cut - seg_a
    put(seg_a, nt(joined[0:size, :], h1t[...]))
    go_on(first, rest, scalars)
    put(cut, nt(joined[size:, :], h1t[...]))
    go_on(second, first)
    for _ in range(5):
        go_on(second, first, rest, scalars)
    go_on(second, first)
    go_on(second)
    for c in started:
        c.wait_send()


def in_hbm(*arrays):
    return [pltpu.with_memory_space_constraint(a, pltpu.HBM) for a in arrays]


def summed_gradients(peers, cap, seeds, fan, nbr, msk, xt, w1, wr, srow, scnt, lab, smask, wht, bias):
    fin, nodes = xt.shape
    hidden = w1.shape[1]
    finp = round_up(fin, 16)
    wide = round_up(fin, 128)
    slots = peers * cap
    span = slots + round_up(seeds * (FAN_REST + 1), 256)
    classp = round_up(wht.shape[0], 16)
    rows = 4 * hidden + 2 * finp + classp + 16
    nz = peers // 2
    vmem = pltpu.VMEM
    sems = 64
    some = peers * seeds
    scratch = [
        vmem(nbr.shape, i32),
        vmem(msk.shape, i32),
        vmem(xt.shape, bf16),
        vmem(srow.shape, i32),
        vmem(scnt.shape, i32),
        vmem(lab.shape, i32),
        vmem(smask.shape, i32),
        vmem(wht.shape, f32),
        vmem(bias.shape, f32),
        vmem((2 * finp, nodes), bf16),
        vmem((nodes, nodes + slots), bf16),
        vmem((2 * span, nodes), bf16),
        vmem((span, slots), bf16),
        vmem((slots, span), bf16),
        vmem((hidden, nodes), f32),
        vmem((nodes, 128), f32),
        vmem((nodes // 8, 256), f32),
        vmem((nodes // 8, 256), f32),
        vmem((span, 128), f32),
        vmem((span // 16, 256), f32),
        vmem((span // 16, 256), f32),
        vmem((8, nodes), f32),
        vmem(w1.shape, f32),
        vmem(wr.shape, f32),
        vmem((hidden, 2 * finp), bf16),
        vmem((hidden, nodes), f32),
        vmem((hidden, nodes), f32),
        vmem((8, nodes), f32),
        vmem((hidden, nodes), bf16),
        vmem((slots, wide), bf16),
        vmem((slots, wide), bf16),
        vmem((slots, hidden), bf16),
        vmem((slots, hidden), bf16),
        vmem((some, hidden), bf16),
        vmem((some, hidden), bf16),
        vmem((seeds, hidden), bf16),
        vmem((some, hidden), bf16),
        vmem((slots, hidden), bf16),
        vmem((slots, hidden), bf16),
        vmem((some, 128), bf16),
        vmem((some, 128), bf16),
        vmem((2, rows, 128), bf16),
        vmem((rows, 128), f32),
        vmem((rows, 128), bf16),
        vmem((rows, 128), bf16),
        vmem((3, rows // 4, 128), bf16),
        vmem((rows // 4, 128), bf16),
        vmem((nz - 1, rows // (4 * nz), 128), bf16),
        vmem((2, rows, 128), bf16),
        vmem((4, 8, 128), f32),
        vmem((3, 8, 128), f32),
        vmem((4, 8, 128), f32),
        vmem((nz, 8, 128), f32),
        pltpu.SemaphoreType.DMA((11,)),
        pltpu.SemaphoreType.DMA((6, peers - 1)),
        pltpu.SemaphoreType.DMA((6, peers - 1)),
        pltpu.SemaphoreType.DMA((sems,)),
        pltpu.SemaphoreType.DMA((sems,)),
    ]
    inside = pl.BlockSpec(memory_space=vmem)
    outside = pl.BlockSpec(memory_space=pl.ANY)
    return pl.pallas_call(
        functools.partial(graph_kernel, peers, cap, seeds, fan),
        out_shape=(
            jax.ShapeDtypeStruct((2, rows, 128), bf16),
            jax.ShapeDtypeStruct((8, 128), f32),
        ),
        in_specs=[outside] * 11,
        out_specs=(outside, inside),
        scratch_shapes=scratch,
        compiler_params=pltpu.CompilerParams(
            collective_id=0, has_side_effects=True, vmem_limit_bytes=47 * 2**20
        ),
        cost_estimate=pl.CostEstimate(flops=24 * 10**9, bytes_accessed=12 * 2**20, transcendentals=2**20),
        name="graph_step",
    )(*in_hbm(nbr, msk, xt, w1, wr, srow, scnt, lab, smask, wht, bias))


def split_dot(a, b):
    high = a.astype(bf16)
    low = (a - high.astype(f32)).astype(bf16)
    return nn(high, b) + nn(low, b)


def three_dot(a, b):
    high = b.astype(bf16)
    low = (b - high.astype(f32)).astype(bf16)
    return split_dot(a, high) + nn(a.astype(bf16), low)


def update_kernel(
    fin,
    g_all, scalars, wht, bias, sth, rth, bm, bv,
    w1, wr, st1, rt1, stm, rtm, sts, rts,
    loss_o, total_o, norm_o, gh_o, m_o, v_o, lh_o, nh_o, nb_o, nh_low,
    g1_hbm, gr_hbm, l1_hbm, lm_hbm, ls_hbm, n1_hbm, nr_hbm, n1_low_hbm, nr_low_hbm,
    g1_o, gr_o, l1_o, lm_o, ls_o, n1_o, nr_o, n1_low, nr_low,
    g1, g_mine, w_mine, full, gb, out_sem,
):
    hidden = w1.shape[1]
    classes = wht.shape[0]
    classp = round_up(classes, 16)
    finp = round_up(fin, 16)
    seg_a = 4 * hidden
    part = lax.axis_index("rep")

    stores = []

    def store(src, dst):
        copy = pltpu.make_async_copy(src, dst, out_sem.at[len(stores)])
        stores.append(copy)
        copy.start()

    def grads(start, size):
        return jnp.concatenate(
            [g_all[0, start : start + size, :], g_all[1, start : start + size, :]], axis=1
        )

    total = scalars[0:1, 1:2]
    square = jnp.zeros((16, hidden), f32)
    spare = lax.broadcasted_iota(i32, (16, hidden), 0) >= 16 - (finp - fin)
    for r in range(0, g_all.shape[1], 16):
        g = grads(r, 16).astype(f32)
        if r == seg_a + 2 * finp - 16:
            g = jnp.where(spare, 0.0, g)
        square = square + g * g
    square = jnp.sum(jnp.sum(square, axis=0, keepdims=True), axis=1, keepdims=True)
    norm = jnp.sqrt(square) / total
    scale = clip_limit / jnp.maximum(norm, clip_limit) / total
    loss_o[...] = scalars[0:1, 0:1]
    total_o[...] = total
    norm_o[...] = norm
    lift = (1.0 - decay) * scale * scale
    move = shampoo_rate * scale

    g1[0:fin, :] = grads(seg_a, finp)[0:fin].astype(f32)
    g1[fin : 2 * fin, :] = grads(seg_a + finp, finp)[0:fin].astype(f32)
    count = st1.shape[0]
    g_low = g1[...].astype(bf16)
    full[0] = nn(g1[...].T.astype(bf16), g_low)
    half = split_dot(rt1[...], g_low)
    for i in range(2 * fin // count):

        @pl.when(part == i)
        def _():
            g_mine[...] = g1[i * count : (i + 1) * count, :]
            w_mine[...] = w1[i * count : (i + 1) * count, :]

    g_rows = g_mine[...]
    g1_o[...] = g_rows * scale
    store(g1_o, g1_hbm)
    fresh = w_mine[...] - move * three_dot(half, rts[0])
    n1_o[...] = fresh
    n1_low[...] = fresh.astype(bf16)
    store(n1_o, n1_hbm)
    store(n1_low, n1_low_hbm)
    product = nt(g_rows.astype(bf16), g_low)
    l1_o[...] = decay * st1[...] + lift * product
    store(l1_o, l1_hbm)

    count = stm.shape[1]
    at = pl.ds(pl.multiple_of(part * count, count), count)
    products = []
    for i in range(2):
        g = grads(i * 2 * hidden, 2 * hidden)
        base = pl.ds(pl.multiple_of(i * 2 * hidden + part * count, 16), count)
        g_rows = jnp.concatenate([g_all[0, base, :], g_all[1, base, :]], axis=1)
        gr_o[i] = g_rows.astype(f32) * scale
        full[1 + i] = nn(flip(g), g)
        products.append((nt(g_rows, g), three_dot(split_dot(rtm[i], g), rts[1 + i])))
    store(gr_o, gr_hbm)
    for i, (product, step) in enumerate(products):
        lm_o[i] = decay * stm[i] + lift * product
        fresh = wr[i, at, :] - move * step
        nr_o[i] = fresh
        nr_low[i] = fresh.astype(bf16)
    store(lm_o, lm_hbm)
    store(nr_o, nr_hbm)
    store(nr_low, nr_low_hbm)

    gt = grads(seg_a + 2 * finp, classp)
    full[3] = nn(flip(gt), gt)
    count = sts.shape[1]
    mine = pl.ds(pl.multiple_of(part * count, count), count)
    for i in range(4):
        ls_o[i] = decay * sts[i] + lift * full[i, mine, :]
    store(ls_o, ls_hbm)
    lh_o[...] = decay * sth[...] + lift * nt(gt, gt)[0:classes, 0:classes]
    root = rts[3, mine, :]
    high = root.astype(bf16)
    low = (root - high.astype(f32)).astype(bf16)
    left = (nt(gt, high) + nt(gt, low))[0:classes]
    step = three_dot(rth[...], left)
    gt_mine = jnp.zeros((classes, count), f32)
    wt_mine = jnp.zeros((classes, count), f32)
    gt_wide = gt.astype(f32)
    for i in range(hidden // count):
        here = slice(i * count, (i + 1) * count)
        gt_mine = jnp.where(part == i, gt_wide[0:classes, here], gt_mine)
        wt_mine = jnp.where(part == i, wht[:, here], wt_mine)
    gh_o[...] = gt_mine * scale
    fresh = wt_mine - move * step
    nh_o[...] = fresh
    nh_low[...] = fresh.astype(bf16)

    lines = grads(seg_a + 2 * finp + classp, 16).astype(f32)
    gb[0:1, 0:hidden] = grads(seg_a + finp - 16, 16).astype(f32)[fin - finp + 16 : fin - finp + 17, :]
    for i in range(1, 4):
        gb[0:1, i * hidden : (i + 1) * hidden] = lines[i : i + 1, :]
    size = bias.shape[0]
    g = gb[0:1, 0:size] * scale
    bias = bias[...].reshape(1, size)
    new_m = beta_one * bm[...].reshape(1, size) + (1.0 - beta_one) * g
    new_v = beta_two * bv[...].reshape(1, size) + (1.0 - beta_two) * g * g
    m_hat = new_m / (1.0 - beta_one**STEP)
    v_hat = new_v / (1.0 - beta_two**STEP)
    m_o[...] = new_m.reshape(size)
    v_o[...] = new_v.reshape(size)
    fresh = bias - bias_rate * (m_hat / (jnp.sqrt(v_hat) + adam_eps) + weight_decay * bias)
    nb_o[...] = fresh.reshape(size)
    for copy in stores:
        copy.wait()


def updates(fin, g_all, scalars, w1, wr, wht, bias, st1, rt1, stm, rtm, sts, rts, sth, rth, bm, bv):
    hidden = w1.shape[1]
    classes = wht.shape[0]
    count = sts.shape[1]
    n1 = (st1.shape[0], hidden)
    nr = (2, stm.shape[1], hidden)
    nh = (classes, count)

    def of(shape, kind=f32):
        return jax.ShapeDtypeStruct(shape, kind)

    def room(a):
        return pltpu.VMEM(a.shape, a.dtype)

    one = of((1, 1))
    line = of(bias.shape)
    small = [one, one, one, of(nh), line, line, of(sth.shape), of(nh), line, of(nh, bf16)]
    large = [of(n1), of(nr), of(st1.shape), of(stm.shape), of(sts.shape), of(n1), of(nr), of(n1, bf16), of(nr, bf16)]
    loaded = [w1, wr, st1, rt1, stm, rtm, sts, rts]
    inside = pl.BlockSpec(memory_space=pltpu.VMEM)
    outside = pl.BlockSpec(memory_space=pl.ANY)
    (loss, total, norm, gh, m, v, lh, nh_new, nb, nh_low, g1, gr, l1, lm, ls, n1_new, nr_new, n1_low, nr_low) = pl.pallas_call(
        functools.partial(update_kernel, fin),
        out_shape=tuple(small + large),
        in_specs=[inside] * (8 + len(loaded)),
        out_specs=(inside,) * len(small) + (outside,) * len(large),
        scratch_shapes=[room(a) for a in large] + [
            pltpu.VMEM((2 * fin, hidden), f32),
            pltpu.VMEM(n1, f32),
            pltpu.VMEM(n1, f32),
            pltpu.VMEM((4, hidden, hidden), f32),
            pltpu.VMEM((1, 4 * hidden), f32),
            pltpu.SemaphoreType.DMA((len(large),)),
        ],
        compiler_params=pltpu.CompilerParams(vmem_limit_bytes=40 * 2**20),
        name="update_step",
    )(g_all, scalars, wht, bias, sth, rth, bm, bv, *loaded)
    return [
        loss, total, norm, g1, gr, gh, m, v, l1, lm, ls, lh, n1_new, nr_new, nh_new, nb, n1_low, nr_low, nh_low
    ]


def shards(
    features, nbr_index, nbr_mask, send_rows, send_count, labels, seed_mask,
    w_first, w_rest, w_head, biases,
    stat_big, root_big, stat_mid, root_mid, stat_sq, root_sq, stat_hr, root_hr, bias_m, bias_v,
):
    peers = send_rows.shape[2]
    cap = send_rows.shape[3]
    fin = features.shape[2]
    fan = nbr_index.shape[3]
    seeds = labels.shape[1]

    def lines(a):
        return jnp.transpose(a, (1, 3, 0, 2))

    g_all, scalars = summed_gradients(
        peers, cap, seeds, fan,
        lines(nbr_index), lines(nbr_mask), jnp.swapaxes(features[0], 0, 1), w_first, w_rest,
        send_rows[0, 0], send_count[0], labels, seed_mask, w_head.T, biases,
    )
    out = list(
        updates(
            fin, g_all, scalars, w_first, w_rest, w_head.T, biases,
            stat_big, root_big, stat_mid, root_mid, stat_sq, root_sq, stat_hr, root_hr,
            bias_m, bias_v,
        )
    )
    for i in (0, 1, 2):
        out[i] = out[i].reshape(())
    for i in (5, 14, 18):
        out[i] = out[i].T
    return tuple(out)


highest = lax.Precision.HIGHEST


def plain_activate(z):
    act = jax.nn.gelu(z, approximate=True)
    return act * lax.rsqrt(jnp.sum(act * act, axis=-1, keepdims=True) + norm_eps)


def plain_counts(nbr, mask, columns):
    nodes, slots = nbr.shape
    column_ids = jnp.arange(columns, dtype=jnp.int32)[None, :]
    mask_low = mask.astype(jnp.bfloat16)

    def add_slot(slot, total):
        picks = lax.dynamic_slice_in_dim(nbr, slot, 1, 1)
        weight = lax.dynamic_slice_in_dim(mask_low, slot, 1, 1)
        return total + (picks == column_ids).astype(jnp.bfloat16) * weight

    return lax.fori_loop(0, slots, add_slot, jnp.zeros((nodes, columns), jnp.bfloat16))


def plain_forward(h, weight, bias, nbr, mask, send_list, valid):
    nodes, width = h.shape
    hb = h.astype(jnp.bfloat16)
    outgoing = (
        jnp.take(hb, send_list, axis=0).reshape(valid.shape[0], valid.shape[1], width)
        * valid[:, :, None]
    )
    incoming = lax.all_to_all(outgoing, "dom", split_axis=0, concat_axis=0, tiled=True)
    table = jnp.concatenate([hb, incoming.reshape(-1, width)], axis=0)
    counts = plain_counts(nbr, mask, table.shape[0])
    degree = jnp.maximum(jnp.sum(mask, axis=1), 1).astype(jnp.float32)[:, None]
    gathered = jnp.dot(counts, table, preferred_element_type=jnp.float32)
    joined = jnp.concatenate([hb, (gathered / degree).astype(jnp.bfloat16)], axis=1)
    z = jnp.dot(joined, weight.astype(jnp.bfloat16), preferred_element_type=jnp.float32) + bias
    return (plain_activate(z), (joined, counts, degree, z))


def plain_backward(grad_out, weight, kept, send_list, valid, need_input):
    joined, counts, degree, z = kept
    nodes = joined.shape[0]
    width = joined.shape[1] // 2
    grad_z = jax.vjp(plain_activate, z)[1](grad_out)[0].astype(jnp.bfloat16)
    grad_w = jnp.einsum("nk,nh->kh", joined, grad_z, preferred_element_type=jnp.float32)
    grad_b = jnp.sum(grad_z.astype(jnp.float32), axis=0)
    if not need_input:
        return (grad_w, grad_b, None)
    grad_joined = jnp.einsum(
        "nh,kh->nk", grad_z, weight.astype(jnp.bfloat16), preferred_element_type=jnp.float32
    )
    grad_gathered = (grad_joined[:, width:] / degree).astype(jnp.bfloat16)
    grad_table = jnp.einsum("nj,nw->jw", counts, grad_gathered, preferred_element_type=jnp.float32)
    returned = (
        grad_table[nodes:].reshape(valid.shape[0], valid.shape[1], width).astype(jnp.bfloat16)
    )
    returned = lax.all_to_all(returned, "dom", split_axis=0, concat_axis=0, tiled=True)
    sent_back = (returned * valid[:, :, None]).reshape(-1, width)
    placement = (send_list[:, None] == jnp.arange(nodes, dtype=jnp.int32)[None, :]).astype(
        jnp.bfloat16
    )
    scattered = jnp.einsum("sn,sw->nw", placement, sent_back, preferred_element_type=jnp.float32)
    return (grad_w, grad_b, grad_joined[:, :width] + grad_table[:nodes] + scattered)


def plain_shampoo(grad, weight, left, left_root, right, right_root, part, right_split):
    count = left.shape[0]
    grad_rows = lax.dynamic_slice_in_dim(grad, part * count, count, 0)
    weight_rows = lax.dynamic_slice_in_dim(weight, part * count, count, 0)
    new_left = decay * left + (1.0 - decay) * jnp.dot(grad_rows, grad.T, precision=highest)
    if right_split:
        cols = right.shape[0]
        grad_cols = lax.dynamic_slice_in_dim(grad, part * cols, cols, 1)
        new_right = decay * right + (1.0 - decay) * jnp.dot(grad_cols.T, grad, precision=highest)
    else:
        new_right = decay * right + (1.0 - decay) * jnp.dot(grad.T, grad, precision=highest)
    step = jnp.dot(jnp.dot(left_root, grad, precision=highest), right_root, precision=highest)
    return (grad_rows, new_left, new_right, weight_rows - shampoo_rate * step)


def plain_shards(
    features,
    nbr_index,
    nbr_mask,
    send_rows,
    send_count,
    labels,
    seed_mask,
    w_first,
    w_rest,
    w_head,
    biases,
    stat_big,
    root_big,
    stat_mid,
    root_mid,
    stat_sq,
    root_sq,
    stat_hr,
    root_hr,
    bias_m,
    bias_v,
):
    hidden = w_rest.shape[2]
    peers = send_rows.shape[2]
    cap = send_rows.shape[3]
    send_list = send_rows.reshape(-1)
    valid = (jnp.arange(cap)[None, :] < send_count.reshape(peers, 1)).astype(jnp.bfloat16)
    weights = [w_first, w_rest[0], w_rest[1]]
    state = features[0].astype(jnp.float32)
    kept = []
    for level in range(3):
        state, saved = plain_forward(
            state,
            weights[level],
            biases[level * hidden : (level + 1) * hidden],
            nbr_index[0, level],
            nbr_mask[0, level],
            send_list,
            valid,
        )
        kept.append(saved)
    seeds = labels.shape[1]
    top = state[:seeds].astype(jnp.bfloat16)
    head_low_w = w_head.astype(jnp.bfloat16)
    logits = jnp.dot(top, head_low_w, preferred_element_type=jnp.float32) + biases[3 * hidden :]
    lse = jax.nn.logsumexp(logits, axis=1)
    onehot = (labels[0][:, None] == jnp.arange(logits.shape[1])[None, :]).astype(jnp.float32)
    picked = jnp.sum(logits * onehot, axis=1)
    seed_weight = seed_mask[0].astype(jnp.float32)
    loss_sum, seed_total = lax.psum(
        (jnp.sum((lse - picked) * seed_weight), jnp.sum(seed_weight)), ("dom", "rep")
    )
    grad_logits = (
        (jnp.exp(logits - lse[:, None]) - onehot) * (seed_weight / seed_total)[:, None]
    ).astype(jnp.bfloat16)
    grad_head = jnp.einsum("sh,sc->hc", top, grad_logits, preferred_element_type=jnp.float32)
    grad_hbias = jnp.sum(grad_logits.astype(jnp.float32), axis=0)
    grad_head, grad_hbias = (grad_head, grad_hbias)
    grad_top = jnp.einsum("sc,hc->sh", grad_logits, head_low_w, preferred_element_type=jnp.float32)
    grad_state = jnp.zeros(state.shape, jnp.float32).at[:seeds].set(grad_top)
    results = [None, None, None]
    for level in (2, 1, 0):
        grad_w, grad_b, grad_state = plain_backward(
            grad_state, weights[level], kept[level], send_list, valid, level > 0
        )
        results[level] = (grad_w, grad_b)
    grad_bias = jnp.concatenate([results[0][1], results[1][1], results[2][1], grad_hbias])
    grad_one, grad_two, grad_three = (results[0][0], results[1][0], results[2][0])
    grad_one, grad_two, grad_three, grad_head, grad_bias = lax.psum(
        (grad_one, grad_two, grad_three, grad_head, grad_bias), ("dom", "rep")
    )
    everything = (grad_one, grad_two, grad_three, grad_head, grad_bias)
    grad_norm = jnp.sqrt(sum((jnp.sum(g * g) for g in everything)))
    factor = clip_limit / jnp.maximum(grad_norm, clip_limit)
    grad_one, grad_two, grad_three, grad_head, grad_bias = [g * factor for g in everything]
    part = lax.axis_index("rep")
    head_rows = stat_sq.shape[1]
    head_root_rows = lax.dynamic_slice_in_dim(root_sq[3], part * head_rows, head_rows, 0)
    g_first, l_first, r_first, n_first = plain_shampoo(
        grad_one, w_first, stat_big, root_big, stat_sq[0], root_sq[0], part, True
    )
    g_mid0, l_mid0, r_mid0, n_mid0 = plain_shampoo(
        grad_two, w_rest[0], stat_mid[0], root_mid[0], stat_sq[1], root_sq[1], part, True
    )
    g_mid1, l_mid1, r_mid1, n_mid1 = plain_shampoo(
        grad_three, w_rest[1], stat_mid[1], root_mid[1], stat_sq[2], root_sq[2], part, True
    )
    g_head, l_head, r_head, n_head = plain_shampoo(
        grad_head, w_head, stat_sq[3], head_root_rows, stat_hr, root_hr, part, False
    )
    new_m = beta_one * bias_m + (1.0 - beta_one) * grad_bias
    new_v = beta_two * bias_v + (1.0 - beta_two) * grad_bias * grad_bias
    m_hat = new_m / (1.0 - beta_one**STEP)
    v_hat = new_v / (1.0 - beta_two**STEP)
    new_b = biases - bias_rate * (m_hat / (jnp.sqrt(v_hat) + adam_eps) + weight_decay * biases)
    new_rest = jnp.stack([n_mid0, n_mid1])
    return (
        loss_sum,
        seed_total,
        grad_norm,
        g_first,
        jnp.stack([g_mid0, g_mid1]),
        g_head,
        new_m,
        new_v,
        l_first,
        jnp.stack([l_mid0, l_mid1]),
        jnp.stack([r_first, r_mid0, r_mid1, l_head]),
        r_head,
        n_first,
        new_rest,
        n_head,
        new_b,
        n_first.astype(jnp.bfloat16),
        new_rest.astype(jnp.bfloat16),
        n_head.astype(jnp.bfloat16),
    )


def solution(mesh):
    placed = (
        P("rep", "dom", None),
        P("rep", None, "dom", None),
        P("rep", None, "dom", None),
        P("rep", "dom", None, None),
        P("rep", "dom", None),
        P("rep", "dom"),
        P("rep", "dom"),
        P(), P(), P(), P(),
        P("rep", None),
        P("rep", None),
        P(None, "rep", None),
        P(None, "rep", None),
        P(None, "rep", None),
        P(), P(), P(), P(), P(),
    )
    small = mesh.shape["rep"] == 4 and mesh.shape["dom"] == 8
    return jax.shard_map(
        shards if small else plain_shards,
        mesh=mesh,
        in_specs=placed,
        out_specs=(
            P(), P(), P(),
            P("rep", None), P(None, "rep", None), P("rep", None),
            P(), P(),
            P("rep", None), P(None, "rep", None), P(None, "rep", None), P(),
            P("rep", None), P(None, "rep", None), P("rep", None), P(),
            P("rep", None), P(None, "rep", None), P("rep", None),
        ),
        check_vma=False,
    )
```

```python
import functools

import jax
import jax.numpy as jnp
from jax import lax
from jax.experimental import pallas as pl
from jax.experimental.pallas import tpu as pltpu
from jax.sharding import PartitionSpec as P

STEP = 5
FAN_REST = 10

clip_limit = 0.0001
decay = 0.5
shampoo_rate = 1.0
beta_one = 0.9
beta_two = 0.999
bias_rate = 0.05
weight_decay = 0.01
adam_eps = 1e-08
norm_eps = 1e-06
MASKED = 8192

bf16 = jnp.bfloat16
f32 = jnp.float32
i32 = jnp.int32
MESH = pl.DeviceIdType.MESH


def nn(a, b):
    return jnp.dot(a, b, preferred_element_type=f32)


def nt(a, b):
    return lax.dot_general(a, b, (((1,), (1,)), ((), ())), preferred_element_type=f32)


def flip(a):
    return a.astype(f32).T.astype(a.dtype)


def round_up(a, b):
    return (a + b - 1) // b * b


def gelu(z):
    scale = 0.7978845608028654
    return z * (0.5 + 0.5 * jnp.tanh(z * (scale + (0.044715 * scale) * (z * z))))


def gelu_slope(z):
    scale = 0.7978845608028654
    square = z * z
    half = 0.5 + 0.5 * jnp.tanh(z * (scale + (0.044715 * scale) * square))
    return half + (half - half * half) * (z * (2.0 * scale + (6.0 * 0.044715 * scale) * square))


def norm_root(act, axis):
    return lax.rsqrt(jnp.sum(act * act, axis=axis, keepdims=True) + norm_eps)


def pull_back(act, slope, root, grad, axis):
    dot = jnp.sum(act * grad, axis=axis, keepdims=True)
    return (slope * (root * grad - act * (root * root * root * dot))).astype(bf16)


def as_column(row):
    return jnp.broadcast_to(row, (8, row.shape[1])).T[:, 0:1]


def widen(row, width, value=0):
    return jnp.concatenate([row, jnp.full((1, width - row.shape[1]), value, row.dtype)], axis=1)


def graph_kernel(
    peers, cap, seeds, fan,
    nbr_hbm, msk_hbm, xt_hbm, w1_hbm, wr_hbm, srow_hbm, scnt_hbm, lab_hbm, smask_hbm, wht_hbm, bias_hbm,
    g_out, s_out,
    nbr, msk, xt, srow, scnt, lab, smask, wht, bias, joined, near, chosen, far2, far2t, grad1, ctmp, crow, lrow, lcode, crow2, lrow2, rdeg,
    w1, wr, w1t, act1, slope1, root1, h1t, ob0, ib0, ob1, ib1, ob2, ib2, ob3, ib3, ob4, ib4, ob5, ib5,
    gl, acc, rc, sbq, rbq, sbz, rbz, gout, ssend, srecv, sqv, szv,
    load_sem, send_sem, recv_sem, red_send, red_recv,
):
    fin, nodes = xt.shape
    hidden = w1.shape[1]
    finp = round_up(fin, 16)
    slots = peers * cap
    table = nodes + slots
    groups = table // 128
    chunks = nodes // 128
    blocks = nodes // 256
    span = far2.shape[0]
    local = span - slots
    me = lax.axis_index("dom")
    rep = lax.axis_index("rep")
    core = lax.rem(rep, 2)
    xpos = rep // 2
    ypos = lax.rem(me, 2)
    zpos = me // 2
    nz = peers // 2
    mate_c = xpos * 2 + (1 - core)
    mate_x = (1 - xpos) * 2 + core
    mate_y = zpos * 2 + (1 - ypos)

    loads = [
        pltpu.make_async_copy(src, dst, load_sem.at[k])
        for k, (src, dst) in enumerate(
            (
                (srow_hbm, srow), (scnt_hbm, scnt), (xt_hbm, xt), (nbr_hbm, nbr), (msk_hbm, msk),
                (w1_hbm, w1), (wr_hbm, wr), (lab_hbm, lab), (smask_hbm, smask), (wht_hbm, wht), (bias_hbm, bias),
            )
        )
    ]
    for load in loads:
        load.start()
    barrier = pltpu.get_barrier_semaphore()
    for off in range(1, peers):
        pl.semaphore_signal(barrier, inc=1, device_id={"dom": lax.rem(me + off, peers)}, device_id_type=MESH)
    for mate in (mate_c, mate_x):
        pl.semaphore_signal(barrier, inc=1, device_id={"rep": mate}, device_id_type=MESH)
    mate_xy = {"dom": mate_y, "rep": mate_x}
    pl.semaphore_signal(barrier, inc=1, device_id=mate_xy, device_id_type=MESH)

    def exchange(stage, src, dst, same=False):
        size = dst.shape[0] // peers
        copies = []
        for off in range(1, peers):
            peer = lax.rem(me + off, peers)
            copies.append(
                pltpu.make_async_remote_copy(
                    src_ref=src if same else src.at[pl.ds(pl.multiple_of(peer * size, 16), size)],
                    dst_ref=dst.at[pl.ds(pl.multiple_of(me * size, 16), size)],
                    send_sem=send_sem.at[stage, off - 1],
                    recv_sem=recv_sem.at[stage, off - 1],
                    device_id={"dom": peer},
                    device_id_type=MESH,
                )
            )
        for c in copies:
            c.start()
        return copies

    started = []

    def finish(copies):
        for c in copies:
            c.wait_recv()
        started.extend(copies)

    loads[0].wait()
    loads[1].wait()
    count = jnp.broadcast_to(scnt[...], (peers, peers))
    count = jnp.where(
        lax.broadcasted_iota(i32, (peers, peers), 0) == lax.broadcasted_iota(i32, (peers, peers), 1), count, 0
    )
    count = jnp.sum(count.astype(f32), axis=1, keepdims=True)
    in_use = lax.broadcasted_iota(i32, (peers, cap), 1).astype(f32) < count
    slot = jnp.where(in_use, srow[...].astype(f32), -1.0)
    per = 128 // cap
    slot = jnp.concatenate([slot] * per, axis=1)
    owner = lax.broadcasted_iota(i32, (peers, 128), 0)
    place = lax.broadcasted_iota(i32, (peers, 128), 1) // cap
    send_row = jnp.concatenate(
        [
            jnp.sum(jnp.where(owner == place + t * per, slot, 0.0), axis=0, keepdims=True)
            for t in range(slots // 128)
        ],
        axis=1,
    )
    node_id = lax.broadcasted_iota(i32, (256, nodes), 1).astype(f32)
    send_col = as_column(send_row)
    for r in range(0, slots, 256):
        chosen[r : r + 256, :] = jnp.where(send_col[r : r + 256] == node_id, 1.0, 0.0).astype(bf16)
    line = lax.broadcasted_iota(i32, (16, nodes), 0)
    joined[finp - 16 : finp, :] = jnp.where(line == 16 - (finp - fin), 1.0, 0.0).astype(bf16)
    r_id = lax.broadcasted_iota(i32, (2 * seeds, local), 0)
    l_id = lax.broadcasted_iota(i32, (2 * seeds, local), 1)
    is_self = (r_id < seeds) & (l_id == r_id + FAN_REST * seeds)
    is_nbr = (r_id >= seeds) & (l_id < FAN_REST * seeds) & (lax.rem(l_id, seeds) == r_id - seeds)
    spread = jnp.where(is_self | is_nbr, 1.0, 0.0)
    spread_t = spread.T.astype(bf16)
    spread = spread.astype(bf16)
    loads[2].wait()
    joined[0:fin, :] = xt[...]
    ob0[:, finp:] = jnp.zeros((slots, ob0.shape[1] - finp), bf16)
    ob0[:, 0:finp] = nt(chosen[0:slots, :], joined[0:finp, :]).astype(bf16)
    for buf in (ib0, ib1, ib2, ib3, ib4, ib5):
        size = buf.shape[0] // peers
        buf[pl.ds(pl.multiple_of(me * size, 16), size), :] = jnp.zeros((size, buf.shape[1]), bf16)
    pl.semaphore_wait(barrier, peers - 1 + 3)
    sent = exchange(0, ob0, ib0)

    loads[3].wait()
    loads[4].wait()

    def codes(level, size, here):
        at = slice(0, size)
        return jnp.where(msk[level, at, 0, here] == 1, nbr[level, at, 0, here], MASKED).astype(f32)

    code3 = codes(2, FAN_REST, slice(0, 128))
    code3t = jnp.concatenate([code3, jnp.full((16 - FAN_REST, 128), float(MASKED), f32)], axis=0).T[0:seeds]
    degree = jnp.sum(jnp.where(code3t < float(MASKED), 1.0, 0.0), axis=1, keepdims=True)
    rdeg3 = 1.0 / jnp.maximum(degree, 1.0)
    tiled = jnp.concatenate([code3t] * peers, axis=0)
    r_id = lax.broadcasted_iota(i32, (peers * seeds, 128), 0)
    l_id = lax.broadcasted_iota(i32, (peers * seeds, 128), 1)
    wanted = jnp.where(l_id < cap, nodes + (r_id // seeds) * cap + l_id, -1).astype(f32)
    far3 = jnp.zeros(wanted.shape, f32)
    for k in range(FAN_REST):
        far3 = far3 + jnp.where(wanted == tiled[:, k : k + 1], 1.0, 0.0)
    ob5[...] = far3.astype(bf16)
    sent_far = exchange(5, ob5, ib5)

    fill = jnp.full((32 - fan, 128), float(MASKED), f32)
    fill2 = jnp.full((16 - FAN_REST, 128), float(MASKED), f32)
    for c in range(chunks):
        here = slice(c * 128, (c + 1) * 128)
        code = codes(0, fan, here)
        degree = jnp.sum((code < MASKED).astype(f32), axis=0, keepdims=True)
        rdeg[0:1, here] = 1.0 / jnp.maximum(degree, 1.0)
        code2 = jnp.concatenate([codes(1, FAN_REST, here), fill2], axis=0).astype(i32)
        ctmp[here, 0:64] = jnp.concatenate(
            [code, fill, (code2 >> 7).astype(f32), (code2 & 127).astype(f32)], axis=0
        ).T

    def grouped(source, count, width):
        each = 256 // width
        lane = lax.broadcasted_iota(i32, (count, 256), 1) // width
        code = jnp.zeros((count, 256), f32)
        for n in range(each):
            piece = source[pl.ds(n, count, stride=each), :]
            piece = jnp.concatenate([piece, piece], axis=1)
            piece = pltpu.roll(piece, n * width, 1) if n else piece
            code = jnp.where(lane == n, piece, code)
        code = code.astype(i32)
        return ((code >> 7) * each + lane).astype(f32), (code & 127).astype(f32)

    crow[...], lrow[...] = grouped(ctmp, nodes // 8, 32)

    lane = lax.broadcasted_iota(i32, (1, 128), 1)
    fits = 128 // seeds
    tiles = []
    for t in range(local // 128):
        tile = jnp.full((1, 128), -1.0, f32)
        for j in range(fits):
            k = t * fits + j
            here = lane // seeds == j
            if k < FAN_REST:
                piece = code3[k : k + 1, :]
                piece = pltpu.roll(piece, j * seeds, 1) if j else piece
                tile = jnp.where(here & (piece < nodes), piece, tile)
            elif k == FAN_REST:
                tile = jnp.where(here, (lane - j * seeds).astype(f32), tile)
        tiles.append(tile)
    local_col = as_column(jnp.concatenate(tiles, axis=1))
    for r in range(0, local, 256):
        chosen[slots + r : slots + r + 256, :] = jnp.where(
            local_col[r : r + 256] == node_id, 1.0, 0.0
        ).astype(bf16)
    keep = jnp.where(jnp.concatenate([send_col, local_col], axis=0) >= 0.0, 1.0, 0.0)
    found = nn(chosen[0:span, :], ctmp[...].astype(bf16))
    lcode[...] = pltpu.roll(found, 96, 1) * 128.0 + pltpu.roll(found, 80, 1)
    lane = lax.broadcasted_iota(i32, (span, 128), 1)
    degree = jnp.sum(
        jnp.where((lcode[...] < float(MASKED)) & (lane < FAN_REST), 1.0, 0.0), axis=1, keepdims=True
    )
    rdeg2 = 1.0 / jnp.maximum(degree, 1.0)
    crow2[...], lrow2[...] = grouped(lcode, span // 16, 16)

    rows_a = lax.broadcasted_iota(i32, (groups * 8, 256), 0).astype(f32)
    rows_b = lax.broadcasted_iota(i32, (128, 256), 0).astype(f32)
    rows_c = lax.broadcasted_iota(i32, (groups * 16, 256), 0).astype(f32)

    def list_counts(b, _):
        for p in range(16):
            g = b * 16 + p
            left = jnp.where(rows_c == crow2[pl.ds(g, 1), :], 1.0, 0.0).astype(bf16)
            right = jnp.where(rows_b == lrow2[pl.ds(g, 1), :], 1.0, 0.0).astype(bf16)
            value = nt(left, right).astype(bf16)
            for a in range(groups):
                tile = value[a * 16 : (a + 1) * 16]
                if a < chunks:
                    chosen[pl.ds(pl.multiple_of(span + g * 16, 16), 16), a * 128 : (a + 1) * 128] = tile
                else:
                    at = pl.ds(pl.multiple_of(g * 16, 16), 16)
                    far2[at, (a - chunks) * 128 : (a - chunks + 1) * 128] = tile
        return 0

    lax.fori_loop(0, span // 256, list_counts, 0)

    def build(b, _):
        for p in range(16):
            pair = []
            for half in range(2):
                g = b * 32 + p * 2 + half
                left = jnp.where(rows_a == crow[pl.ds(g, 1), :], 1.0, 0.0).astype(bf16)
                right = jnp.where(rows_b == lrow[pl.ds(g, 1), :], 1.0, 0.0).astype(bf16)
                pair.append(nt(left, right))
            at = pl.ds(pl.multiple_of(b * 256 + p * 16, 16), 16)
            for a in range(groups):
                tile = jnp.concatenate([pair[0][a * 8 : (a + 1) * 8], pair[1][a * 8 : (a + 1) * 8]], axis=0)
                near[at, a * 128 : (a + 1) * 128] = tile.astype(bf16)
        return 0

    lax.fori_loop(0, blocks, build, 0)

    for load in loads[5:]:
        load.wait()
    bias = bias[...].reshape(1, bias.shape[0])
    wpad = jnp.concatenate(
        [w1[0:fin, :], jnp.zeros((finp - fin, hidden), f32), w1[fin : 2 * fin, :], jnp.zeros((finp - fin, hidden), f32)],
        axis=0,
    )
    w1t[...] = wpad.T.astype(bf16)
    b1 = as_column(bias[0:1, 0:hidden])

    finish(sent)
    ibt = flip(ib0[...])[0:finp, :]

    def block(b):
        return pl.ds(b * 256 if isinstance(b, int) else pl.multiple_of(b * 256, 256), 256)

    def gather(b):
        blk = block(b)
        total = nt(joined[0:finp, :], near[blk, 0:nodes]) + nt(ibt, near[blk, nodes:])
        joined[finp:, blk] = (total * rdeg[0:1, blk]).astype(bf16)

    def product(b):
        blk = block(b)
        grad1[:, blk] = nn(w1t[...], joined[:, blk]) + b1

    def activate(b):
        blk = block(b)
        z = grad1[:, blk]
        act = gelu(z)
        root = norm_root(act, 0)
        act1[:, blk] = act
        root1[0:1, blk] = root
        h1t[:, blk] = (act * root).astype(bf16)

    gather(0)
    far2t[...] = flip(far2[...])
    w2 = wr[0].astype(bf16)
    w3 = wr[1].astype(bf16)
    product(0)
    gather(1)

    def layer_one(b, _):
        activate(b - 2)
        product(b - 1)
        gather(b)
        return 0

    lax.fori_loop(2, blocks, layer_one, 0)
    activate(blocks - 2)
    product(blocks - 1)
    activate(blocks - 1)
    sent_rows = nt(chosen[0:slots, :], h1t[...]).astype(bf16)
    ob1[...] = sent_rows
    sent = exchange(1, ob1, ib1)

    own2 = nt(chosen[slots:, :], h1t[...])

    def slopes(b, _):
        blk = block(b)
        slope1[:, blk] = gelu_slope(grad1[:, blk])
        return 0

    lax.fori_loop(0, blocks, slopes, 0)
    finish(sent_far)
    far3r = ib5[...].astype(f32)[:, 0:cap]
    spots = peers * cap
    r_id = lax.broadcasted_iota(i32, (peers * seeds, spots), 0) // seeds
    l_id = lax.broadcasted_iota(i32, (peers * seeds, spots), 1) // cap
    collect = jnp.where(r_id == l_id, jnp.concatenate([far3r] * peers, axis=1), 0.0)
    scatter = collect.T.astype(bf16)
    collect = collect.astype(bf16)

    finish(sent)

    def rows_two(own_self, own_sum, at):
        agg = (own_sum + nn(far2[at, :], ib1[...])) * rdeg2[at]
        both = jnp.concatenate([own_self, agg.astype(bf16)], axis=1)
        z = nn(both, w2) + bias[0:1, hidden : 2 * hidden]
        act = gelu(z)
        root = norm_root(act, 1)
        return both, z, act, root, (act * (root * keep[at])).astype(bf16)

    out_at, in_at = slice(0, slots), slice(slots, span)
    joined2a, z2a, act2a, root2a, h2a = rows_two(sent_rows, own2[local:span], out_at)
    ob2[...] = nn(collect, h2a).astype(bf16)
    sent = exchange(2, ob2, ib2)

    joined2b, z2b, act2b, root2b, h2b = rows_two(own2[0:local].astype(bf16), own2[span:], in_at)
    near3 = nn(spread, h2b)
    slope2b = gelu_slope(z2b)
    classes = wht.shape[0]
    classp = round_up(classes, 16)
    wht_low = jnp.concatenate([wht[...], jnp.zeros((classp - classes, hidden), f32)], axis=0).astype(bf16)
    bh = widen(bias[0:1, 3 * hidden : 3 * hidden + classes], classp)
    class_id = lax.broadcasted_iota(i32, (seeds, classp), 1)
    label = as_column(widen(lab[...].astype(f32), 128))[0:seeds]
    hot = jnp.where(class_id.astype(f32) == label, 1.0, 0.0)
    weight = as_column(widen(smask[...].astype(f32), 128))[0:seeds]
    finish(sent)
    total = near3[seeds:]
    for q in range(peers):
        total = total + ib2[q * seeds : (q + 1) * seeds, :].astype(f32)
    joined3 = jnp.concatenate([near3[0:seeds].astype(bf16), (total * rdeg3).astype(bf16)], axis=1)
    z3 = nn(joined3, w3) + bias[0:1, 2 * hidden : 3 * hidden]
    act3 = gelu(z3)
    slope3 = gelu_slope(z3)
    root3 = norm_root(act3, 1)
    top = (act3 * root3).astype(bf16)

    logits = nt(top, wht_low) + bh
    logits = jnp.where(class_id < classes, logits, -1e30)
    peak = jnp.max(logits, axis=1, keepdims=True)
    lse = peak + jnp.log(jnp.sum(jnp.exp(logits - peak), axis=1, keepdims=True))
    dlog = ((jnp.exp(logits - lse) - hot) * weight).astype(bf16)
    dtop = nn(dlog, wht_low)

    dz3 = pull_back(act3, slope3, root3, dtop, 1)
    dj3 = nt(dz3, w3)
    dg3 = (dj3[:, hidden:] * rdeg3).astype(bf16)
    ob3[...] = dg3
    sent = exchange(3, ob3, ib3, same=True)
    dloc = nn(spread_t, jnp.concatenate([dj3[:, 0:hidden].astype(bf16), dg3], axis=0))

    seg_a = 4 * hidden
    row_head = seg_a + 2 * finp
    row_bias = row_head + classp
    rows = gl.shape[1]

    def put(row, value):
        size = value.shape[0]
        gl[0, row : row + size, :] = value[:, 0:128].astype(bf16)
        gl[1, row : row + size, :] = value[:, 128:].astype(bf16)

    picked = jnp.sum(logits * hot, axis=1, keepdims=True)
    loss = jnp.sum((lse - picked) * weight, axis=0, keepdims=True)
    total = jnp.sum(weight, axis=0, keepdims=True)
    sc_lane = lax.broadcasted_iota(i32, (8, 128), 1)
    ssend[0] = jnp.where(sc_lane == 0, loss, jnp.where(sc_lane == 1, total, 0.0))
    dz2b = pull_back(act2b, slope2b, root2b, dloc * keep[in_at], 1)
    dj2b = nt(dz2b, w2)
    dg2b = (dj2b[:, hidden:] * rdeg2[in_at]).astype(bf16)
    near_ret = nn(far2t[:, in_at], dg2b)
    slope2a = gelu_slope(z2a)
    put(row_head, nn(dlog.astype(f32).T.astype(bf16), top))
    put(2 * hidden, nn(joined3.astype(f32).T.astype(bf16), dz3))
    bias_3 = jnp.sum(dz3.astype(f32), axis=0, keepdims=True)
    bias_h = widen(jnp.sum(dlog.astype(f32), axis=0, keepdims=True), hidden)
    finish(sent)

    dh2a = nn(scatter, ib3[...]) * keep[out_at]
    dz2a = pull_back(act2a, slope2a, root2a, dh2a, 1)
    dj2a = nt(dz2a, w2)
    dg2a = (dj2a[:, hidden:] * rdeg2[out_at]).astype(bf16)
    ob4[...] = (near_ret + nn(far2t[:, out_at], dg2a)).astype(bf16)
    sent = exchange(4, ob4, ib4)
    put(0, nn(flip(joined2a), dz2a) + nn(flip(joined2b), dz2b))

    used = []

    def hop(src, dst, who):
        used.append(0)
        k = len(used) - 1
        copy = pltpu.make_async_remote_copy(
            src_ref=src, dst_ref=dst, send_sem=red_send.at[k], recv_sem=red_recv.at[k],
            device_id=who, device_id_type=MESH,
        )
        copy.start()
        return copy

    def rows_of(start, size):
        return pl.ds(pl.multiple_of(start, 16), size)

    to_core = {"rep": mate_c}
    plane = (
        xpos * 2 + ypos,
        (
            ((1 - xpos) * 2 + ypos, {"rep": mate_x}),
            (xpos * 2 + 1 - ypos, {"dom": mate_y}),
            ((1 - xpos) * 2 + 1 - ypos, mate_xy),
        ),
    )
    others = [lax.rem(zpos + off, nz) for off in range(1, nz)]
    column = (zpos, tuple((to, {"dom": to * 2 + ypos}) for to in others))

    def summing(start, size, out_sem, one, two):
        (mine1, group1), (mine2, group2) = one, two
        quarter = size // (len(group1) + 1)
        piece = quarter // (len(group2) + 1)
        whole = slice(start, start + size)
        at1, at2 = start // 4, start // (4 * nz)
        at1, at2 = slice(at1, at1 + quarter), slice(at2, at2 + piece)
        kept = rows_of(start + mine1 * quarter, quarter)
        here = rows_of(start + mine1 * quarter + mine2 * piece, piece)
        copies = [hop(gl.at[1 - core, whole], rc.at[whole], to_core)]
        yield
        finish(copies)
        value = gl[core, whole, :].astype(f32) + rc[whole, :].astype(f32)
        acc[whole, :] = value
        sbq[whole, :] = value.astype(bf16)
        copies = [
            hop(sbq.at[rows_of(start + to * quarter, quarter)], rbq.at[k, at1], who)
            for k, (to, who) in enumerate(group1)
        ]
        yield
        finish(copies)
        value = acc[kept, :]
        for k in range(len(group1)):
            value = value + rbq[k, at1, :].astype(f32)
        acc[kept, :] = value
        sbz[at1, :] = value.astype(bf16)
        copies = [
            hop(sbz.at[rows_of(start // 4 + to * piece, piece)], rbz.at[k, at2], who)
            for k, (to, who) in enumerate(group2)
        ]
        yield
        finish(copies)
        value = acc[here, :]
        for k in range(len(group2)):
            value = value + rbz[k, at2, :].astype(f32)
        gout[core, here, :] = value.astype(bf16)
        part = gout.at[core, here]
        copies = [hop(part, part, who) for _, who in group2]
        yield
        finish(copies)
        part = gout.at[core, kept]
        copies = [hop(part, part, who) for _, who in group1]
        copies.append(hop(part, part, to_core))
        yield
        finish(copies)
        copies = []
        for to, _ in group1:
            part = gout.at[core, rows_of(start + to * quarter, quarter)]
            copies.append(hop(part, part, to_core))
        out = [
            pltpu.make_async_copy(gout.at[h, whole], g_out.at[h, whole], load_sem.at[out_sem + k])
            for k, h in enumerate((core, 1 - core))
        ]
        out[0].start()
        yield
        finish(copies)
        out[1].start()
        yield
        for c in out:
            c.wait()

    def summing_scalars():
        copies = [hop(ssend.at[0], srecv.at[0], to_core)]
        yield
        finish(copies)
        ssend[1] = ssend[0] + srecv[0]
        mine = plane[0]
        sqv[mine] = ssend[1]
        copies = [hop(ssend.at[1], sqv.at[mine], who) for _, who in plane[1]]
        yield
        finish(copies)
        ssend[2] = sqv[0] + sqv[1] + sqv[2] + sqv[3]
        szv[zpos] = ssend[2]
        copies = [hop(ssend.at[2], szv.at[zpos], who) for _, who in column[1]]
        yield
        finish(copies)
        total = szv[0]
        for k in range(1, nz):
            total = total + szv[k]
        s_out[...] = total

    def go_on(*runs):
        for run in runs:
            next(run, None)

    cut = seg_a + 2 * (4 * nz * 16)
    rest = summing(0, seg_a, 4, plane, column)
    first = summing(seg_a, cut - seg_a, 0, column, plane)
    second = summing(cut, rows - cut, 2, plane, column)
    scalars = summing_scalars()
    go_on(rest, scalars)

    bias_2 = jnp.sum(dz2a.astype(f32), axis=0, keepdims=True) + jnp.sum(dz2b.astype(f32), axis=0, keepdims=True)
    line = lax.broadcasted_iota(i32, (16, hidden), 0)
    put(
        row_bias,
        jnp.where(line == 1, bias_2, 0.0) + jnp.where(line == 2, bias_3, 0.0) + jnp.where(line == 3, bias_h, 0.0),
    )
    both = flip(
        jnp.concatenate(
            [dj2a[:, 0:hidden].astype(bf16), dj2b[:, 0:hidden].astype(bf16), dg2a, dg2b], axis=0
        )
    )
    grad1[...] = nn(both, chosen[...])
    go_on(rest, scalars)
    finish(sent)
    back = flip(ib4[...])

    def layer_one_back(b, _):
        blk = block(b)
        grad = grad1[:, blk] + nn(back, chosen[0:slots, blk])
        h1t[:, blk] = pull_back(act1[:, blk], slope1[:, blk], root1[0:1, blk], grad, 0)
        return 0

    lax.fori_loop(0, blocks, layer_one_back, 0, unroll=2)
    size = cut - seg_a
    put(seg_a, nt(joined[0:size, :], h1t[...]))
    go_on(first, rest, scalars)
    put(cut, nt(joined[size:, :], h1t[...]))
    go_on(second, first)
    for _ in range(5):
        go_on(second, rest, first, scalars)
    go_on(second, first)
    go_on(second)
    for c in started:
        c.wait_send()


def in_hbm(*arrays):
    return [pltpu.with_memory_space_constraint(a, pltpu.HBM) for a in arrays]


def summed_gradients(peers, cap, seeds, fan, nbr, msk, xt, w1, wr, srow, scnt, lab, smask, wht, bias):
    fin, nodes = xt.shape
    hidden = w1.shape[1]
    finp = round_up(fin, 16)
    wide = round_up(fin, 128)
    slots = peers * cap
    span = slots + round_up(seeds * (FAN_REST + 1), 256)
    classp = round_up(wht.shape[0], 16)
    rows = 4 * hidden + 2 * finp + classp + 16
    nz = peers // 2
    vmem = pltpu.VMEM
    sems = 64
    some = peers * seeds
    scratch = [
        vmem(nbr.shape, i32),
        vmem(msk.shape, i32),
        vmem(xt.shape, bf16),
        vmem(srow.shape, i32),
        vmem(scnt.shape, i32),
        vmem(lab.shape, i32),
        vmem(smask.shape, i32),
        vmem(wht.shape, f32),
        vmem(bias.shape, f32),
        vmem((2 * finp, nodes), bf16),
        vmem((nodes, nodes + slots), bf16),
        vmem((2 * span, nodes), bf16),
        vmem((span, slots), bf16),
        vmem((slots, span), bf16),
        vmem((hidden, nodes), f32),
        vmem((nodes, 128), f32),
        vmem((nodes // 8, 256), f32),
        vmem((nodes // 8, 256), f32),
        vmem((span, 128), f32),
        vmem((span // 16, 256), f32),
        vmem((span // 16, 256), f32),
        vmem((8, nodes), f32),
        vmem(w1.shape, f32),
        vmem(wr.shape, f32),
        vmem((hidden, 2 * finp), bf16),
        vmem((hidden, nodes), f32),
        vmem((hidden, nodes), f32),
        vmem((8, nodes), f32),
        vmem((hidden, nodes), bf16),
        vmem((slots, wide), bf16),
        vmem((slots, wide), bf16),
        vmem((slots, hidden), bf16),
        vmem((slots, hidden), bf16),
        vmem((some, hidden), bf16),
        vmem((some, hidden), bf16),
        vmem((seeds, hidden), bf16),
        vmem((some, hidden), bf16),
        vmem((slots, hidden), bf16),
        vmem((slots, hidden), bf16),
        vmem((some, 128), bf16),
        vmem((some, 128), bf16),
        vmem((2, rows, 128), bf16),
        vmem((rows, 128), f32),
        vmem((rows, 128), bf16),
        vmem((rows, 128), bf16),
        vmem((3, rows // 4, 128), bf16),
        vmem((rows // 4, 128), bf16),
        vmem((nz - 1, rows // (4 * nz), 128), bf16),
        vmem((2, rows, 128), bf16),
        vmem((4, 8, 128), f32),
        vmem((3, 8, 128), f32),
        vmem((4, 8, 128), f32),
        vmem((nz, 8, 128), f32),
        pltpu.SemaphoreType.DMA((11,)),
        pltpu.SemaphoreType.DMA((6, peers - 1)),
        pltpu.SemaphoreType.DMA((6, peers - 1)),
        pltpu.SemaphoreType.DMA((sems,)),
        pltpu.SemaphoreType.DMA((sems,)),
    ]
    inside = pl.BlockSpec(memory_space=vmem)
    outside = pl.BlockSpec(memory_space=pl.ANY)
    return pl.pallas_call(
        functools.partial(graph_kernel, peers, cap, seeds, fan),
        out_shape=(
            jax.ShapeDtypeStruct((2, rows, 128), bf16),
            jax.ShapeDtypeStruct((8, 128), f32),
        ),
        in_specs=[outside] * 11,
        out_specs=(outside, inside),
        scratch_shapes=scratch,
        compiler_params=pltpu.CompilerParams(
            collective_id=0, has_side_effects=True, vmem_limit_bytes=47 * 2**20
        ),
        cost_estimate=pl.CostEstimate(flops=24 * 10**9, bytes_accessed=12 * 2**20, transcendentals=2**20),
        name="graph_step",
    )(*in_hbm(nbr, msk, xt, w1, wr, srow, scnt, lab, smask, wht, bias))


def split_dot(a, b):
    high = a.astype(bf16)
    low = (a - high.astype(f32)).astype(bf16)
    return nn(high, b) + nn(low, b)


def three_dot(a, b):
    high = b.astype(bf16)
    low = (b - high.astype(f32)).astype(bf16)
    return split_dot(a, high) + nn(a.astype(bf16), low)


def update_kernel(
    fin,
    g_all, scalars, wht, bias, sth, rth, bm, bv,
    w1, wr, st1, rt1, stm, rtm, sts, rts,
    loss_o, total_o, norm_o, gh_o, m_o, v_o, lh_o, nh_o, nb_o, nh_low,
    g1_hbm, gr_hbm, l1_hbm, lm_hbm, ls_hbm, n1_hbm, nr_hbm, n1_low_hbm, nr_low_hbm,
    g1_o, gr_o, l1_o, lm_o, ls_o, n1_o, nr_o, n1_low, nr_low,
    g1, g_mine, w_mine, full, gb, out_sem,
):
    hidden = w1.shape[1]
    classes = wht.shape[0]
    classp = round_up(classes, 16)
    finp = round_up(fin, 16)
    seg_a = 4 * hidden
    part = lax.axis_index("rep")

    stores = []

    def store(src, dst):
        copy = pltpu.make_async_copy(src, dst, out_sem.at[len(stores)])
        stores.append(copy)
        copy.start()

    def grads(start, size):
        return jnp.concatenate(
            [g_all[0, start : start + size, :], g_all[1, start : start + size, :]], axis=1
        )

    total = scalars[0:1, 1:2]
    square = jnp.zeros((16, hidden), f32)
    spare = lax.broadcasted_iota(i32, (16, hidden), 0) >= 16 - (finp - fin)
    for r in range(0, g_all.shape[1], 16):
        g = grads(r, 16).astype(f32)
        if r == seg_a + 2 * finp - 16:
            g = jnp.where(spare, 0.0, g)
        square = square + g * g
    square = jnp.sum(jnp.sum(square, axis=0, keepdims=True), axis=1, keepdims=True)
    norm = jnp.sqrt(square) / total
    scale = clip_limit / jnp.maximum(norm, clip_limit) / total
    loss_o[...] = scalars[0:1, 0:1]
    total_o[...] = total
    norm_o[...] = norm
    lift = (1.0 - decay) * scale * scale
    move = shampoo_rate * scale

    g1[0:fin, :] = grads(seg_a, finp)[0:fin].astype(f32)
    g1[fin : 2 * fin, :] = grads(seg_a + finp, finp)[0:fin].astype(f32)
    count = st1.shape[0]
    g_low = g1[...].astype(bf16)
    full[0] = nn(g1[...].T.astype(bf16), g_low)
    half = split_dot(rt1[...], g_low)
    for i in range(2 * fin // count):

        @pl.when(part == i)
        def _():
            g_mine[...] = g1[i * count : (i + 1) * count, :]
            w_mine[...] = w1[i * count : (i + 1) * count, :]

    g_rows = g_mine[...]
    g1_o[...] = g_rows * scale
    store(g1_o, g1_hbm)
    fresh = w_mine[...] - move * three_dot(half, rts[0])
    n1_o[...] = fresh
    n1_low[...] = fresh.astype(bf16)
    store(n1_o, n1_hbm)
    store(n1_low, n1_low_hbm)
    product = nt(g_rows.astype(bf16), g_low)
    l1_o[...] = decay * st1[...] + lift * product
    store(l1_o, l1_hbm)

    count = stm.shape[1]
    at = pl.ds(pl.multiple_of(part * count, count), count)
    products = []
    for i in range(2):
        g = grads(i * 2 * hidden, 2 * hidden)
        base = pl.ds(pl.multiple_of(i * 2 * hidden + part * count, 16), count)
        g_rows = jnp.concatenate([g_all[0, base, :], g_all[1, base, :]], axis=1)
        gr_o[i] = g_rows.astype(f32) * scale
        full[1 + i] = nn(flip(g), g)
        products.append((nt(g_rows, g), three_dot(split_dot(rtm[i], g), rts[1 + i])))
    store(gr_o, gr_hbm)
    for i, (product, step) in enumerate(products):
        lm_o[i] = decay * stm[i] + lift * product
        fresh = wr[i, at, :] - move * step
        nr_o[i] = fresh
        nr_low[i] = fresh.astype(bf16)
    store(lm_o, lm_hbm)
    store(nr_o, nr_hbm)
    store(nr_low, nr_low_hbm)

    gt = grads(seg_a + 2 * finp, classp)
    full[3] = nn(flip(gt), gt)
    count = sts.shape[1]
    mine = pl.ds(pl.multiple_of(part * count, count), count)
    for i in range(4):
        ls_o[i] = decay * sts[i] + lift * full[i, mine, :]
    store(ls_o, ls_hbm)
    lh_o[...] = decay * sth[...] + lift * nt(gt, gt)[0:classes, 0:classes]
    root = rts[3, mine, :]
    high = root.astype(bf16)
    low = (root - high.astype(f32)).astype(bf16)
    left = (nt(gt, high) + nt(gt, low))[0:classes]
    step = three_dot(rth[...], left)
    gt_mine = jnp.zeros((classes, count), f32)
    wt_mine = jnp.zeros((classes, count), f32)
    gt_wide = gt.astype(f32)
    for i in range(hidden // count):
        here = slice(i * count, (i + 1) * count)
        gt_mine = jnp.where(part == i, gt_wide[0:classes, here], gt_mine)
        wt_mine = jnp.where(part == i, wht[:, here], wt_mine)
    gh_o[...] = gt_mine * scale
    fresh = wt_mine - move * step
    nh_o[...] = fresh
    nh_low[...] = fresh.astype(bf16)

    lines = grads(seg_a + 2 * finp + classp, 16).astype(f32)
    gb[0:1, 0:hidden] = grads(seg_a + finp - 16, 16).astype(f32)[fin - finp + 16 : fin - finp + 17, :]
    for i in range(1, 4):
        gb[0:1, i * hidden : (i + 1) * hidden] = lines[i : i + 1, :]
    size = bias.shape[0]
    g = gb[0:1, 0:size] * scale
    bias = bias[...].reshape(1, size)
    new_m = beta_one * bm[...].reshape(1, size) + (1.0 - beta_one) * g
    new_v = beta_two * bv[...].reshape(1, size) + (1.0 - beta_two) * g * g
    m_hat = new_m / (1.0 - beta_one**STEP)
    v_hat = new_v / (1.0 - beta_two**STEP)
    m_o[...] = new_m.reshape(size)
    v_o[...] = new_v.reshape(size)
    fresh = bias - bias_rate * (m_hat / (jnp.sqrt(v_hat) + adam_eps) + weight_decay * bias)
    nb_o[...] = fresh.reshape(size)
    for copy in stores:
        copy.wait()


def updates(fin, g_all, scalars, w1, wr, wht, bias, st1, rt1, stm, rtm, sts, rts, sth, rth, bm, bv):
    hidden = w1.shape[1]
    classes = wht.shape[0]
    count = sts.shape[1]
    n1 = (st1.shape[0], hidden)
    nr = (2, stm.shape[1], hidden)
    nh = (classes, count)

    def of(shape, kind=f32):
        return jax.ShapeDtypeStruct(shape, kind)

    def room(a):
        return pltpu.VMEM(a.shape, a.dtype)

    one = of((1, 1))
    line = of(bias.shape)
    small = [one, one, one, of(nh), line, line, of(sth.shape), of(nh), line, of(nh, bf16)]
    large = [of(n1), of(nr), of(st1.shape), of(stm.shape), of(sts.shape), of(n1), of(nr), of(n1, bf16), of(nr, bf16)]
    loaded = [w1, wr, st1, rt1, stm, rtm, sts, rts]
    inside = pl.BlockSpec(memory_space=pltpu.VMEM)
    outside = pl.BlockSpec(memory_space=pl.ANY)
    (loss, total, norm, gh, m, v, lh, nh_new, nb, nh_low, g1, gr, l1, lm, ls, n1_new, nr_new, n1_low, nr_low) = pl.pallas_call(
        functools.partial(update_kernel, fin),
        out_shape=tuple(small + large),
        in_specs=[inside] * (8 + len(loaded)),
        out_specs=(inside,) * len(small) + (outside,) * len(large),
        scratch_shapes=[room(a) for a in large] + [
            pltpu.VMEM((2 * fin, hidden), f32),
            pltpu.VMEM(n1, f32),
            pltpu.VMEM(n1, f32),
            pltpu.VMEM((4, hidden, hidden), f32),
            pltpu.VMEM((1, 4 * hidden), f32),
            pltpu.SemaphoreType.DMA((len(large),)),
        ],
        compiler_params=pltpu.CompilerParams(vmem_limit_bytes=40 * 2**20),
        name="update_step",
    )(g_all, scalars, wht, bias, sth, rth, bm, bv, *loaded)
    return [
        loss, total, norm, g1, gr, gh, m, v, l1, lm, ls, lh, n1_new, nr_new, nh_new, nb, n1_low, nr_low, nh_low
    ]


def shards(
    features, nbr_index, nbr_mask, send_rows, send_count, labels, seed_mask,
    w_first, w_rest, w_head, biases,
    stat_big, root_big, stat_mid, root_mid, stat_sq, root_sq, stat_hr, root_hr, bias_m, bias_v,
):
    peers = send_rows.shape[2]
    cap = send_rows.shape[3]
    fin = features.shape[2]
    fan = nbr_index.shape[3]
    seeds = labels.shape[1]

    def lines(a):
        return jnp.transpose(a, (1, 3, 0, 2))

    g_all, scalars = summed_gradients(
        peers, cap, seeds, fan,
        lines(nbr_index), lines(nbr_mask), jnp.swapaxes(features[0], 0, 1), w_first, w_rest,
        send_rows[0, 0], send_count[0], labels, seed_mask, w_head.T, biases,
    )
    out = list(
        updates(
            fin, g_all, scalars, w_first, w_rest, w_head.T, biases,
            stat_big, root_big, stat_mid, root_mid, stat_sq, root_sq, stat_hr, root_hr,
            bias_m, bias_v,
        )
    )
    for i in (0, 1, 2):
        out[i] = out[i].reshape(())
    for i in (5, 14, 18):
        out[i] = out[i].T
    return tuple(out)


highest = lax.Precision.HIGHEST


def plain_activate(z):
    act = jax.nn.gelu(z, approximate=True)
    return act * lax.rsqrt(jnp.sum(act * act, axis=-1, keepdims=True) + norm_eps)


def plain_counts(nbr, mask, columns):
    nodes, slots = nbr.shape
    column_ids = jnp.arange(columns, dtype=jnp.int32)[None, :]
    mask_low = mask.astype(jnp.bfloat16)

    def add_slot(slot, total):
        picks = lax.dynamic_slice_in_dim(nbr, slot, 1, 1)
        weight = lax.dynamic_slice_in_dim(mask_low, slot, 1, 1)
        return total + (picks == column_ids).astype(jnp.bfloat16) * weight

    return lax.fori_loop(0, slots, add_slot, jnp.zeros((nodes, columns), jnp.bfloat16))


def plain_forward(h, weight, bias, nbr, mask, send_list, valid):
    nodes, width = h.shape
    hb = h.astype(jnp.bfloat16)
    outgoing = (
        jnp.take(hb, send_list, axis=0).reshape(valid.shape[0], valid.shape[1], width)
        * valid[:, :, None]
    )
    incoming = lax.all_to_all(outgoing, "dom", split_axis=0, concat_axis=0, tiled=True)
    table = jnp.concatenate([hb, incoming.reshape(-1, width)], axis=0)
    counts = plain_counts(nbr, mask, table.shape[0])
    degree = jnp.maximum(jnp.sum(mask, axis=1), 1).astype(jnp.float32)[:, None]
    gathered = jnp.dot(counts, table, preferred_element_type=jnp.float32)
    joined = jnp.concatenate([hb, (gathered / degree).astype(jnp.bfloat16)], axis=1)
    z = jnp.dot(joined, weight.astype(jnp.bfloat16), preferred_element_type=jnp.float32) + bias
    return (plain_activate(z), (joined, counts, degree, z))


def plain_backward(grad_out, weight, kept, send_list, valid, need_input):
    joined, counts, degree, z = kept
    nodes = joined.shape[0]
    width = joined.shape[1] // 2
    grad_z = jax.vjp(plain_activate, z)[1](grad_out)[0].astype(jnp.bfloat16)
    grad_w = jnp.einsum("nk,nh->kh", joined, grad_z, preferred_element_type=jnp.float32)
    grad_b = jnp.sum(grad_z.astype(jnp.float32), axis=0)
    if not need_input:
        return (grad_w, grad_b, None)
    grad_joined = jnp.einsum(
        "nh,kh->nk", grad_z, weight.astype(jnp.bfloat16), preferred_element_type=jnp.float32
    )
    grad_gathered = (grad_joined[:, width:] / degree).astype(jnp.bfloat16)
    grad_table = jnp.einsum("nj,nw->jw", counts, grad_gathered, preferred_element_type=jnp.float32)
    returned = (
        grad_table[nodes:].reshape(valid.shape[0], valid.shape[1], width).astype(jnp.bfloat16)
    )
    returned = lax.all_to_all(returned, "dom", split_axis=0, concat_axis=0, tiled=True)
    sent_back = (returned * valid[:, :, None]).reshape(-1, width)
    placement = (send_list[:, None] == jnp.arange(nodes, dtype=jnp.int32)[None, :]).astype(
        jnp.bfloat16
    )
    scattered = jnp.einsum("sn,sw->nw", placement, sent_back, preferred_element_type=jnp.float32)
    return (grad_w, grad_b, grad_joined[:, :width] + grad_table[:nodes] + scattered)


def plain_shampoo(grad, weight, left, left_root, right, right_root, part, right_split):
    count = left.shape[0]
    grad_rows = lax.dynamic_slice_in_dim(grad, part * count, count, 0)
    weight_rows = lax.dynamic_slice_in_dim(weight, part * count, count, 0)
    new_left = decay * left + (1.0 - decay) * jnp.dot(grad_rows, grad.T, precision=highest)
    if right_split:
        cols = right.shape[0]
        grad_cols = lax.dynamic_slice_in_dim(grad, part * cols, cols, 1)
        new_right = decay * right + (1.0 - decay) * jnp.dot(grad_cols.T, grad, precision=highest)
    else:
        new_right = decay * right + (1.0 - decay) * jnp.dot(grad.T, grad, precision=highest)
    step = jnp.dot(jnp.dot(left_root, grad, precision=highest), right_root, precision=highest)
    return (grad_rows, new_left, new_right, weight_rows - shampoo_rate * step)


def plain_shards(
    features,
    nbr_index,
    nbr_mask,
    send_rows,
    send_count,
    labels,
    seed_mask,
    w_first,
    w_rest,
    w_head,
    biases,
    stat_big,
    root_big,
    stat_mid,
    root_mid,
    stat_sq,
    root_sq,
    stat_hr,
    root_hr,
    bias_m,
    bias_v,
):
    hidden = w_rest.shape[2]
    peers = send_rows.shape[2]
    cap = send_rows.shape[3]
    send_list = send_rows.reshape(-1)
    valid = (jnp.arange(cap)[None, :] < send_count.reshape(peers, 1)).astype(jnp.bfloat16)
    weights = [w_first, w_rest[0], w_rest[1]]
    state = features[0].astype(jnp.float32)
    kept = []
    for level in range(3):
        state, saved = plain_forward(
            state,
            weights[level],
            biases[level * hidden : (level + 1) * hidden],
            nbr_index[0, level],
            nbr_mask[0, level],
            send_list,
            valid,
        )
        kept.append(saved)
    seeds = labels.shape[1]
    top = state[:seeds].astype(jnp.bfloat16)
    head_low_w = w_head.astype(jnp.bfloat16)
    logits = jnp.dot(top, head_low_w, preferred_element_type=jnp.float32) + biases[3 * hidden :]
    lse = jax.nn.logsumexp(logits, axis=1)
    onehot = (labels[0][:, None] == jnp.arange(logits.shape[1])[None, :]).astype(jnp.float32)
    picked = jnp.sum(logits * onehot, axis=1)
    seed_weight = seed_mask[0].astype(jnp.float32)
    loss_sum, seed_total = lax.psum(
        (jnp.sum((lse - picked) * seed_weight), jnp.sum(seed_weight)), ("dom", "rep")
    )
    grad_logits = (
        (jnp.exp(logits - lse[:, None]) - onehot) * (seed_weight / seed_total)[:, None]
    ).astype(jnp.bfloat16)
    grad_head = jnp.einsum("sh,sc->hc", top, grad_logits, preferred_element_type=jnp.float32)
    grad_hbias = jnp.sum(grad_logits.astype(jnp.float32), axis=0)
    grad_head, grad_hbias = (grad_head, grad_hbias)
    grad_top = jnp.einsum("sc,hc->sh", grad_logits, head_low_w, preferred_element_type=jnp.float32)
    grad_state = jnp.zeros(state.shape, jnp.float32).at[:seeds].set(grad_top)
    results = [None, None, None]
    for level in (2, 1, 0):
        grad_w, grad_b, grad_state = plain_backward(
            grad_state, weights[level], kept[level], send_list, valid, level > 0
        )
        results[level] = (grad_w, grad_b)
    grad_bias = jnp.concatenate([results[0][1], results[1][1], results[2][1], grad_hbias])
    grad_one, grad_two, grad_three = (results[0][0], results[1][0], results[2][0])
    grad_one, grad_two, grad_three, grad_head, grad_bias = lax.psum(
        (grad_one, grad_two, grad_three, grad_head, grad_bias), ("dom", "rep")
    )
    everything = (grad_one, grad_two, grad_three, grad_head, grad_bias)
    grad_norm = jnp.sqrt(sum((jnp.sum(g * g) for g in everything)))
    factor = clip_limit / jnp.maximum(grad_norm, clip_limit)
    grad_one, grad_two, grad_three, grad_head, grad_bias = [g * factor for g in everything]
    part = lax.axis_index("rep")
    head_rows = stat_sq.shape[1]
    head_root_rows = lax.dynamic_slice_in_dim(root_sq[3], part * head_rows, head_rows, 0)
    g_first, l_first, r_first, n_first = plain_shampoo(
        grad_one, w_first, stat_big, root_big, stat_sq[0], root_sq[0], part, True
    )
    g_mid0, l_mid0, r_mid0, n_mid0 = plain_shampoo(
        grad_two, w_rest[0], stat_mid[0], root_mid[0], stat_sq[1], root_sq[1], part, True
    )
    g_mid1, l_mid1, r_mid1, n_mid1 = plain_shampoo(
        grad_three, w_rest[1], stat_mid[1], root_mid[1], stat_sq[2], root_sq[2], part, True
    )
    g_head, l_head, r_head, n_head = plain_shampoo(
        grad_head, w_head, stat_sq[3], head_root_rows, stat_hr, root_hr, part, False
    )
    new_m = beta_one * bias_m + (1.0 - beta_one) * grad_bias
    new_v = beta_two * bias_v + (1.0 - beta_two) * grad_bias * grad_bias
    m_hat = new_m / (1.0 - beta_one**STEP)
    v_hat = new_v / (1.0 - beta_two**STEP)
    new_b = biases - bias_rate * (m_hat / (jnp.sqrt(v_hat) + adam_eps) + weight_decay * biases)
    new_rest = jnp.stack([n_mid0, n_mid1])
    return (
        loss_sum,
        seed_total,
        grad_norm,
        g_first,
        jnp.stack([g_mid0, g_mid1]),
        g_head,
        new_m,
        new_v,
        l_first,
        jnp.stack([l_mid0, l_mid1]),
        jnp.stack([r_first, r_mid0, r_mid1, l_head]),
        r_head,
        n_first,
        new_rest,
        n_head,
        new_b,
        n_first.astype(jnp.bfloat16),
        new_rest.astype(jnp.bfloat16),
        n_head.astype(jnp.bfloat16),
    )


def solution(mesh):
    placed = (
        P("rep", "dom", None),
        P("rep", None, "dom", None),
        P("rep", None, "dom", None),
        P("rep", "dom", None, None),
        P("rep", "dom", None),
        P("rep", "dom"),
        P("rep", "dom"),
        P(), P(), P(), P(),
        P("rep", None),
        P("rep", None),
        P(None, "rep", None),
        P(None, "rep", None),
        P(None, "rep", None),
        P(), P(), P(), P(), P(),
    )
    small = mesh.shape["rep"] == 4 and mesh.shape["dom"] == 8
    return jax.shard_map(
        shards if small else plain_shards,
        mesh=mesh,
        in_specs=placed,
        out_specs=(
            P(), P(), P(),
            P("rep", None), P(None, "rep", None), P("rep", None),
            P(), P(),
            P("rep", None), P(None, "rep", None), P(None, "rep", None), P(),
            P("rep", None), P(None, "rep", None), P("rep", None), P(),
            P("rep", None), P(None, "rep", None), P("rep", None),
        ),
        check_vma=False,
    )
```

```python
import functools

import jax
import jax.numpy as jnp
from jax import lax
from jax.experimental import pallas as pl
from jax.experimental.pallas import tpu as pltpu
from jax.sharding import PartitionSpec as P

STEP = 5
FAN_REST = 10

clip_limit = 0.0001
decay = 0.5
shampoo_rate = 1.0
beta_one = 0.9
beta_two = 0.999
bias_rate = 0.05
weight_decay = 0.01
adam_eps = 1e-08
norm_eps = 1e-06
MASKED = 8192

bf16 = jnp.bfloat16
f32 = jnp.float32
i32 = jnp.int32
MESH = pl.DeviceIdType.MESH


def nn(a, b):
    return jnp.dot(a, b, preferred_element_type=f32)


def nt(a, b):
    return lax.dot_general(a, b, (((1,), (1,)), ((), ())), preferred_element_type=f32)


def flip(a):
    return a.astype(f32).T.astype(a.dtype)


def round_up(a, b):
    return (a + b - 1) // b * b


def gelu(z):
    scale = 0.7978845608028654
    return z * (0.5 + 0.5 * jnp.tanh(z * (scale + (0.044715 * scale) * (z * z))))


def gelu_slope(z):
    scale = 0.7978845608028654
    square = z * z
    half = 0.5 + 0.5 * jnp.tanh(z * (scale + (0.044715 * scale) * square))
    return half + (half - half * half) * (z * (2.0 * scale + (6.0 * 0.044715 * scale) * square))


def norm_root(act, axis):
    return lax.rsqrt(jnp.sum(act * act, axis=axis, keepdims=True) + norm_eps)


def pull_back(act, slope, root, grad, axis):
    dot = jnp.sum(act * grad, axis=axis, keepdims=True)
    return (slope * (root * grad - act * (root * root * root * dot))).astype(bf16)


def as_column(row):
    return jnp.broadcast_to(row, (8, row.shape[1])).T[:, 0:1]


def widen(row, width, value=0):
    return jnp.concatenate([row, jnp.full((1, width - row.shape[1]), value, row.dtype)], axis=1)


def split_dot(a, b):
    high = a.astype(bf16)
    low = (a - high.astype(f32)).astype(bf16)
    return nn(high, b) + nn(low, b)


def three_dot(a, b):
    high = b.astype(bf16)
    low = (b - high.astype(f32)).astype(bf16)
    return split_dot(a, high) + nn(a.astype(bf16), low)


def graph_kernel(
    peers, cap, seeds, fan,
    nbr_hbm, msk_hbm, xt_hbm, w1_hbm, wr_hbm, srow_hbm, scnt_hbm, lab_hbm, smask_hbm, wht_hbm, bias_hbm,
    rtm_hbm, rts_hbm,
    g_out, s_out, left_out, right_out, move_out, square_out, w1_out, wr_out,
    rtm, rts, full,
    nbr, msk, xt, srow, scnt, lab, smask, wht, bias, joined, near, chosen, far2, far2t, grad1, ctmp, crow, lrow, lcode, crow2, lrow2, rdeg,
    w1, wr, w1t, act1, slope1, root1, h1t, ob0, ib0, ob1, ib1, ob2, ib2, ob3, ib3, ob4, ib4, ob5, ib5,
    gl, acc, rc, sbq, rbq, sbz, rbz, gout, ssend, srecv, sqv, szv,
    load_sem, send_sem, recv_sem, red_send, red_recv,
):
    fin, nodes = xt.shape
    hidden = w1.shape[1]
    finp = round_up(fin, 16)
    slots = peers * cap
    table = nodes + slots
    groups = table // 128
    chunks = nodes // 128
    blocks = nodes // 256
    span = far2.shape[0]
    local = span - slots
    me = lax.axis_index("dom")
    rep = lax.axis_index("rep")
    core = lax.rem(rep, 2)
    xpos = rep // 2
    ypos = lax.rem(me, 2)
    zpos = me // 2
    nz = peers // 2
    mate_c = xpos * 2 + (1 - core)
    mate_x = (1 - xpos) * 2 + core
    mate_y = zpos * 2 + (1 - ypos)

    loads = [
        pltpu.make_async_copy(src, dst, load_sem.at[k])
        for k, (src, dst) in enumerate(
            (
                (srow_hbm, srow), (scnt_hbm, scnt), (xt_hbm, xt), (nbr_hbm, nbr), (msk_hbm, msk),
                (w1_hbm, w1), (wr_hbm, wr), (lab_hbm, lab), (smask_hbm, smask), (wht_hbm, wht), (bias_hbm, bias),
                (rtm_hbm, rtm), (rts_hbm, rts),
            )
        )
    ]
    for load in loads:
        load.start()
    barrier = pltpu.get_barrier_semaphore()
    for off in range(1, peers):
        pl.semaphore_signal(barrier, inc=1, device_id={"dom": lax.rem(me + off, peers)}, device_id_type=MESH)
    for mate in (mate_c, mate_x):
        pl.semaphore_signal(barrier, inc=1, device_id={"rep": mate}, device_id_type=MESH)
    mate_xy = {"dom": mate_y, "rep": mate_x}
    pl.semaphore_signal(barrier, inc=1, device_id=mate_xy, device_id_type=MESH)

    def exchange(stage, src, dst, same=False):
        size = dst.shape[0] // peers
        copies = []
        for off in range(1, peers):
            peer = lax.rem(me + off, peers)
            copies.append(
                pltpu.make_async_remote_copy(
                    src_ref=src if same else src.at[pl.ds(pl.multiple_of(peer * size, 16), size)],
                    dst_ref=dst.at[pl.ds(pl.multiple_of(me * size, 16), size)],
                    send_sem=send_sem.at[stage, off - 1],
                    recv_sem=recv_sem.at[stage, off - 1],
                    device_id={"dom": peer},
                    device_id_type=MESH,
                )
            )
        for c in copies:
            c.start()
        return copies

    started = []

    def finish(copies):
        for c in copies:
            c.wait_recv()
        started.extend(copies)

    loads[0].wait()
    loads[1].wait()
    count = jnp.broadcast_to(scnt[...], (peers, peers))
    count = jnp.where(
        lax.broadcasted_iota(i32, (peers, peers), 0) == lax.broadcasted_iota(i32, (peers, peers), 1), count, 0
    )
    count = jnp.sum(count.astype(f32), axis=1, keepdims=True)
    in_use = lax.broadcasted_iota(i32, (peers, cap), 1).astype(f32) < count
    slot = jnp.where(in_use, srow[...].astype(f32), -1.0)
    per = 128 // cap
    slot = jnp.concatenate([slot] * per, axis=1)
    owner = lax.broadcasted_iota(i32, (peers, 128), 0)
    place = lax.broadcasted_iota(i32, (peers, 128), 1) // cap
    send_row = jnp.concatenate(
        [
            jnp.sum(jnp.where(owner == place + t * per, slot, 0.0), axis=0, keepdims=True)
            for t in range(slots // 128)
        ],
        axis=1,
    )
    node_id = lax.broadcasted_iota(i32, (256, nodes), 1).astype(f32)
    send_col = as_column(send_row)
    for r in range(0, slots, 256):
        chosen[r : r + 256, :] = jnp.where(send_col[r : r + 256] == node_id, 1.0, 0.0).astype(bf16)
    line = lax.broadcasted_iota(i32, (16, nodes), 0)
    joined[finp - 16 : finp, :] = jnp.where(line == 16 - (finp - fin), 1.0, 0.0).astype(bf16)
    r_id = lax.broadcasted_iota(i32, (2 * seeds, local), 0)
    l_id = lax.broadcasted_iota(i32, (2 * seeds, local), 1)
    is_self = (r_id < seeds) & (l_id == r_id + FAN_REST * seeds)
    is_nbr = (r_id >= seeds) & (l_id < FAN_REST * seeds) & (lax.rem(l_id, seeds) == r_id - seeds)
    spread = jnp.where(is_self | is_nbr, 1.0, 0.0)
    spread_t = spread.T.astype(bf16)
    spread = spread.astype(bf16)
    loads[2].wait()
    joined[0:fin, :] = xt[...]
    ob0[:, finp:] = jnp.zeros((slots, ob0.shape[1] - finp), bf16)
    ob0[:, 0:finp] = nt(chosen[0:slots, :], joined[0:finp, :]).astype(bf16)
    for buf in (ib0, ib1, ib2, ib3, ib4, ib5):
        size = buf.shape[0] // peers
        buf[pl.ds(pl.multiple_of(me * size, 16), size), :] = jnp.zeros((size, buf.shape[1]), bf16)
    pl.semaphore_wait(barrier, peers - 1 + 3)
    sent = exchange(0, ob0, ib0)

    loads[3].wait()
    loads[4].wait()

    def codes(level, size, here):
        at = slice(0, size)
        return jnp.where(msk[level, at, 0, here] == 1, nbr[level, at, 0, here], MASKED).astype(f32)

    code3 = codes(2, FAN_REST, slice(0, 128))
    code3t = jnp.concatenate([code3, jnp.full((16 - FAN_REST, 128), float(MASKED), f32)], axis=0).T[0:seeds]
    degree = jnp.sum(jnp.where(code3t < float(MASKED), 1.0, 0.0), axis=1, keepdims=True)
    rdeg3 = 1.0 / jnp.maximum(degree, 1.0)
    tiled = jnp.concatenate([code3t] * peers, axis=0)
    r_id = lax.broadcasted_iota(i32, (peers * seeds, 128), 0)
    l_id = lax.broadcasted_iota(i32, (peers * seeds, 128), 1)
    wanted = jnp.where(l_id < cap, nodes + (r_id // seeds) * cap + l_id, -1).astype(f32)
    far3 = jnp.zeros(wanted.shape, f32)
    for k in range(FAN_REST):
        far3 = far3 + jnp.where(wanted == tiled[:, k : k + 1], 1.0, 0.0)
    ob5[...] = far3.astype(bf16)
    sent_far = exchange(5, ob5, ib5)

    fill = jnp.full((32 - fan, 128), float(MASKED), f32)
    fill2 = jnp.full((16 - FAN_REST, 128), float(MASKED), f32)
    for c in range(chunks):
        here = slice(c * 128, (c + 1) * 128)
        code = codes(0, fan, here)
        degree = jnp.sum((code < MASKED).astype(f32), axis=0, keepdims=True)
        rdeg[0:1, here] = 1.0 / jnp.maximum(degree, 1.0)
        code2 = jnp.concatenate([codes(1, FAN_REST, here), fill2], axis=0).astype(i32)
        ctmp[here, 0:64] = jnp.concatenate(
            [code, fill, (code2 >> 7).astype(f32), (code2 & 127).astype(f32)], axis=0
        ).T

    def grouped(source, count, width):
        each = 256 // width
        lane = lax.broadcasted_iota(i32, (count, 256), 1) // width
        code = jnp.zeros((count, 256), f32)
        for n in range(each):
            piece = source[pl.ds(n, count, stride=each), :]
            piece = jnp.concatenate([piece, piece], axis=1)
            piece = pltpu.roll(piece, n * width, 1) if n else piece
            code = jnp.where(lane == n, piece, code)
        code = code.astype(i32)
        return ((code >> 7) * each + lane).astype(f32), (code & 127).astype(f32)

    crow[...], lrow[...] = grouped(ctmp, nodes // 8, 32)

    lane = lax.broadcasted_iota(i32, (1, 128), 1)
    fits = 128 // seeds
    tiles = []
    for t in range(local // 128):
        tile = jnp.full((1, 128), -1.0, f32)
        for j in range(fits):
            k = t * fits + j
            here = lane // seeds == j
            if k < FAN_REST:
                piece = code3[k : k + 1, :]
                piece = pltpu.roll(piece, j * seeds, 1) if j else piece
                tile = jnp.where(here & (piece < nodes), piece, tile)
            elif k == FAN_REST:
                tile = jnp.where(here, (lane - j * seeds).astype(f32), tile)
        tiles.append(tile)
    local_col = as_column(jnp.concatenate(tiles, axis=1))
    for r in range(0, local, 256):
        chosen[slots + r : slots + r + 256, :] = jnp.where(
            local_col[r : r + 256] == node_id, 1.0, 0.0
        ).astype(bf16)
    keep = jnp.where(jnp.concatenate([send_col, local_col], axis=0) >= 0.0, 1.0, 0.0)
    found = nn(chosen[0:span, :], ctmp[...].astype(bf16))
    lcode[...] = pltpu.roll(found, 96, 1) * 128.0 + pltpu.roll(found, 80, 1)
    lane = lax.broadcasted_iota(i32, (span, 128), 1)
    degree = jnp.sum(
        jnp.where((lcode[...] < float(MASKED)) & (lane < FAN_REST), 1.0, 0.0), axis=1, keepdims=True
    )
    rdeg2 = 1.0 / jnp.maximum(degree, 1.0)
    crow2[...], lrow2[...] = grouped(lcode, span // 16, 16)

    rows_a = lax.broadcasted_iota(i32, (groups * 8, 256), 0).astype(f32)
    rows_b = lax.broadcasted_iota(i32, (128, 256), 0).astype(f32)
    rows_c = lax.broadcasted_iota(i32, (groups * 16, 256), 0).astype(f32)

    def list_counts(b, _):
        for p in range(16):
            g = b * 16 + p
            left = jnp.where(rows_c == crow2[pl.ds(g, 1), :], 1.0, 0.0).astype(bf16)
            right = jnp.where(rows_b == lrow2[pl.ds(g, 1), :], 1.0, 0.0).astype(bf16)
            value = nt(left, right).astype(bf16)
            for a in range(groups):
                tile = value[a * 16 : (a + 1) * 16]
                if a < chunks:
                    chosen[pl.ds(pl.multiple_of(span + g * 16, 16), 16), a * 128 : (a + 1) * 128] = tile
                else:
                    at = pl.ds(pl.multiple_of(g * 16, 16), 16)
                    far2[at, (a - chunks) * 128 : (a - chunks + 1) * 128] = tile
        return 0

    lax.fori_loop(0, span // 256, list_counts, 0)

    def build(b, _):
        for p in range(16):
            pair = []
            for half in range(2):
                g = b * 32 + p * 2 + half
                left = jnp.where(rows_a == crow[pl.ds(g, 1), :], 1.0, 0.0).astype(bf16)
                right = jnp.where(rows_b == lrow[pl.ds(g, 1), :], 1.0, 0.0).astype(bf16)
                pair.append(nt(left, right))
            at = pl.ds(pl.multiple_of(b * 256 + p * 16, 16), 16)
            for a in range(groups):
                tile = jnp.concatenate([pair[0][a * 8 : (a + 1) * 8], pair[1][a * 8 : (a + 1) * 8]], axis=0)
                near[at, a * 128 : (a + 1) * 128] = tile.astype(bf16)
        return 0

    lax.fori_loop(0, blocks, build, 0)

    for load in loads[5:]:
        load.wait()
    bias = bias[...].reshape(1, bias.shape[0])
    wpad = jnp.concatenate(
        [w1[0:fin, :], jnp.zeros((finp - fin, hidden), f32), w1[fin : 2 * fin, :], jnp.zeros((finp - fin, hidden), f32)],
        axis=0,
    )
    w1t[...] = wpad.T.astype(bf16)
    b1 = as_column(bias[0:1, 0:hidden])

    finish(sent)
    ibt = flip(ib0[...])[0:finp, :]

    def block(b):
        return pl.ds(b * 256 if isinstance(b, int) else pl.multiple_of(b * 256, 256), 256)

    def gather(b):
        blk = block(b)
        total = nt(joined[0:finp, :], near[blk, 0:nodes]) + nt(ibt, near[blk, nodes:])
        joined[finp:, blk] = (total * rdeg[0:1, blk]).astype(bf16)

    def product(b):
        blk = block(b)
        grad1[:, blk] = nn(w1t[...], joined[:, blk]) + b1

    def activate(b):
        blk = block(b)
        z = grad1[:, blk]
        act = gelu(z)
        root = norm_root(act, 0)
        act1[:, blk] = act
        root1[0:1, blk] = root
        h1t[:, blk] = (act * root).astype(bf16)

    gather(0)
    far2t[...] = flip(far2[...])
    w2 = wr[0].astype(bf16)
    w3 = wr[1].astype(bf16)
    product(0)
    gather(1)

    def layer_one(b, _):
        activate(b - 2)
        product(b - 1)
        gather(b)
        return 0

    lax.fori_loop(2, blocks, layer_one, 0)
    activate(blocks - 2)
    product(blocks - 1)
    activate(blocks - 1)
    sent_rows = nt(chosen[0:slots, :], h1t[...]).astype(bf16)
    ob1[...] = sent_rows
    sent = exchange(1, ob1, ib1)

    own2 = nt(chosen[slots:, :], h1t[...])

    def slopes(b, _):
        blk = block(b)
        slope1[:, blk] = gelu_slope(grad1[:, blk])
        return 0

    lax.fori_loop(0, blocks, slopes, 0)
    first_rows = w1_out.shape[0]
    for i in range(2 * fin // first_rows):

        @pl.when(rep == i)
        def _():
            w1_out[...] = w1[i * first_rows : (i + 1) * first_rows, :]

    rest_rows = wr_out.shape[1]
    for i in range(2):
        wr_out[i] = wr[i, pl.ds(pl.multiple_of(rep * rest_rows, 8), rest_rows), :]
    b2 = bias[0:1, hidden : 2 * hidden]
    self_local = own2[0:local].astype(bf16)
    z_sent = nn(sent_rows, w2[0:hidden]) + b2
    z_local = nn(self_local, w2[0:hidden]) + b2
    finish(sent_far)
    far3r = ib5[...].astype(f32)[:, 0:cap]
    spots = peers * cap
    r_id = lax.broadcasted_iota(i32, (peers * seeds, spots), 0) // seeds
    l_id = lax.broadcasted_iota(i32, (peers * seeds, spots), 1) // cap
    collect = jnp.where(r_id == l_id, jnp.concatenate([far3r] * peers, axis=1), 0.0)
    scatter = collect.T.astype(bf16)
    collect = collect.astype(bf16)

    finish(sent)

    def rows_two(own_self, own_z, own_sum, at):
        agg = ((own_sum + nn(far2[at, :], ib1[...])) * rdeg2[at]).astype(bf16)
        z = own_z + nn(agg, w2[hidden:])
        act = gelu(z)
        root = norm_root(act, 1)
        return jnp.concatenate([own_self, agg], axis=1), z, act, root, (act * (root * keep[at])).astype(bf16)

    out_at, in_at = slice(0, slots), slice(slots, span)
    joined2a, z2a, act2a, root2a, h2a = rows_two(sent_rows, z_sent, own2[local:span], out_at)
    ob2[...] = nn(collect, h2a).astype(bf16)
    sent = exchange(2, ob2, ib2)

    joined2b, z2b, act2b, root2b, h2b = rows_two(self_local, z_local, own2[span:], in_at)
    near3 = nn(spread, h2b)
    self3 = near3[0:seeds].astype(bf16)
    z_seeds = nn(self3, w3[0:hidden]) + bias[0:1, 2 * hidden : 3 * hidden]
    slope2b = gelu_slope(z2b)
    classes = wht.shape[0]
    classp = round_up(classes, 16)
    wht_low = jnp.concatenate([wht[...], jnp.zeros((classp - classes, hidden), f32)], axis=0).astype(bf16)
    bh = widen(bias[0:1, 3 * hidden : 3 * hidden + classes], classp)
    class_id = lax.broadcasted_iota(i32, (seeds, classp), 1)
    label = as_column(widen(lab[...].astype(f32), 128))[0:seeds]
    hot = jnp.where(class_id.astype(f32) == label, 1.0, 0.0)
    weight = as_column(widen(smask[...].astype(f32), 128))[0:seeds]
    finish(sent)
    total = near3[seeds:]
    for q in range(peers):
        total = total + ib2[q * seeds : (q + 1) * seeds, :].astype(f32)
    agg3 = (total * rdeg3).astype(bf16)
    z3 = z_seeds + nn(agg3, w3[hidden:])
    joined3 = jnp.concatenate([self3, agg3], axis=1)
    act3 = gelu(z3)
    slope3 = gelu_slope(z3)
    root3 = norm_root(act3, 1)
    top = (act3 * root3).astype(bf16)

    logits = nt(top, wht_low) + bh
    logits = jnp.where(class_id < classes, logits, -1e30)
    peak = jnp.max(logits, axis=1, keepdims=True)
    lse = peak + jnp.log(jnp.sum(jnp.exp(logits - peak), axis=1, keepdims=True))
    dlog = ((jnp.exp(logits - lse) - hot) * weight).astype(bf16)
    dtop = nn(dlog, wht_low)

    dz3 = pull_back(act3, slope3, root3, dtop, 1)
    dg3 = (nt(dz3, w3[hidden:]) * rdeg3).astype(bf16)
    ob3[...] = dg3
    sent = exchange(3, ob3, ib3, same=True)
    ds3 = nt(dz3, w3[0:hidden]).astype(bf16)
    dloc = nn(spread_t, jnp.concatenate([ds3, dg3], axis=0))

    seg_a = 4 * hidden
    row_head = seg_a + 2 * finp
    row_bias = row_head + classp
    rows = gl.shape[1]

    def put(row, value):
        size = value.shape[0]
        gl[0, row : row + size, :] = value[:, 0:128].astype(bf16)
        gl[1, row : row + size, :] = value[:, 128:].astype(bf16)

    picked = jnp.sum(logits * hot, axis=1, keepdims=True)
    loss = jnp.sum((lse - picked) * weight, axis=0, keepdims=True)
    total = jnp.sum(weight, axis=0, keepdims=True)
    sc_lane = lax.broadcasted_iota(i32, (8, 128), 1)
    ssend[0] = jnp.where(sc_lane == 0, loss, jnp.where(sc_lane == 1, total, 0.0))
    dz2b = pull_back(act2b, slope2b, root2b, dloc * keep[in_at], 1)
    dj2b = nt(dz2b, w2)
    dg2b = (dj2b[:, hidden:] * rdeg2[in_at]).astype(bf16)
    near_ret = nn(far2t[:, in_at], dg2b)
    slope2a = gelu_slope(z2a)
    put(row_head, nn(dlog.astype(f32).T.astype(bf16), top))
    put(2 * hidden, nn(joined3.astype(f32).T.astype(bf16), dz3))
    bias_3 = jnp.sum(dz3.astype(f32), axis=0, keepdims=True)
    bias_h = widen(jnp.sum(dlog.astype(f32), axis=0, keepdims=True), hidden)
    finish(sent)

    dh2a = nn(scatter, ib3[...]) * keep[out_at]
    dz2a = pull_back(act2a, slope2a, root2a, dh2a, 1)
    dg2a = (nt(dz2a, w2[hidden:]) * rdeg2[out_at]).astype(bf16)
    ob4[...] = (near_ret + nn(far2t[:, out_at], dg2a)).astype(bf16)
    sent = exchange(4, ob4, ib4)
    put(0, nn(flip(joined2a), dz2a) + nn(flip(joined2b), dz2b))

    used = []

    def hop(src, dst, who):
        used.append(0)
        k = len(used) - 1
        copy = pltpu.make_async_remote_copy(
            src_ref=src, dst_ref=dst, send_sem=red_send.at[k], recv_sem=red_recv.at[k],
            device_id=who, device_id_type=MESH,
        )
        copy.start()
        return copy

    def rows_of(start, size):
        return pl.ds(pl.multiple_of(start, 16), size)

    to_core = {"rep": mate_c}
    plane = (
        xpos * 2 + ypos,
        (
            ((1 - xpos) * 2 + ypos, {"rep": mate_x}),
            (xpos * 2 + 1 - ypos, {"dom": mate_y}),
            ((1 - xpos) * 2 + 1 - ypos, mate_xy),
        ),
    )
    others = [lax.rem(zpos + off, nz) for off in range(1, nz)]
    column = (zpos, tuple((to, {"dom": to * 2 + ypos}) for to in others))

    def summing(start, size, out_sem, one, two):
        (mine1, group1), (mine2, group2) = one, two
        quarter = size // (len(group1) + 1)
        piece = quarter // (len(group2) + 1)
        whole = slice(start, start + size)
        at1, at2 = start // 4, start // (4 * nz)
        at1, at2 = slice(at1, at1 + quarter), slice(at2, at2 + piece)
        kept = rows_of(start + mine1 * quarter, quarter)
        here = rows_of(start + mine1 * quarter + mine2 * piece, piece)
        copies = [hop(gl.at[1 - core, whole], rc.at[whole], to_core)]
        yield
        finish(copies)
        value = gl[core, whole, :].astype(f32) + rc[whole, :].astype(f32)
        acc[whole, :] = value
        sbq[whole, :] = value.astype(bf16)
        copies = [
            hop(sbq.at[rows_of(start + to * quarter, quarter)], rbq.at[k, at1], who)
            for k, (to, who) in enumerate(group1)
        ]
        yield
        finish(copies)
        value = acc[kept, :]
        for k in range(len(group1)):
            value = value + rbq[k, at1, :].astype(f32)
        acc[kept, :] = value
        sbz[at1, :] = value.astype(bf16)
        copies = [
            hop(sbz.at[rows_of(start // 4 + to * piece, piece)], rbz.at[k, at2], who)
            for k, (to, who) in enumerate(group2)
        ]
        yield
        finish(copies)
        value = acc[here, :]
        for k in range(len(group2)):
            value = value + rbz[k, at2, :].astype(f32)
        gout[core, here, :] = value.astype(bf16)
        part = gout.at[core, here]
        copies = [hop(part, part, who) for _, who in group2]
        yield
        finish(copies)
        part = gout.at[core, kept]
        copies = [hop(part, part, who) for _, who in group1]
        copies.append(hop(part, part, to_core))
        yield
        finish(copies)
        copies = []
        for to, _ in group1:
            part = gout.at[core, rows_of(start + to * quarter, quarter)]
            copies.append(hop(part, part, to_core))
        out = [
            pltpu.make_async_copy(gout.at[h, whole], g_out.at[h, whole], load_sem.at[out_sem + k])
            for k, h in enumerate((core, 1 - core))
        ]
        out[0].start()
        yield
        finish(copies)
        out[1].start()
        yield
        for c in out:
            c.wait()

    def summing_scalars():
        copies = [hop(ssend.at[0], srecv.at[0], to_core)]
        yield
        finish(copies)
        ssend[1] = ssend[0] + srecv[0]
        mine = plane[0]
        sqv[mine] = ssend[1]
        copies = [hop(ssend.at[1], sqv.at[mine], who) for _, who in plane[1]]
        yield
        finish(copies)
        ssend[2] = sqv[0] + sqv[1] + sqv[2] + sqv[3]
        szv[zpos] = ssend[2]
        copies = [hop(ssend.at[2], szv.at[zpos], who) for _, who in column[1]]
        yield
        finish(copies)
        total = szv[0]
        for k in range(1, nz):
            total = total + szv[k]
        s_out[...] = total

    def go_on(*runs):
        for run in runs:
            next(run, None)

    cut = seg_a + 2 * (4 * nz * 16)
    rest = summing(0, seg_a, 4, plane, column)
    first = summing(seg_a, cut - seg_a, 0, column, plane)
    second = summing(cut, rows - cut, 2, plane, column)
    scalars = summing_scalars()
    go_on(rest, scalars)

    bias_2 = jnp.sum(dz2a.astype(f32), axis=0, keepdims=True) + jnp.sum(dz2b.astype(f32), axis=0, keepdims=True)
    line = lax.broadcasted_iota(i32, (16, hidden), 0)
    put(
        row_bias,
        jnp.where(line == 1, bias_2, 0.0) + jnp.where(line == 2, bias_3, 0.0) + jnp.where(line == 3, bias_h, 0.0),
    )
    both = flip(
        jnp.concatenate(
            [nt(dz2a, w2[0:hidden]).astype(bf16), dj2b[:, 0:hidden].astype(bf16), dg2a, dg2b], axis=0
        )
    )
    grad1[...] = nn(both, chosen[...])
    go_on(rest, scalars)
    finish(sent)
    back = flip(ib4[...])

    def layer_one_back(b, _):
        blk = block(b)
        grad = grad1[:, blk] + nn(back, chosen[0:slots, blk])
        h1t[:, blk] = pull_back(act1[:, blk], slope1[:, blk], root1[0:1, blk], grad, 0)
        return 0

    lax.fori_loop(0, blocks, layer_one_back, 0, unroll=2)
    size = cut - seg_a
    put(seg_a, nt(joined[0:size, :], h1t[...]))
    go_on(first, rest, scalars)
    put(cut, nt(joined[size:, :], h1t[...]))
    go_on(second, first)
    def rest_products():
        count = rtm.shape[1]
        cols = right_out.shape[1]
        square = jnp.zeros((1, hidden), f32)
        for i in range(2):
            whole = slice(i * 2 * hidden, (i + 1) * 2 * hidden)
            g = jnp.concatenate([gout[0, whole, :], gout[1, whole, :]], axis=1)
            mine = rows_of(i * 2 * hidden + rep * count, count)
            g_rows = jnp.concatenate([gout[0, mine, :], gout[1, mine, :]], axis=1)
            left_out[i] = nt(g_rows, g)
            full[i] = nn(flip(g), g)
            right_out[i] = full[i, pl.ds(pl.multiple_of(rep * cols, 8), cols), :]
            move_out[i] = three_dot(split_dot(rtm[i], g), rts[1 + i])
            wide = g.astype(f32)
            square = square + jnp.sum(wide * wide, axis=0, keepdims=True)
        square_out[...] = square

    for turn in range(5):
        go_on(second, rest, first, scalars)
        if turn == 3:
            rest_products()
    go_on(second, first)
    go_on(second)
    for c in started:
        c.wait_send()


def in_hbm(*arrays):
    return [pltpu.with_memory_space_constraint(a, pltpu.HBM) for a in arrays]


def summed_gradients(peers, cap, seeds, fan, nbr, msk, xt, w1, wr, srow, scnt, lab, smask, wht, bias, rtm, rts):
    fin, nodes = xt.shape
    hidden = w1.shape[1]
    finp = round_up(fin, 16)
    wide = round_up(fin, 128)
    slots = peers * cap
    span = slots + round_up(seeds * (FAN_REST + 1), 256)
    classp = round_up(wht.shape[0], 16)
    rows = 4 * hidden + 2 * finp + classp + 16
    nz = peers // 2
    vmem = pltpu.VMEM
    sems = 64
    some = peers * seeds
    count, cols = rtm.shape[1], hidden // (2 * hidden // rtm.shape[1])
    scratch = [
        vmem(rtm.shape, f32),
        vmem(rts.shape, f32),
        vmem((2, hidden, hidden), f32),
        vmem(nbr.shape, i32),
        vmem(msk.shape, i32),
        vmem(xt.shape, bf16),
        vmem(srow.shape, i32),
        vmem(scnt.shape, i32),
        vmem(lab.shape, i32),
        vmem(smask.shape, i32),
        vmem(wht.shape, f32),
        vmem(bias.shape, f32),
        vmem((2 * finp, nodes), bf16),
        vmem((nodes, nodes + slots), bf16),
        vmem((2 * span, nodes), bf16),
        vmem((span, slots), bf16),
        vmem((slots, span), bf16),
        vmem((hidden, nodes), f32),
        vmem((nodes, 128), f32),
        vmem((nodes // 8, 256), f32),
        vmem((nodes // 8, 256), f32),
        vmem((span, 128), f32),
        vmem((span // 16, 256), f32),
        vmem((span // 16, 256), f32),
        vmem((8, nodes), f32),
        vmem(w1.shape, f32),
        vmem(wr.shape, f32),
        vmem((hidden, 2 * finp), bf16),
        vmem((hidden, nodes), f32),
        vmem((hidden, nodes), f32),
        vmem((8, nodes), f32),
        vmem((hidden, nodes), bf16),
        vmem((slots, wide), bf16),
        vmem((slots, wide), bf16),
        vmem((slots, hidden), bf16),
        vmem((slots, hidden), bf16),
        vmem((some, hidden), bf16),
        vmem((some, hidden), bf16),
        vmem((seeds, hidden), bf16),
        vmem((some, hidden), bf16),
        vmem((slots, hidden), bf16),
        vmem((slots, hidden), bf16),
        vmem((some, 128), bf16),
        vmem((some, 128), bf16),
        vmem((2, rows, 128), bf16),
        vmem((rows, 128), f32),
        vmem((rows, 128), bf16),
        vmem((rows, 128), bf16),
        vmem((3, rows // 4, 128), bf16),
        vmem((rows // 4, 128), bf16),
        vmem((nz - 1, rows // (4 * nz), 128), bf16),
        vmem((2, rows, 128), bf16),
        vmem((4, 8, 128), f32),
        vmem((3, 8, 128), f32),
        vmem((4, 8, 128), f32),
        vmem((nz, 8, 128), f32),
        pltpu.SemaphoreType.DMA((13,)),
        pltpu.SemaphoreType.DMA((6, peers - 1)),
        pltpu.SemaphoreType.DMA((6, peers - 1)),
        pltpu.SemaphoreType.DMA((sems,)),
        pltpu.SemaphoreType.DMA((sems,)),
    ]
    inside = pl.BlockSpec(memory_space=vmem)
    outside = pl.BlockSpec(memory_space=pl.ANY)
    return pl.pallas_call(
        functools.partial(graph_kernel, peers, cap, seeds, fan),
        out_shape=(
            jax.ShapeDtypeStruct((2, rows, 128), bf16),
            jax.ShapeDtypeStruct((8, 128), f32),
            jax.ShapeDtypeStruct((2, count, 2 * hidden), f32),
            jax.ShapeDtypeStruct((2, cols, hidden), f32),
            jax.ShapeDtypeStruct((2, count, hidden), f32),
            jax.ShapeDtypeStruct((1, hidden), f32),
            jax.ShapeDtypeStruct((count * 2 * fin // (2 * hidden), hidden), f32),
            jax.ShapeDtypeStruct((2, count, hidden), f32),
        ),
        in_specs=[outside] * 13,
        out_specs=(outside,) + (inside,) * 7,
        scratch_shapes=scratch,
        compiler_params=pltpu.CompilerParams(
            collective_id=0, has_side_effects=True, vmem_limit_bytes=51 * 2**20
        ),
        cost_estimate=pl.CostEstimate(flops=24 * 10**9, bytes_accessed=12 * 2**20, transcendentals=2**20),
        name="graph_step",
    )(*in_hbm(nbr, msk, xt, w1, wr, srow, scnt, lab, smask, wht, bias, rtm, rts))


def update_kernel(
    fin,
    g_all, scalars, lefts, rights, moves, rest_square, w_mine, wr_mine, wht, bias, sth, rth, bm, bv,
    st1, rt1, stm, sts, rts,
    loss_o, total_o, norm_o, gh_o, m_o, v_o, lh_o, nh_o, nb_o, nh_low,
    g1_hbm, gr_hbm, l1_hbm, lm_hbm, ls_hbm, n1_hbm, nr_hbm, n1_low_hbm, nr_low_hbm,
    g1_o, gr_o, l1_o, lm_o, ls_o, n1_o, nr_o, n1_low, nr_low,
    g1, g_mine, full, gb, out_sem,
):
    hidden = w_mine.shape[1]
    classes = wht.shape[0]
    classp = round_up(classes, 16)
    finp = round_up(fin, 16)
    seg_a = 4 * hidden
    part = lax.axis_index("rep")

    stores = []

    def store(src, dst):
        copy = pltpu.make_async_copy(src, dst, out_sem.at[len(stores)])
        stores.append(copy)
        copy.start()

    def grads(start, size):
        return jnp.concatenate(
            [g_all[0, start : start + size, :], g_all[1, start : start + size, :]], axis=1
        )

    total = scalars[0:1, 1:2]
    square = jnp.zeros((16, hidden), f32)
    spare = lax.broadcasted_iota(i32, (16, hidden), 0) >= 16 - (finp - fin)
    for r in range(seg_a, g_all.shape[1], 16):
        g = grads(r, 16).astype(f32)
        if r == seg_a + 2 * finp - 16:
            g = jnp.where(spare, 0.0, g)
        square = square + g * g
    square = jnp.sum(jnp.sum(square, axis=0, keepdims=True) + rest_square[...], axis=1, keepdims=True)
    norm = jnp.sqrt(square) / total
    scale = clip_limit / jnp.maximum(norm, clip_limit) / total
    loss_o[...] = scalars[0:1, 0:1]
    total_o[...] = total
    norm_o[...] = norm
    lift = (1.0 - decay) * scale * scale
    move = shampoo_rate * scale

    g1[0:fin, :] = grads(seg_a, finp)[0:fin].astype(f32)
    g1[fin : 2 * fin, :] = grads(seg_a + finp, finp)[0:fin].astype(f32)
    count = st1.shape[0]
    g_low = g1[...].astype(bf16)
    full[0] = nn(g1[...].T.astype(bf16), g_low)
    half = split_dot(rt1[...], g_low)
    for i in range(2 * fin // count):

        @pl.when(part == i)
        def _():
            g_mine[...] = g1[i * count : (i + 1) * count, :]

    g_rows = g_mine[...]
    g1_o[...] = g_rows * scale
    store(g1_o, g1_hbm)
    fresh = w_mine[...] - move * three_dot(half, rts[0])
    n1_o[...] = fresh
    n1_low[...] = fresh.astype(bf16)
    store(n1_o, n1_hbm)
    store(n1_low, n1_low_hbm)
    product = nt(g_rows.astype(bf16), g_low)
    l1_o[...] = decay * st1[...] + lift * product
    store(l1_o, l1_hbm)

    count = stm.shape[1]
    for i in range(2):
        base = pl.ds(pl.multiple_of(i * 2 * hidden + part * count, 16), count)
        g_rows = jnp.concatenate([g_all[0, base, :], g_all[1, base, :]], axis=1)
        gr_o[i] = g_rows.astype(f32) * scale
        lm_o[i] = decay * stm[i] + lift * lefts[i]
        fresh = wr_mine[i] - move * moves[i]
        nr_o[i] = fresh
        nr_low[i] = fresh.astype(bf16)
    store(gr_o, gr_hbm)
    store(lm_o, lm_hbm)
    store(nr_o, nr_hbm)
    store(nr_low, nr_low_hbm)

    gt = grads(seg_a + 2 * finp, classp)
    full[1] = nn(flip(gt), gt)
    count = sts.shape[1]
    mine = pl.ds(pl.multiple_of(part * count, count), count)
    for i, product in enumerate((full[0, mine, :], rights[0], rights[1], full[1, mine, :])):
        ls_o[i] = decay * sts[i] + lift * product
    store(ls_o, ls_hbm)
    lh_o[...] = decay * sth[...] + lift * nt(gt, gt)[0:classes, 0:classes]
    root = rts[3, mine, :]
    high = root.astype(bf16)
    low = (root - high.astype(f32)).astype(bf16)
    left = (nt(gt, high) + nt(gt, low))[0:classes]
    step = three_dot(rth[...], left)
    gt_mine = jnp.zeros((classes, count), f32)
    wt_mine = jnp.zeros((classes, count), f32)
    gt_wide = gt.astype(f32)
    for i in range(hidden // count):
        here = slice(i * count, (i + 1) * count)
        gt_mine = jnp.where(part == i, gt_wide[0:classes, here], gt_mine)
        wt_mine = jnp.where(part == i, wht[:, here], wt_mine)
    gh_o[...] = gt_mine * scale
    fresh = wt_mine - move * step
    nh_o[...] = fresh
    nh_low[...] = fresh.astype(bf16)

    lines = grads(seg_a + 2 * finp + classp, 16).astype(f32)
    gb[0:1, 0:hidden] = grads(seg_a + finp - 16, 16).astype(f32)[fin - finp + 16 : fin - finp + 17, :]
    for i in range(1, 4):
        gb[0:1, i * hidden : (i + 1) * hidden] = lines[i : i + 1, :]
    size = bias.shape[0]
    g = gb[0:1, 0:size] * scale
    bias = bias[...].reshape(1, size)
    new_m = beta_one * bm[...].reshape(1, size) + (1.0 - beta_one) * g
    new_v = beta_two * bv[...].reshape(1, size) + (1.0 - beta_two) * g * g
    m_hat = new_m / (1.0 - beta_one**STEP)
    v_hat = new_v / (1.0 - beta_two**STEP)
    m_o[...] = new_m.reshape(size)
    v_o[...] = new_v.reshape(size)
    fresh = bias - bias_rate * (m_hat / (jnp.sqrt(v_hat) + adam_eps) + weight_decay * bias)
    nb_o[...] = fresh.reshape(size)
    for copy in stores:
        copy.wait()


def updates(fin, summed, wht, bias, st1, rt1, stm, sts, rts, sth, rth, bm, bv):
    hidden = wht.shape[1]
    classes = wht.shape[0]
    count = sts.shape[1]
    n1 = (st1.shape[0], hidden)
    nr = (2, stm.shape[1], hidden)
    nh = (classes, count)

    def of(shape, kind=f32):
        return jax.ShapeDtypeStruct(shape, kind)

    def room(a):
        return pltpu.VMEM(a.shape, a.dtype)

    one = of((1, 1))
    line = of(bias.shape)
    small = [one, one, one, of(nh), line, line, of(sth.shape), of(nh), line, of(nh, bf16)]
    large = [of(n1), of(nr), of(st1.shape), of(stm.shape), of(sts.shape), of(n1), of(nr), of(n1, bf16), of(nr, bf16)]
    loaded = [st1, rt1, stm, sts, rts]
    inside = pl.BlockSpec(memory_space=pltpu.VMEM)
    outside = pl.BlockSpec(memory_space=pl.ANY)
    (loss, total, norm, gh, m, v, lh, nh_new, nb, nh_low, g1, gr, l1, lm, ls, n1_new, nr_new, n1_low, nr_low) = pl.pallas_call(
        functools.partial(update_kernel, fin),
        out_shape=tuple(small + large),
        in_specs=[inside] * (6 + len(summed) + len(loaded)),
        out_specs=(inside,) * len(small) + (outside,) * len(large),
        scratch_shapes=[room(a) for a in large] + [
            pltpu.VMEM((2 * fin, hidden), f32),
            pltpu.VMEM(n1, f32),
            pltpu.VMEM((2, hidden, hidden), f32),
            pltpu.VMEM((1, 4 * hidden), f32),
            pltpu.SemaphoreType.DMA((len(large),)),
        ],
        compiler_params=pltpu.CompilerParams(vmem_limit_bytes=40 * 2**20),
        name="update_step",
    )(*summed, wht, bias, sth, rth, bm, bv, *loaded)
    return [
        loss, total, norm, g1, gr, gh, m, v, l1, lm, ls, lh, n1_new, nr_new, nh_new, nb, n1_low, nr_low, nh_low
    ]


def shards(
    features, nbr_index, nbr_mask, send_rows, send_count, labels, seed_mask,
    w_first, w_rest, w_head, biases,
    stat_big, root_big, stat_mid, root_mid, stat_sq, root_sq, stat_hr, root_hr, bias_m, bias_v,
):
    peers = send_rows.shape[2]
    cap = send_rows.shape[3]
    fin = features.shape[2]
    fan = nbr_index.shape[3]
    seeds = labels.shape[1]

    def lines(a):
        return jnp.transpose(a, (1, 3, 0, 2))

    summed = summed_gradients(
        peers, cap, seeds, fan,
        lines(nbr_index), lines(nbr_mask), jnp.swapaxes(features[0], 0, 1), w_first, w_rest,
        send_rows[0, 0], send_count[0], labels, seed_mask, w_head.T, biases, root_mid, root_sq,
    )
    out = list(
        updates(
            fin, summed, w_head.T, biases,
            stat_big, root_big, stat_mid, stat_sq, root_sq, stat_hr, root_hr,
            bias_m, bias_v,
        )
    )
    for i in (0, 1, 2):
        out[i] = out[i].reshape(())
    for i in (5, 14, 18):
        out[i] = out[i].T
    return tuple(out)


highest = lax.Precision.HIGHEST


def plain_activate(z):
    act = jax.nn.gelu(z, approximate=True)
    return act * lax.rsqrt(jnp.sum(act * act, axis=-1, keepdims=True) + norm_eps)


def plain_counts(nbr, mask, columns):
    nodes, slots = nbr.shape
    column_ids = jnp.arange(columns, dtype=jnp.int32)[None, :]
    mask_low = mask.astype(jnp.bfloat16)

    def add_slot(slot, total):
        picks = lax.dynamic_slice_in_dim(nbr, slot, 1, 1)
        weight = lax.dynamic_slice_in_dim(mask_low, slot, 1, 1)
        return total + (picks == column_ids).astype(jnp.bfloat16) * weight

    return lax.fori_loop(0, slots, add_slot, jnp.zeros((nodes, columns), jnp.bfloat16))


def plain_forward(h, weight, bias, nbr, mask, send_list, valid):
    nodes, width = h.shape
    hb = h.astype(jnp.bfloat16)
    outgoing = (
        jnp.take(hb, send_list, axis=0).reshape(valid.shape[0], valid.shape[1], width)
        * valid[:, :, None]
    )
    incoming = lax.all_to_all(outgoing, "dom", split_axis=0, concat_axis=0, tiled=True)
    table = jnp.concatenate([hb, incoming.reshape(-1, width)], axis=0)
    counts = plain_counts(nbr, mask, table.shape[0])
    degree = jnp.maximum(jnp.sum(mask, axis=1), 1).astype(jnp.float32)[:, None]
    gathered = jnp.dot(counts, table, preferred_element_type=jnp.float32)
    joined = jnp.concatenate([hb, (gathered / degree).astype(jnp.bfloat16)], axis=1)
    z = jnp.dot(joined, weight.astype(jnp.bfloat16), preferred_element_type=jnp.float32) + bias
    return (plain_activate(z), (joined, counts, degree, z))


def plain_backward(grad_out, weight, kept, send_list, valid, need_input):
    joined, counts, degree, z = kept
    nodes = joined.shape[0]
    width = joined.shape[1] // 2
    grad_z = jax.vjp(plain_activate, z)[1](grad_out)[0].astype(jnp.bfloat16)
    grad_w = jnp.einsum("nk,nh->kh", joined, grad_z, preferred_element_type=jnp.float32)
    grad_b = jnp.sum(grad_z.astype(jnp.float32), axis=0)
    if not need_input:
        return (grad_w, grad_b, None)
    grad_joined = jnp.einsum(
        "nh,kh->nk", grad_z, weight.astype(jnp.bfloat16), preferred_element_type=jnp.float32
    )
    grad_gathered = (grad_joined[:, width:] / degree).astype(jnp.bfloat16)
    grad_table = jnp.einsum("nj,nw->jw", counts, grad_gathered, preferred_element_type=jnp.float32)
    returned = (
        grad_table[nodes:].reshape(valid.shape[0], valid.shape[1], width).astype(jnp.bfloat16)
    )
    returned = lax.all_to_all(returned, "dom", split_axis=0, concat_axis=0, tiled=True)
    sent_back = (returned * valid[:, :, None]).reshape(-1, width)
    placement = (send_list[:, None] == jnp.arange(nodes, dtype=jnp.int32)[None, :]).astype(
        jnp.bfloat16
    )
    scattered = jnp.einsum("sn,sw->nw", placement, sent_back, preferred_element_type=jnp.float32)
    return (grad_w, grad_b, grad_joined[:, :width] + grad_table[:nodes] + scattered)


def plain_shampoo(grad, weight, left, left_root, right, right_root, part, right_split):
    count = left.shape[0]
    grad_rows = lax.dynamic_slice_in_dim(grad, part * count, count, 0)
    weight_rows = lax.dynamic_slice_in_dim(weight, part * count, count, 0)
    new_left = decay * left + (1.0 - decay) * jnp.dot(grad_rows, grad.T, precision=highest)
    if right_split:
        cols = right.shape[0]
        grad_cols = lax.dynamic_slice_in_dim(grad, part * cols, cols, 1)
        new_right = decay * right + (1.0 - decay) * jnp.dot(grad_cols.T, grad, precision=highest)
    else:
        new_right = decay * right + (1.0 - decay) * jnp.dot(grad.T, grad, precision=highest)
    step = jnp.dot(jnp.dot(left_root, grad, precision=highest), right_root, precision=highest)
    return (grad_rows, new_left, new_right, weight_rows - shampoo_rate * step)


def plain_shards(
    features,
    nbr_index,
    nbr_mask,
    send_rows,
    send_count,
    labels,
    seed_mask,
    w_first,
    w_rest,
    w_head,
    biases,
    stat_big,
    root_big,
    stat_mid,
    root_mid,
    stat_sq,
    root_sq,
    stat_hr,
    root_hr,
    bias_m,
    bias_v,
):
    hidden = w_rest.shape[2]
    peers = send_rows.shape[2]
    cap = send_rows.shape[3]
    send_list = send_rows.reshape(-1)
    valid = (jnp.arange(cap)[None, :] < send_count.reshape(peers, 1)).astype(jnp.bfloat16)
    weights = [w_first, w_rest[0], w_rest[1]]
    state = features[0].astype(jnp.float32)
    kept = []
    for level in range(3):
        state, saved = plain_forward(
            state,
            weights[level],
            biases[level * hidden : (level + 1) * hidden],
            nbr_index[0, level],
            nbr_mask[0, level],
            send_list,
            valid,
        )
        kept.append(saved)
    seeds = labels.shape[1]
    top = state[:seeds].astype(jnp.bfloat16)
    head_low_w = w_head.astype(jnp.bfloat16)
    logits = jnp.dot(top, head_low_w, preferred_element_type=jnp.float32) + biases[3 * hidden :]
    lse = jax.nn.logsumexp(logits, axis=1)
    onehot = (labels[0][:, None] == jnp.arange(logits.shape[1])[None, :]).astype(jnp.float32)
    picked = jnp.sum(logits * onehot, axis=1)
    seed_weight = seed_mask[0].astype(jnp.float32)
    loss_sum, seed_total = lax.psum(
        (jnp.sum((lse - picked) * seed_weight), jnp.sum(seed_weight)), ("dom", "rep")
    )
    grad_logits = (
        (jnp.exp(logits - lse[:, None]) - onehot) * (seed_weight / seed_total)[:, None]
    ).astype(jnp.bfloat16)
    grad_head = jnp.einsum("sh,sc->hc", top, grad_logits, preferred_element_type=jnp.float32)
    grad_hbias = jnp.sum(grad_logits.astype(jnp.float32), axis=0)
    grad_head, grad_hbias = (grad_head, grad_hbias)
    grad_top = jnp.einsum("sc,hc->sh", grad_logits, head_low_w, preferred_element_type=jnp.float32)
    grad_state = jnp.zeros(state.shape, jnp.float32).at[:seeds].set(grad_top)
    results = [None, None, None]
    for level in (2, 1, 0):
        grad_w, grad_b, grad_state = plain_backward(
            grad_state, weights[level], kept[level], send_list, valid, level > 0
        )
        results[level] = (grad_w, grad_b)
    grad_bias = jnp.concatenate([results[0][1], results[1][1], results[2][1], grad_hbias])
    grad_one, grad_two, grad_three = (results[0][0], results[1][0], results[2][0])
    grad_one, grad_two, grad_three, grad_head, grad_bias = lax.psum(
        (grad_one, grad_two, grad_three, grad_head, grad_bias), ("dom", "rep")
    )
    everything = (grad_one, grad_two, grad_three, grad_head, grad_bias)
    grad_norm = jnp.sqrt(sum((jnp.sum(g * g) for g in everything)))
    factor = clip_limit / jnp.maximum(grad_norm, clip_limit)
    grad_one, grad_two, grad_three, grad_head, grad_bias = [g * factor for g in everything]
    part = lax.axis_index("rep")
    head_rows = stat_sq.shape[1]
    head_root_rows = lax.dynamic_slice_in_dim(root_sq[3], part * head_rows, head_rows, 0)
    g_first, l_first, r_first, n_first = plain_shampoo(
        grad_one, w_first, stat_big, root_big, stat_sq[0], root_sq[0], part, True
    )
    g_mid0, l_mid0, r_mid0, n_mid0 = plain_shampoo(
        grad_two, w_rest[0], stat_mid[0], root_mid[0], stat_sq[1], root_sq[1], part, True
    )
    g_mid1, l_mid1, r_mid1, n_mid1 = plain_shampoo(
        grad_three, w_rest[1], stat_mid[1], root_mid[1], stat_sq[2], root_sq[2], part, True
    )
    g_head, l_head, r_head, n_head = plain_shampoo(
        grad_head, w_head, stat_sq[3], head_root_rows, stat_hr, root_hr, part, False
    )
    new_m = beta_one * bias_m + (1.0 - beta_one) * grad_bias
    new_v = beta_two * bias_v + (1.0 - beta_two) * grad_bias * grad_bias
    m_hat = new_m / (1.0 - beta_one**STEP)
    v_hat = new_v / (1.0 - beta_two**STEP)
    new_b = biases - bias_rate * (m_hat / (jnp.sqrt(v_hat) + adam_eps) + weight_decay * biases)
    new_rest = jnp.stack([n_mid0, n_mid1])
    return (
        loss_sum,
        seed_total,
        grad_norm,
        g_first,
        jnp.stack([g_mid0, g_mid1]),
        g_head,
        new_m,
        new_v,
        l_first,
        jnp.stack([l_mid0, l_mid1]),
        jnp.stack([r_first, r_mid0, r_mid1, l_head]),
        r_head,
        n_first,
        new_rest,
        n_head,
        new_b,
        n_first.astype(jnp.bfloat16),
        new_rest.astype(jnp.bfloat16),
        n_head.astype(jnp.bfloat16),
    )


def solution(mesh):
    placed = (
        P("rep", "dom", None),
        P("rep", None, "dom", None),
        P("rep", None, "dom", None),
        P("rep", "dom", None, None),
        P("rep", "dom", None),
        P("rep", "dom"),
        P("rep", "dom"),
        P(), P(), P(), P(),
        P("rep", None),
        P("rep", None),
        P(None, "rep", None),
        P(None, "rep", None),
        P(None, "rep", None),
        P(), P(), P(), P(), P(),
    )
    small = mesh.shape["rep"] == 4 and mesh.shape["dom"] == 8
    return jax.shard_map(
        shards if small else plain_shards,
        mesh=mesh,
        in_specs=placed,
        out_specs=(
            P(), P(), P(),
            P("rep", None), P(None, "rep", None), P("rep", None),
            P(), P(),
            P("rep", None), P(None, "rep", None), P(None, "rep", None), P(),
            P("rep", None), P(None, "rep", None), P("rep", None), P(),
            P("rep", None), P(None, "rep", None), P("rep", None),
        ),
        check_vma=False,
    )
```

```python
import functools

import jax
import jax.numpy as jnp
from jax import lax
from jax.experimental import pallas as pl
from jax.experimental.pallas import tpu as pltpu
from jax.sharding import PartitionSpec as P

STEP = 5
FAN_REST = 10

clip_limit = 0.0001
decay = 0.5
shampoo_rate = 1.0
beta_one = 0.9
beta_two = 0.999
bias_rate = 0.05
weight_decay = 0.01
adam_eps = 1e-08
norm_eps = 1e-06
MASKED = 8192

bf16 = jnp.bfloat16
f32 = jnp.float32
i32 = jnp.int32
MESH = pl.DeviceIdType.MESH


def nn(a, b):
    return jnp.dot(a, b, preferred_element_type=f32)


def nt(a, b):
    return lax.dot_general(a, b, (((1,), (1,)), ((), ())), preferred_element_type=f32)


def flip(a):
    return a.astype(f32).T.astype(a.dtype)


def round_up(a, b):
    return (a + b - 1) // b * b


def gelu(z):
    scale = 0.7978845608028654
    return z * (0.5 + 0.5 * jnp.tanh(z * (scale + (0.044715 * scale) * (z * z))))


def gelu_slope(z):
    scale = 0.7978845608028654
    square = z * z
    half = 0.5 + 0.5 * jnp.tanh(z * (scale + (0.044715 * scale) * square))
    return half + (half - half * half) * (z * (2.0 * scale + (6.0 * 0.044715 * scale) * square))


def norm_root(act, axis):
    return lax.rsqrt(jnp.sum(act * act, axis=axis, keepdims=True) + norm_eps)


def pull_back(act, slope, root, grad, axis):
    dot = jnp.sum(act * grad, axis=axis, keepdims=True)
    return (slope * (root * grad - act * (root * root * root * dot))).astype(bf16)


def as_column(row):
    return jnp.broadcast_to(row, (8, row.shape[1])).T[:, 0:1]


def widen(row, width, value=0):
    return jnp.concatenate([row, jnp.full((1, width - row.shape[1]), value, row.dtype)], axis=1)


def split_dot(a, b):
    high = a.astype(bf16)
    low = (a - high.astype(f32)).astype(bf16)
    return nn(high, b) + nn(low, b)


def three_dot(a, b):
    high = b.astype(bf16)
    low = (b - high.astype(f32)).astype(bf16)
    return split_dot(a, high) + nn(a.astype(bf16), low)


def graph_kernel(
    peers, cap, seeds, fan,
    nbr_hbm, msk_hbm, xt_hbm, w1_hbm, wr_hbm, srow_hbm, scnt_hbm, lab_hbm, smask_hbm, wht_hbm, bias_hbm,
    rtm_hbm, rts_hbm,
    g_out, s_out, left_out, right_out, move_out, square_out, w1_out, wr_out,
    rtm, rts, full,
    nbr, msk, xt, srow, scnt, lab, smask, wht, bias, joined, near, chosen, far2, far2t, grad1, ctmp, crow, lrow, lcode, crow2, lrow2, rdeg,
    w1, wr, w1t, act1, slope1, root1, h1t, ob0, ib0, ob1, ib1, ob2, ib2, ob3, ib3, ob4, ib4, ob5, ib5,
    gl, acc, rc, sbq, rbq, sbz, rbz, gout, ssend, srecv, sqv, szv,
    load_sem, send_sem, recv_sem, red_send, red_recv,
):
    fin, nodes = xt.shape
    hidden = w1.shape[1]
    finp = round_up(fin, 16)
    slots = peers * cap
    table = nodes + slots
    groups = table // 128
    chunks = nodes // 128
    blocks = nodes // 256
    span = far2.shape[0]
    local = span - slots
    me = lax.axis_index("dom")
    rep = lax.axis_index("rep")
    core = lax.rem(rep, 2)
    xpos = rep // 2
    ypos = lax.rem(me, 2)
    zpos = me // 2
    nz = peers // 2
    mate_c = xpos * 2 + (1 - core)
    mate_x = (1 - xpos) * 2 + core
    mate_y = zpos * 2 + (1 - ypos)

    loads = [
        pltpu.make_async_copy(src, dst, load_sem.at[k])
        for k, (src, dst) in enumerate(
            (
                (srow_hbm, srow), (scnt_hbm, scnt), (xt_hbm, xt), (nbr_hbm, nbr), (msk_hbm, msk),
                (w1_hbm, w1), (wr_hbm, wr), (lab_hbm, lab), (smask_hbm, smask), (wht_hbm, wht), (bias_hbm, bias),
                (rtm_hbm, rtm), (rts_hbm, rts),
            )
        )
    ]
    for load in loads:
        load.start()
    barrier = pltpu.get_barrier_semaphore()
    for off in range(1, peers):
        pl.semaphore_signal(barrier, inc=1, device_id={"dom": lax.rem(me + off, peers)}, device_id_type=MESH)
    for mate in (mate_c, mate_x):
        pl.semaphore_signal(barrier, inc=1, device_id={"rep": mate}, device_id_type=MESH)
    mate_xy = {"dom": mate_y, "rep": mate_x}
    pl.semaphore_signal(barrier, inc=1, device_id=mate_xy, device_id_type=MESH)

    def exchange(stage, src, dst, same=False):
        size = dst.shape[0] // peers
        copies = []
        for off in range(1, peers):
            peer = lax.rem(me + off, peers)
            copies.append(
                pltpu.make_async_remote_copy(
                    src_ref=src if same else src.at[pl.ds(pl.multiple_of(peer * size, 16), size)],
                    dst_ref=dst.at[pl.ds(pl.multiple_of(me * size, 16), size)],
                    send_sem=send_sem.at[stage, off - 1],
                    recv_sem=recv_sem.at[stage, off - 1],
                    device_id={"dom": peer},
                    device_id_type=MESH,
                )
            )
        for c in copies:
            c.start()
        return copies

    started = []

    def finish(copies):
        for c in copies:
            c.wait_recv()
        started.extend(copies)

    loads[0].wait()
    loads[1].wait()
    count = jnp.broadcast_to(scnt[...], (peers, peers))
    count = jnp.where(
        lax.broadcasted_iota(i32, (peers, peers), 0) == lax.broadcasted_iota(i32, (peers, peers), 1), count, 0
    )
    count = jnp.sum(count.astype(f32), axis=1, keepdims=True)
    in_use = lax.broadcasted_iota(i32, (peers, cap), 1).astype(f32) < count
    slot = jnp.where(in_use, srow[...].astype(f32), -1.0)
    per = 128 // cap
    slot = jnp.concatenate([slot] * per, axis=1)
    owner = lax.broadcasted_iota(i32, (peers, 128), 0)
    place = lax.broadcasted_iota(i32, (peers, 128), 1) // cap
    send_row = jnp.concatenate(
        [
            jnp.sum(jnp.where(owner == place + t * per, slot, 0.0), axis=0, keepdims=True)
            for t in range(slots // 128)
        ],
        axis=1,
    )
    node_id = lax.broadcasted_iota(i32, (256, nodes), 1).astype(f32)
    send_col = as_column(send_row)
    for r in range(0, slots, 256):
        chosen[r : r + 256, :] = jnp.where(send_col[r : r + 256] == node_id, 1.0, 0.0).astype(bf16)
    line = lax.broadcasted_iota(i32, (16, nodes), 0)
    joined[finp - 16 : finp, :] = jnp.where(line == 16 - (finp - fin), 1.0, 0.0).astype(bf16)
    r_id = lax.broadcasted_iota(i32, (2 * seeds, local), 0)
    l_id = lax.broadcasted_iota(i32, (2 * seeds, local), 1)
    is_self = (r_id < seeds) & (l_id == r_id + FAN_REST * seeds)
    is_nbr = (r_id >= seeds) & (l_id < FAN_REST * seeds) & (lax.rem(l_id, seeds) == r_id - seeds)
    spread = jnp.where(is_self | is_nbr, 1.0, 0.0)
    spread_t = spread.T.astype(bf16)
    spread = spread.astype(bf16)
    loads[2].wait()
    joined[0:fin, :] = xt[...]
    ob0[:, finp:] = jnp.zeros((slots, ob0.shape[1] - finp), bf16)
    ob0[:, 0:finp] = nt(chosen[0:slots, :], joined[0:finp, :]).astype(bf16)
    for buf in (ib0, ib1, ib2, ib3, ib4, ib5):
        size = buf.shape[0] // peers
        buf[pl.ds(pl.multiple_of(me * size, 16), size), :] = jnp.zeros((size, buf.shape[1]), bf16)
    pl.semaphore_wait(barrier, peers - 1 + 3)
    sent = exchange(0, ob0, ib0)

    loads[3].wait()
    loads[4].wait()

    def codes(level, size, here):
        at = slice(0, size)
        return jnp.where(msk[level, at, 0, here] == 1, nbr[level, at, 0, here], MASKED).astype(f32)

    code3 = codes(2, FAN_REST, slice(0, 128))
    code3t = jnp.concatenate([code3, jnp.full((16 - FAN_REST, 128), float(MASKED), f32)], axis=0).T[0:seeds]
    degree = jnp.sum(jnp.where(code3t < float(MASKED), 1.0, 0.0), axis=1, keepdims=True)
    rdeg3 = 1.0 / jnp.maximum(degree, 1.0)
    tiled = jnp.concatenate([code3t] * peers, axis=0)
    r_id = lax.broadcasted_iota(i32, (peers * seeds, 128), 0)
    l_id = lax.broadcasted_iota(i32, (peers * seeds, 128), 1)
    wanted = jnp.where(l_id < cap, nodes + (r_id // seeds) * cap + l_id, -1).astype(f32)
    far3 = jnp.zeros(wanted.shape, f32)
    for k in range(FAN_REST):
        far3 = far3 + jnp.where(wanted == tiled[:, k : k + 1], 1.0, 0.0)
    ob5[...] = far3.astype(bf16)
    sent_far = exchange(5, ob5, ib5)

    fill = jnp.full((32 - fan, 128), float(MASKED), f32)
    fill2 = jnp.full((16 - FAN_REST, 128), float(MASKED), f32)
    for c in range(chunks):
        here = slice(c * 128, (c + 1) * 128)
        code = codes(0, fan, here)
        degree = jnp.sum((code < MASKED).astype(f32), axis=0, keepdims=True)
        rdeg[0:1, here] = 1.0 / jnp.maximum(degree, 1.0)
        code2 = jnp.concatenate([codes(1, FAN_REST, here), fill2], axis=0).astype(i32)
        ctmp[here, 0:64] = jnp.concatenate(
            [code, fill, (code2 >> 7).astype(f32), (code2 & 127).astype(f32)], axis=0
        ).T

    def grouped(source, count, width):
        each = 256 // width
        lane = lax.broadcasted_iota(i32, (count, 256), 1) // width
        code = jnp.zeros((count, 256), f32)
        for n in range(each):
            piece = source[pl.ds(n, count, stride=each), :]
            piece = jnp.concatenate([piece, piece], axis=1)
            piece = pltpu.roll(piece, n * width, 1) if n else piece
            code = jnp.where(lane == n, piece, code)
        code = code.astype(i32)
        return ((code >> 7) * each + lane).astype(f32), (code & 127).astype(f32)

    crow[...], lrow[...] = grouped(ctmp, nodes // 8, 32)

    lane = lax.broadcasted_iota(i32, (1, 128), 1)
    fits = 128 // seeds
    tiles = []
    for t in range(local // 128):
        tile = jnp.full((1, 128), -1.0, f32)
        for j in range(fits):
            k = t * fits + j
            here = lane // seeds == j
            if k < FAN_REST:
                piece = code3[k : k + 1, :]
                piece = pltpu.roll(piece, j * seeds, 1) if j else piece
                tile = jnp.where(here & (piece < nodes), piece, tile)
            elif k == FAN_REST:
                tile = jnp.where(here, (lane - j * seeds).astype(f32), tile)
        tiles.append(tile)
    local_col = as_column(jnp.concatenate(tiles, axis=1))
    for r in range(0, local, 256):
        chosen[slots + r : slots + r + 256, :] = jnp.where(
            local_col[r : r + 256] == node_id, 1.0, 0.0
        ).astype(bf16)
    keep = jnp.where(jnp.concatenate([send_col, local_col], axis=0) >= 0.0, 1.0, 0.0)
    found = nn(chosen[0:span, :], ctmp[...].astype(bf16))
    lcode[...] = pltpu.roll(found, 96, 1) * 128.0 + pltpu.roll(found, 80, 1)
    lane = lax.broadcasted_iota(i32, (span, 128), 1)
    degree = jnp.sum(
        jnp.where((lcode[...] < float(MASKED)) & (lane < FAN_REST), 1.0, 0.0), axis=1, keepdims=True
    )
    rdeg2 = 1.0 / jnp.maximum(degree, 1.0)
    crow2[...], lrow2[...] = grouped(lcode, span // 16, 16)

    rows_a = lax.broadcasted_iota(i32, (groups * 8, 256), 0).astype(f32)
    rows_b = lax.broadcasted_iota(i32, (128, 256), 0).astype(f32)
    rows_c = lax.broadcasted_iota(i32, (groups * 16, 256), 0).astype(f32)

    def list_counts(b, _):
        for p in range(16):
            g = b * 16 + p
            left = jnp.where(rows_c == crow2[pl.ds(g, 1), :], 1.0, 0.0).astype(bf16)
            right = jnp.where(rows_b == lrow2[pl.ds(g, 1), :], 1.0, 0.0).astype(bf16)
            value = nt(left, right).astype(bf16)
            for a in range(groups):
                tile = value[a * 16 : (a + 1) * 16]
                if a < chunks:
                    chosen[pl.ds(pl.multiple_of(span + g * 16, 16), 16), a * 128 : (a + 1) * 128] = tile
                else:
                    at = pl.ds(pl.multiple_of(g * 16, 16), 16)
                    far2[at, (a - chunks) * 128 : (a - chunks + 1) * 128] = tile
        return 0

    lax.fori_loop(0, span // 256, list_counts, 0)

    def build(b, _):
        for p in range(16):
            pair = []
            for half in range(2):
                g = b * 32 + p * 2 + half
                left = jnp.where(rows_a == crow[pl.ds(g, 1), :], 1.0, 0.0).astype(bf16)
                right = jnp.where(rows_b == lrow[pl.ds(g, 1), :], 1.0, 0.0).astype(bf16)
                pair.append(nt(left, right))
            at = pl.ds(pl.multiple_of(b * 256 + p * 16, 16), 16)
            for a in range(groups):
                tile = jnp.concatenate([pair[0][a * 8 : (a + 1) * 8], pair[1][a * 8 : (a + 1) * 8]], axis=0)
                near[at, a * 128 : (a + 1) * 128] = tile.astype(bf16)
        return 0

    lax.fori_loop(0, blocks, build, 0, unroll=2)

    for load in loads[5:]:
        load.wait()
    bias = bias[...].reshape(1, bias.shape[0])
    wpad = jnp.concatenate(
        [w1[0:fin, :], jnp.zeros((finp - fin, hidden), f32), w1[fin : 2 * fin, :], jnp.zeros((finp - fin, hidden), f32)],
        axis=0,
    )
    w1t[...] = wpad.T.astype(bf16)
    b1 = as_column(bias[0:1, 0:hidden])

    finish(sent)
    ibt = flip(ib0[...])[0:finp, :]

    def block(b):
        return pl.ds(b * 256 if isinstance(b, int) else pl.multiple_of(b * 256, 256), 256)

    def gather(b):
        blk = block(b)
        total = nt(joined[0:finp, :], near[blk, 0:nodes]) + nt(ibt, near[blk, nodes:])
        joined[finp:, blk] = (total * rdeg[0:1, blk]).astype(bf16)

    def product(b):
        blk = block(b)
        grad1[:, blk] = nn(w1t[...], joined[:, blk]) + b1

    def activate(b):
        blk = block(b)
        z = grad1[:, blk]
        act = gelu(z)
        root = norm_root(act, 0)
        act1[:, blk] = act
        root1[0:1, blk] = root
        h1t[:, blk] = (act * root).astype(bf16)

    gather(0)
    far2t[...] = flip(far2[...])
    w2 = wr[0].astype(bf16)
    w3 = wr[1].astype(bf16)
    product(0)
    gather(1)

    def layer_one(b, _):
        activate(b - 2)
        product(b - 1)
        gather(b)
        return 0

    lax.fori_loop(2, blocks, layer_one, 0)
    activate(blocks - 2)
    product(blocks - 1)
    activate(blocks - 1)
    sent_rows = nt(chosen[0:slots, :], h1t[...]).astype(bf16)
    ob1[...] = sent_rows
    sent = exchange(1, ob1, ib1)

    own2 = nt(chosen[slots:, :], h1t[...])

    def slopes(b, _):
        blk = block(b)
        slope1[:, blk] = gelu_slope(grad1[:, blk])
        return 0

    lax.fori_loop(0, blocks, slopes, 0, unroll=2)
    first_rows = w1_out.shape[0]
    for i in range(2 * fin // first_rows):

        @pl.when(rep == i)
        def _():
            w1_out[...] = w1[i * first_rows : (i + 1) * first_rows, :]

    rest_rows = wr_out.shape[1]
    for i in range(2):
        wr_out[i] = wr[i, pl.ds(pl.multiple_of(rep * rest_rows, 8), rest_rows), :]
    b2 = bias[0:1, hidden : 2 * hidden]
    self_local = own2[0:local].astype(bf16)
    z_sent = nn(sent_rows, w2[0:hidden]) + b2
    z_local = nn(self_local, w2[0:hidden]) + b2
    finish(sent_far)
    far3r = ib5[...].astype(f32)[:, 0:cap]
    spots = peers * cap
    r_id = lax.broadcasted_iota(i32, (peers * seeds, spots), 0) // seeds
    l_id = lax.broadcasted_iota(i32, (peers * seeds, spots), 1) // cap
    collect = jnp.where(r_id == l_id, jnp.concatenate([far3r] * peers, axis=1), 0.0)
    scatter = collect.T.astype(bf16)
    collect = collect.astype(bf16)

    finish(sent)

    def rows_two(own_self, own_z, own_sum, at):
        agg = ((own_sum + nn(far2[at, :], ib1[...])) * rdeg2[at]).astype(bf16)
        z = own_z + nn(agg, w2[hidden:])
        act = gelu(z)
        root = norm_root(act, 1)
        return jnp.concatenate([own_self, agg], axis=1), z, act, root, (act * (root * keep[at])).astype(bf16)

    out_at, in_at = slice(0, slots), slice(slots, span)
    joined2a, z2a, act2a, root2a, h2a = rows_two(sent_rows, z_sent, own2[local:span], out_at)
    ob2[...] = nn(collect, h2a).astype(bf16)
    sent = exchange(2, ob2, ib2)

    joined2b, z2b, act2b, root2b, h2b = rows_two(self_local, z_local, own2[span:], in_at)
    near3 = nn(spread, h2b)
    self3 = near3[0:seeds].astype(bf16)
    z_seeds = nn(self3, w3[0:hidden]) + bias[0:1, 2 * hidden : 3 * hidden]
    slope2b = gelu_slope(z2b)
    classes = wht.shape[0]
    classp = round_up(classes, 16)
    wht_low = jnp.concatenate([wht[...], jnp.zeros((classp - classes, hidden), f32)], axis=0).astype(bf16)
    bh = widen(bias[0:1, 3 * hidden : 3 * hidden + classes], classp)
    class_id = lax.broadcasted_iota(i32, (seeds, classp), 1)
    label = as_column(widen(lab[...].astype(f32), 128))[0:seeds]
    hot = jnp.where(class_id.astype(f32) == label, 1.0, 0.0)
    weight = as_column(widen(smask[...].astype(f32), 128))[0:seeds]
    finish(sent)
    total = near3[seeds:]
    for q in range(peers):
        total = total + ib2[q * seeds : (q + 1) * seeds, :].astype(f32)
    agg3 = (total * rdeg3).astype(bf16)
    z3 = z_seeds + nn(agg3, w3[hidden:])
    joined3 = jnp.concatenate([self3, agg3], axis=1)
    act3 = gelu(z3)
    slope3 = gelu_slope(z3)
    root3 = norm_root(act3, 1)
    top = (act3 * root3).astype(bf16)

    logits = nt(top, wht_low) + bh
    logits = jnp.where(class_id < classes, logits, -1e30)
    peak = jnp.max(logits, axis=1, keepdims=True)
    lse = peak + jnp.log(jnp.sum(jnp.exp(logits - peak), axis=1, keepdims=True))
    dlog = ((jnp.exp(logits - lse) - hot) * weight).astype(bf16)
    dtop = nn(dlog, wht_low)

    dz3 = pull_back(act3, slope3, root3, dtop, 1)
    dg3 = (nt(dz3, w3[hidden:]) * rdeg3).astype(bf16)
    ob3[...] = dg3
    sent = exchange(3, ob3, ib3, same=True)
    ds3 = nt(dz3, w3[0:hidden]).astype(bf16)
    dloc = nn(spread_t, jnp.concatenate([ds3, dg3], axis=0))

    seg_a = 4 * hidden
    row_head = seg_a + 2 * finp
    row_bias = row_head + classp
    rows = gl.shape[1]

    def put(row, value):
        size = value.shape[0]
        gl[0, row : row + size, :] = value[:, 0:128].astype(bf16)
        gl[1, row : row + size, :] = value[:, 128:].astype(bf16)

    picked = jnp.sum(logits * hot, axis=1, keepdims=True)
    loss = jnp.sum((lse - picked) * weight, axis=0, keepdims=True)
    total = jnp.sum(weight, axis=0, keepdims=True)
    sc_lane = lax.broadcasted_iota(i32, (8, 128), 1)
    ssend[0] = jnp.where(sc_lane == 0, loss, jnp.where(sc_lane == 1, total, 0.0))
    dz2b = pull_back(act2b, slope2b, root2b, dloc * keep[in_at], 1)
    dj2b = nt(dz2b, w2)
    dg2b = (dj2b[:, hidden:] * rdeg2[in_at]).astype(bf16)
    near_ret = nn(far2t[:, in_at], dg2b)
    slope2a = gelu_slope(z2a)
    put(row_head, nn(dlog.astype(f32).T.astype(bf16), top))
    put(2 * hidden, nn(joined3.astype(f32).T.astype(bf16), dz3))
    bias_3 = jnp.sum(dz3.astype(f32), axis=0, keepdims=True)
    bias_h = widen(jnp.sum(dlog.astype(f32), axis=0, keepdims=True), hidden)
    finish(sent)

    dh2a = nn(scatter, ib3[...]) * keep[out_at]
    dz2a = pull_back(act2a, slope2a, root2a, dh2a, 1)
    dg2a = (nt(dz2a, w2[hidden:]) * rdeg2[out_at]).astype(bf16)
    ob4[...] = (near_ret + nn(far2t[:, out_at], dg2a)).astype(bf16)
    sent = exchange(4, ob4, ib4)
    put(0, nn(flip(joined2a), dz2a) + nn(flip(joined2b), dz2b))

    used = []

    def hop(src, dst, who):
        used.append(0)
        k = len(used) - 1
        copy = pltpu.make_async_remote_copy(
            src_ref=src, dst_ref=dst, send_sem=red_send.at[k], recv_sem=red_recv.at[k],
            device_id=who, device_id_type=MESH,
        )
        copy.start()
        return copy

    def rows_of(start, size):
        return pl.ds(pl.multiple_of(start, 16), size)

    to_core = {"rep": mate_c}
    plane = (
        xpos * 2 + ypos,
        (
            ((1 - xpos) * 2 + ypos, {"rep": mate_x}),
            (xpos * 2 + 1 - ypos, {"dom": mate_y}),
            ((1 - xpos) * 2 + 1 - ypos, mate_xy),
        ),
    )
    others = [lax.rem(zpos + off, nz) for off in range(1, nz)]
    column = (zpos, tuple((to, {"dom": to * 2 + ypos}) for to in others))

    def summing(start, size, out_sem, one, two):
        (mine1, group1), (mine2, group2) = one, two
        quarter = size // (len(group1) + 1)
        piece = quarter // (len(group2) + 1)
        whole = slice(start, start + size)
        at1, at2 = start // 4, start // (4 * nz)
        at1, at2 = slice(at1, at1 + quarter), slice(at2, at2 + piece)
        kept = rows_of(start + mine1 * quarter, quarter)
        here = rows_of(start + mine1 * quarter + mine2 * piece, piece)
        copies = [hop(gl.at[1 - core, whole], rc.at[whole], to_core)]
        yield
        finish(copies)
        value = gl[core, whole, :].astype(f32) + rc[whole, :].astype(f32)
        acc[whole, :] = value
        sbq[whole, :] = value.astype(bf16)
        copies = [
            hop(sbq.at[rows_of(start + to * quarter, quarter)], rbq.at[k, at1], who)
            for k, (to, who) in enumerate(group1)
        ]
        yield
        finish(copies)
        value = acc[kept, :]
        for k in range(len(group1)):
            value = value + rbq[k, at1, :].astype(f32)
        acc[kept, :] = value
        sbz[at1, :] = value.astype(bf16)
        copies = [
            hop(sbz.at[rows_of(start // 4 + to * piece, piece)], rbz.at[k, at2], who)
            for k, (to, who) in enumerate(group2)
        ]
        yield
        finish(copies)
        value = acc[here, :]
        for k in range(len(group2)):
            value = value + rbz[k, at2, :].astype(f32)
        gout[core, here, :] = value.astype(bf16)
        part = gout.at[core, here]
        copies = [hop(part, part, who) for _, who in group2]
        yield
        finish(copies)
        part = gout.at[core, kept]
        copies = [hop(part, part, who) for _, who in group1]
        copies.append(hop(part, part, to_core))
        yield
        finish(copies)
        copies = []
        for to, _ in group1:
            part = gout.at[core, rows_of(start + to * quarter, quarter)]
            copies.append(hop(part, part, to_core))
        out = [
            pltpu.make_async_copy(gout.at[h, whole], g_out.at[h, whole], load_sem.at[out_sem + k])
            for k, h in enumerate((core, 1 - core))
        ]
        out[0].start()
        yield
        finish(copies)
        out[1].start()
        yield
        for c in out:
            c.wait()

    def summing_scalars():
        copies = [hop(ssend.at[0], srecv.at[0], to_core)]
        yield
        finish(copies)
        ssend[1] = ssend[0] + srecv[0]
        mine = plane[0]
        sqv[mine] = ssend[1]
        copies = [hop(ssend.at[1], sqv.at[mine], who) for _, who in plane[1]]
        yield
        finish(copies)
        ssend[2] = sqv[0] + sqv[1] + sqv[2] + sqv[3]
        szv[zpos] = ssend[2]
        copies = [hop(ssend.at[2], szv.at[zpos], who) for _, who in column[1]]
        yield
        finish(copies)
        total = szv[0]
        for k in range(1, nz):
            total = total + szv[k]
        s_out[...] = total

    def go_on(*runs):
        for run in runs:
            next(run, None)

    cut = seg_a + 2 * (4 * nz * 16)
    rest = summing(0, seg_a, 4, plane, column)
    first = summing(seg_a, cut - seg_a, 0, column, plane)
    second = summing(cut, rows - cut, 2, plane, column)
    scalars = summing_scalars()
    go_on(rest, scalars)

    bias_2 = jnp.sum(dz2a.astype(f32), axis=0, keepdims=True) + jnp.sum(dz2b.astype(f32), axis=0, keepdims=True)
    line = lax.broadcasted_iota(i32, (16, hidden), 0)
    put(
        row_bias,
        jnp.where(line == 1, bias_2, 0.0) + jnp.where(line == 2, bias_3, 0.0) + jnp.where(line == 3, bias_h, 0.0),
    )
    both = flip(
        jnp.concatenate(
            [nt(dz2a, w2[0:hidden]).astype(bf16), dj2b[:, 0:hidden].astype(bf16), dg2a, dg2b], axis=0
        )
    )
    grad1[...] = nn(both, chosen[...])
    go_on(rest, scalars)
    finish(sent)
    back = flip(ib4[...])

    def layer_one_back(b, _):
        blk = block(b)
        grad = grad1[:, blk] + nn(back, chosen[0:slots, blk])
        h1t[:, blk] = pull_back(act1[:, blk], slope1[:, blk], root1[0:1, blk], grad, 0)
        return 0

    lax.fori_loop(0, blocks, layer_one_back, 0, unroll=2)
    size = cut - seg_a
    put(seg_a, nt(joined[0:size, :], h1t[...]))
    go_on(first, rest, scalars)
    put(cut, nt(joined[size:, :], h1t[...]))
    go_on(second, first)
    def rest_products():
        count = rtm.shape[1]
        cols = right_out.shape[1]
        square = jnp.zeros((1, hidden), f32)
        for i in range(2):
            whole = slice(i * 2 * hidden, (i + 1) * 2 * hidden)
            g = jnp.concatenate([gout[0, whole, :], gout[1, whole, :]], axis=1)
            mine = rows_of(i * 2 * hidden + rep * count, count)
            g_rows = jnp.concatenate([gout[0, mine, :], gout[1, mine, :]], axis=1)
            left_out[i] = nt(g_rows, g)
            full[i] = nn(flip(g), g)
            right_out[i] = full[i, pl.ds(pl.multiple_of(rep * cols, 8), cols), :]
            move_out[i] = three_dot(split_dot(rtm[i], g), rts[1 + i])
            wide = g.astype(f32)
            square = square + jnp.sum(wide * wide, axis=0, keepdims=True)
        square_out[...] = square

    for turn in range(5):
        go_on(second, rest, first, scalars)
        if turn == 3:
            rest_products()
    go_on(second, first)
    go_on(second)
    for c in started:
        c.wait_send()


def in_hbm(*arrays):
    return [pltpu.with_memory_space_constraint(a, pltpu.HBM) for a in arrays]


def summed_gradients(peers, cap, seeds, fan, nbr, msk, xt, w1, wr, srow, scnt, lab, smask, wht, bias, rtm, rts):
    fin, nodes = xt.shape
    hidden = w1.shape[1]
    finp = round_up(fin, 16)
    wide = round_up(fin, 128)
    slots = peers * cap
    span = slots + round_up(seeds * (FAN_REST + 1), 256)
    classp = round_up(wht.shape[0], 16)
    rows = 4 * hidden + 2 * finp + classp + 16
    nz = peers // 2
    vmem = pltpu.VMEM
    sems = 64
    some = peers * seeds
    count, cols = rtm.shape[1], hidden // (2 * hidden // rtm.shape[1])
    scratch = [
        vmem(rtm.shape, f32),
        vmem(rts.shape, f32),
        vmem((2, hidden, hidden), f32),
        vmem(nbr.shape, i32),
        vmem(msk.shape, i32),
        vmem(xt.shape, bf16),
        vmem(srow.shape, i32),
        vmem(scnt.shape, i32),
        vmem(lab.shape, i32),
        vmem(smask.shape, i32),
        vmem(wht.shape, f32),
        vmem(bias.shape, f32),
        vmem((2 * finp, nodes), bf16),
        vmem((nodes, nodes + slots), bf16),
        vmem((2 * span, nodes), bf16),
        vmem((span, slots), bf16),
        vmem((slots, span), bf16),
        vmem((hidden, nodes), f32),
        vmem((nodes, 128), f32),
        vmem((nodes // 8, 256), f32),
        vmem((nodes // 8, 256), f32),
        vmem((span, 128), f32),
        vmem((span // 16, 256), f32),
        vmem((span // 16, 256), f32),
        vmem((8, nodes), f32),
        vmem(w1.shape, f32),
        vmem(wr.shape, f32),
        vmem((hidden, 2 * finp), bf16),
        vmem((hidden, nodes), f32),
        vmem((hidden, nodes), f32),
        vmem((8, nodes), f32),
        vmem((hidden, nodes), bf16),
        vmem((slots, wide), bf16),
        vmem((slots, wide), bf16),
        vmem((slots, hidden), bf16),
        vmem((slots, hidden), bf16),
        vmem((some, hidden), bf16),
        vmem((some, hidden), bf16),
        vmem((seeds, hidden), bf16),
        vmem((some, hidden), bf16),
        vmem((slots, hidden), bf16),
        vmem((slots, hidden), bf16),
        vmem((some, 128), bf16),
        vmem((some, 128), bf16),
        vmem((2, rows, 128), bf16),
        vmem((rows, 128), f32),
        vmem((rows, 128), bf16),
        vmem((rows, 128), bf16),
        vmem((3, rows // 4, 128), bf16),
        vmem((rows // 4, 128), bf16),
        vmem((nz - 1, rows // (4 * nz), 128), bf16),
        vmem((2, rows, 128), bf16),
        vmem((4, 8, 128), f32),
        vmem((3, 8, 128), f32),
        vmem((4, 8, 128), f32),
        vmem((nz, 8, 128), f32),
        pltpu.SemaphoreType.DMA((13,)),
        pltpu.SemaphoreType.DMA((6, peers - 1)),
        pltpu.SemaphoreType.DMA((6, peers - 1)),
        pltpu.SemaphoreType.DMA((sems,)),
        pltpu.SemaphoreType.DMA((sems,)),
    ]
    inside = pl.BlockSpec(memory_space=vmem)
    outside = pl.BlockSpec(memory_space=pl.ANY)
    return pl.pallas_call(
        functools.partial(graph_kernel, peers, cap, seeds, fan),
        out_shape=(
            jax.ShapeDtypeStruct((2, rows, 128), bf16),
            jax.ShapeDtypeStruct((8, 128), f32),
            jax.ShapeDtypeStruct((2, count, 2 * hidden), f32),
            jax.ShapeDtypeStruct((2, cols, hidden), f32),
            jax.ShapeDtypeStruct((2, count, hidden), f32),
            jax.ShapeDtypeStruct((1, hidden), f32),
            jax.ShapeDtypeStruct((count * 2 * fin // (2 * hidden), hidden), f32),
            jax.ShapeDtypeStruct((2, count, hidden), f32),
        ),
        in_specs=[outside] * 13,
        out_specs=(outside,) + (inside,) * 7,
        scratch_shapes=scratch,
        compiler_params=pltpu.CompilerParams(
            collective_id=0, has_side_effects=True, vmem_limit_bytes=51 * 2**20
        ),
        cost_estimate=pl.CostEstimate(flops=24 * 10**9, bytes_accessed=12 * 2**20, transcendentals=2**20),
        name="graph_step",
    )(*in_hbm(nbr, msk, xt, w1, wr, srow, scnt, lab, smask, wht, bias, rtm, rts))


def update_kernel(
    fin,
    g_all, scalars, lefts, rights, moves, rest_square, w_mine, wr_mine, wht, bias, sth, rth, bm, bv,
    st1, rt1, stm, sts, rts,
    loss_o, total_o, norm_o, gh_o, m_o, v_o, lh_o, nh_o, nb_o, nh_low,
    g1_hbm, gr_hbm, l1_hbm, lm_hbm, ls_hbm, n1_hbm, nr_hbm, n1_low_hbm, nr_low_hbm,
    g1_o, gr_o, l1_o, lm_o, ls_o, n1_o, nr_o, n1_low, nr_low,
    g1, g_mine, full, gb, out_sem,
):
    hidden = w_mine.shape[1]
    classes = wht.shape[0]
    classp = round_up(classes, 16)
    finp = round_up(fin, 16)
    seg_a = 4 * hidden
    part = lax.axis_index("rep")

    stores = []

    def store(src, dst):
        copy = pltpu.make_async_copy(src, dst, out_sem.at[len(stores)])
        stores.append(copy)
        copy.start()

    def grads(start, size):
        return jnp.concatenate(
            [g_all[0, start : start + size, :], g_all[1, start : start + size, :]], axis=1
        )

    total = scalars[0:1, 1:2]
    square = jnp.zeros((16, hidden), f32)
    spare = lax.broadcasted_iota(i32, (16, hidden), 0) >= 16 - (finp - fin)
    for r in range(seg_a, g_all.shape[1], 16):
        g = grads(r, 16).astype(f32)
        if r == seg_a + 2 * finp - 16:
            g = jnp.where(spare, 0.0, g)
        square = square + g * g
    square = jnp.sum(jnp.sum(square, axis=0, keepdims=True) + rest_square[...], axis=1, keepdims=True)
    norm = jnp.sqrt(square) / total
    scale = clip_limit / jnp.maximum(norm, clip_limit) / total
    loss_o[...] = scalars[0:1, 0:1]
    total_o[...] = total
    norm_o[...] = norm
    lift = (1.0 - decay) * scale * scale
    move = shampoo_rate * scale

    g1[0:fin, :] = grads(seg_a, finp)[0:fin].astype(f32)
    g1[fin : 2 * fin, :] = grads(seg_a + finp, finp)[0:fin].astype(f32)
    count = st1.shape[0]
    g_low = g1[...].astype(bf16)
    full[0] = nn(g1[...].T.astype(bf16), g_low)
    half = split_dot(rt1[...], g_low)
    for i in range(2 * fin // count):

        @pl.when(part == i)
        def _():
            g_mine[...] = g1[i * count : (i + 1) * count, :]

    g_rows = g_mine[...]
    g1_o[...] = g_rows * scale
    store(g1_o, g1_hbm)
    fresh = w_mine[...] - move * three_dot(half, rts[0])
    n1_o[...] = fresh
    n1_low[...] = fresh.astype(bf16)
    store(n1_o, n1_hbm)
    store(n1_low, n1_low_hbm)
    product = nt(g_rows.astype(bf16), g_low)
    l1_o[...] = decay * st1[...] + lift * product
    store(l1_o, l1_hbm)

    count = stm.shape[1]
    for i in range(2):
        base = pl.ds(pl.multiple_of(i * 2 * hidden + part * count, 16), count)
        g_rows = jnp.concatenate([g_all[0, base, :], g_all[1, base, :]], axis=1)
        gr_o[i] = g_rows.astype(f32) * scale
        lm_o[i] = decay * stm[i] + lift * lefts[i]
        fresh = wr_mine[i] - move * moves[i]
        nr_o[i] = fresh
        nr_low[i] = fresh.astype(bf16)
    store(gr_o, gr_hbm)
    store(lm_o, lm_hbm)
    store(nr_o, nr_hbm)
    store(nr_low, nr_low_hbm)

    gt = grads(seg_a + 2 * finp, classp)
    full[1] = nn(flip(gt), gt)
    count = sts.shape[1]
    mine = pl.ds(pl.multiple_of(part * count, count), count)
    for i, product in enumerate((full[0, mine, :], rights[0], rights[1], full[1, mine, :])):
        ls_o[i] = decay * sts[i] + lift * product
    store(ls_o, ls_hbm)
    lh_o[...] = decay * sth[...] + lift * nt(gt, gt)[0:classes, 0:classes]
    root = rts[3, mine, :]
    high = root.astype(bf16)
    low = (root - high.astype(f32)).astype(bf16)
    left = (nt(gt, high) + nt(gt, low))[0:classes]
    step = three_dot(rth[...], left)
    gt_mine = jnp.zeros((classes, count), f32)
    wt_mine = jnp.zeros((classes, count), f32)
    gt_wide = gt.astype(f32)
    for i in range(hidden // count):
        here = slice(i * count, (i + 1) * count)
        gt_mine = jnp.where(part == i, gt_wide[0:classes, here], gt_mine)
        wt_mine = jnp.where(part == i, wht[:, here], wt_mine)
    gh_o[...] = gt_mine * scale
    fresh = wt_mine - move * step
    nh_o[...] = fresh
    nh_low[...] = fresh.astype(bf16)

    lines = grads(seg_a + 2 * finp + classp, 16).astype(f32)
    gb[0:1, 0:hidden] = grads(seg_a + finp - 16, 16).astype(f32)[fin - finp + 16 : fin - finp + 17, :]
    for i in range(1, 4):
        gb[0:1, i * hidden : (i + 1) * hidden] = lines[i : i + 1, :]
    size = bias.shape[0]
    g = gb[0:1, 0:size] * scale
    bias = bias[...].reshape(1, size)
    new_m = beta_one * bm[...].reshape(1, size) + (1.0 - beta_one) * g
    new_v = beta_two * bv[...].reshape(1, size) + (1.0 - beta_two) * g * g
    m_hat = new_m / (1.0 - beta_one**STEP)
    v_hat = new_v / (1.0 - beta_two**STEP)
    m_o[...] = new_m.reshape(size)
    v_o[...] = new_v.reshape(size)
    fresh = bias - bias_rate * (m_hat / (jnp.sqrt(v_hat) + adam_eps) + weight_decay * bias)
    nb_o[...] = fresh.reshape(size)
    for copy in stores:
        copy.wait()


def updates(fin, summed, wht, bias, st1, rt1, stm, sts, rts, sth, rth, bm, bv):
    hidden = wht.shape[1]
    classes = wht.shape[0]
    count = sts.shape[1]
    n1 = (st1.shape[0], hidden)
    nr = (2, stm.shape[1], hidden)
    nh = (classes, count)

    def of(shape, kind=f32):
        return jax.ShapeDtypeStruct(shape, kind)

    def room(a):
        return pltpu.VMEM(a.shape, a.dtype)

    one = of((1, 1))
    line = of(bias.shape)
    small = [one, one, one, of(nh), line, line, of(sth.shape), of(nh), line, of(nh, bf16)]
    large = [of(n1), of(nr), of(st1.shape), of(stm.shape), of(sts.shape), of(n1), of(nr), of(n1, bf16), of(nr, bf16)]
    loaded = [st1, rt1, stm, sts, rts]
    inside = pl.BlockSpec(memory_space=pltpu.VMEM)
    outside = pl.BlockSpec(memory_space=pl.ANY)
    (loss, total, norm, gh, m, v, lh, nh_new, nb, nh_low, g1, gr, l1, lm, ls, n1_new, nr_new, n1_low, nr_low) = pl.pallas_call(
        functools.partial(update_kernel, fin),
        out_shape=tuple(small + large),
        in_specs=[inside] * (6 + len(summed) + len(loaded)),
        out_specs=(inside,) * len(small) + (outside,) * len(large),
        scratch_shapes=[room(a) for a in large] + [
            pltpu.VMEM((2 * fin, hidden), f32),
            pltpu.VMEM(n1, f32),
            pltpu.VMEM((2, hidden, hidden), f32),
            pltpu.VMEM((1, 4 * hidden), f32),
            pltpu.SemaphoreType.DMA((len(large),)),
        ],
        compiler_params=pltpu.CompilerParams(vmem_limit_bytes=40 * 2**20),
        name="update_step",
    )(*summed, wht, bias, sth, rth, bm, bv, *loaded)
    return [
        loss, total, norm, g1, gr, gh, m, v, l1, lm, ls, lh, n1_new, nr_new, nh_new, nb, n1_low, nr_low, nh_low
    ]


def shards(
    features, nbr_index, nbr_mask, send_rows, send_count, labels, seed_mask,
    w_first, w_rest, w_head, biases,
    stat_big, root_big, stat_mid, root_mid, stat_sq, root_sq, stat_hr, root_hr, bias_m, bias_v,
):
    peers = send_rows.shape[2]
    cap = send_rows.shape[3]
    fin = features.shape[2]
    fan = nbr_index.shape[3]
    seeds = labels.shape[1]

    def lines(a):
        return jnp.transpose(a, (1, 3, 0, 2))

    summed = summed_gradients(
        peers, cap, seeds, fan,
        lines(nbr_index), lines(nbr_mask), jnp.swapaxes(features[0], 0, 1), w_first, w_rest,
        send_rows[0, 0], send_count[0], labels, seed_mask, w_head.T, biases, root_mid, root_sq,
    )
    out = list(
        updates(
            fin, summed, w_head.T, biases,
            stat_big, root_big, stat_mid, stat_sq, root_sq, stat_hr, root_hr,
            bias_m, bias_v,
        )
    )
    for i in (0, 1, 2):
        out[i] = out[i].reshape(())
    for i in (5, 14, 18):
        out[i] = out[i].T
    return tuple(out)


highest = lax.Precision.HIGHEST


def plain_activate(z):
    act = jax.nn.gelu(z, approximate=True)
    return act * lax.rsqrt(jnp.sum(act * act, axis=-1, keepdims=True) + norm_eps)


def plain_counts(nbr, mask, columns):
    nodes, slots = nbr.shape
    column_ids = jnp.arange(columns, dtype=jnp.int32)[None, :]
    mask_low = mask.astype(jnp.bfloat16)

    def add_slot(slot, total):
        picks = lax.dynamic_slice_in_dim(nbr, slot, 1, 1)
        weight = lax.dynamic_slice_in_dim(mask_low, slot, 1, 1)
        return total + (picks == column_ids).astype(jnp.bfloat16) * weight

    return lax.fori_loop(0, slots, add_slot, jnp.zeros((nodes, columns), jnp.bfloat16))


def plain_forward(h, weight, bias, nbr, mask, send_list, valid):
    nodes, width = h.shape
    hb = h.astype(jnp.bfloat16)
    outgoing = (
        jnp.take(hb, send_list, axis=0).reshape(valid.shape[0], valid.shape[1], width)
        * valid[:, :, None]
    )
    incoming = lax.all_to_all(outgoing, "dom", split_axis=0, concat_axis=0, tiled=True)
    table = jnp.concatenate([hb, incoming.reshape(-1, width)], axis=0)
    counts = plain_counts(nbr, mask, table.shape[0])
    degree = jnp.maximum(jnp.sum(mask, axis=1), 1).astype(jnp.float32)[:, None]
    gathered = jnp.dot(counts, table, preferred_element_type=jnp.float32)
    joined = jnp.concatenate([hb, (gathered / degree).astype(jnp.bfloat16)], axis=1)
    z = jnp.dot(joined, weight.astype(jnp.bfloat16), preferred_element_type=jnp.float32) + bias
    return (plain_activate(z), (joined, counts, degree, z))


def plain_backward(grad_out, weight, kept, send_list, valid, need_input):
    joined, counts, degree, z = kept
    nodes = joined.shape[0]
    width = joined.shape[1] // 2
    grad_z = jax.vjp(plain_activate, z)[1](grad_out)[0].astype(jnp.bfloat16)
    grad_w = jnp.einsum("nk,nh->kh", joined, grad_z, preferred_element_type=jnp.float32)
    grad_b = jnp.sum(grad_z.astype(jnp.float32), axis=0)
    if not need_input:
        return (grad_w, grad_b, None)
    grad_joined = jnp.einsum(
        "nh,kh->nk", grad_z, weight.astype(jnp.bfloat16), preferred_element_type=jnp.float32
    )
    grad_gathered = (grad_joined[:, width:] / degree).astype(jnp.bfloat16)
    grad_table = jnp.einsum("nj,nw->jw", counts, grad_gathered, preferred_element_type=jnp.float32)
    returned = (
        grad_table[nodes:].reshape(valid.shape[0], valid.shape[1], width).astype(jnp.bfloat16)
    )
    returned = lax.all_to_all(returned, "dom", split_axis=0, concat_axis=0, tiled=True)
    sent_back = (returned * valid[:, :, None]).reshape(-1, width)
    placement = (send_list[:, None] == jnp.arange(nodes, dtype=jnp.int32)[None, :]).astype(
        jnp.bfloat16
    )
    scattered = jnp.einsum("sn,sw->nw", placement, sent_back, preferred_element_type=jnp.float32)
    return (grad_w, grad_b, grad_joined[:, :width] + grad_table[:nodes] + scattered)


def plain_shampoo(grad, weight, left, left_root, right, right_root, part, right_split):
    count = left.shape[0]
    grad_rows = lax.dynamic_slice_in_dim(grad, part * count, count, 0)
    weight_rows = lax.dynamic_slice_in_dim(weight, part * count, count, 0)
    new_left = decay * left + (1.0 - decay) * jnp.dot(grad_rows, grad.T, precision=highest)
    if right_split:
        cols = right.shape[0]
        grad_cols = lax.dynamic_slice_in_dim(grad, part * cols, cols, 1)
        new_right = decay * right + (1.0 - decay) * jnp.dot(grad_cols.T, grad, precision=highest)
    else:
        new_right = decay * right + (1.0 - decay) * jnp.dot(grad.T, grad, precision=highest)
    step = jnp.dot(jnp.dot(left_root, grad, precision=highest), right_root, precision=highest)
    return (grad_rows, new_left, new_right, weight_rows - shampoo_rate * step)


def plain_shards(
    features,
    nbr_index,
    nbr_mask,
    send_rows,
    send_count,
    labels,
    seed_mask,
    w_first,
    w_rest,
    w_head,
    biases,
    stat_big,
    root_big,
    stat_mid,
    root_mid,
    stat_sq,
    root_sq,
    stat_hr,
    root_hr,
    bias_m,
    bias_v,
):
    hidden = w_rest.shape[2]
    peers = send_rows.shape[2]
    cap = send_rows.shape[3]
    send_list = send_rows.reshape(-1)
    valid = (jnp.arange(cap)[None, :] < send_count.reshape(peers, 1)).astype(jnp.bfloat16)
    weights = [w_first, w_rest[0], w_rest[1]]
    state = features[0].astype(jnp.float32)
    kept = []
    for level in range(3):
        state, saved = plain_forward(
            state,
            weights[level],
            biases[level * hidden : (level + 1) * hidden],
            nbr_index[0, level],
            nbr_mask[0, level],
            send_list,
            valid,
        )
        kept.append(saved)
    seeds = labels.shape[1]
    top = state[:seeds].astype(jnp.bfloat16)
    head_low_w = w_head.astype(jnp.bfloat16)
    logits = jnp.dot(top, head_low_w, preferred_element_type=jnp.float32) + biases[3 * hidden :]
    lse = jax.nn.logsumexp(logits, axis=1)
    onehot = (labels[0][:, None] == jnp.arange(logits.shape[1])[None, :]).astype(jnp.float32)
    picked = jnp.sum(logits * onehot, axis=1)
    seed_weight = seed_mask[0].astype(jnp.float32)
    loss_sum, seed_total = lax.psum(
        (jnp.sum((lse - picked) * seed_weight), jnp.sum(seed_weight)), ("dom", "rep")
    )
    grad_logits = (
        (jnp.exp(logits - lse[:, None]) - onehot) * (seed_weight / seed_total)[:, None]
    ).astype(jnp.bfloat16)
    grad_head = jnp.einsum("sh,sc->hc", top, grad_logits, preferred_element_type=jnp.float32)
    grad_hbias = jnp.sum(grad_logits.astype(jnp.float32), axis=0)
    grad_head, grad_hbias = (grad_head, grad_hbias)
    grad_top = jnp.einsum("sc,hc->sh", grad_logits, head_low_w, preferred_element_type=jnp.float32)
    grad_state = jnp.zeros(state.shape, jnp.float32).at[:seeds].set(grad_top)
    results = [None, None, None]
    for level in (2, 1, 0):
        grad_w, grad_b, grad_state = plain_backward(
            grad_state, weights[level], kept[level], send_list, valid, level > 0
        )
        results[level] = (grad_w, grad_b)
    grad_bias = jnp.concatenate([results[0][1], results[1][1], results[2][1], grad_hbias])
    grad_one, grad_two, grad_three = (results[0][0], results[1][0], results[2][0])
    grad_one, grad_two, grad_three, grad_head, grad_bias = lax.psum(
        (grad_one, grad_two, grad_three, grad_head, grad_bias), ("dom", "rep")
    )
    everything = (grad_one, grad_two, grad_three, grad_head, grad_bias)
    grad_norm = jnp.sqrt(sum((jnp.sum(g * g) for g in everything)))
    factor = clip_limit / jnp.maximum(grad_norm, clip_limit)
    grad_one, grad_two, grad_three, grad_head, grad_bias = [g * factor for g in everything]
    part = lax.axis_index("rep")
    head_rows = stat_sq.shape[1]
    head_root_rows = lax.dynamic_slice_in_dim(root_sq[3], part * head_rows, head_rows, 0)
    g_first, l_first, r_first, n_first = plain_shampoo(
        grad_one, w_first, stat_big, root_big, stat_sq[0], root_sq[0], part, True
    )
    g_mid0, l_mid0, r_mid0, n_mid0 = plain_shampoo(
        grad_two, w_rest[0], stat_mid[0], root_mid[0], stat_sq[1], root_sq[1], part, True
    )
    g_mid1, l_mid1, r_mid1, n_mid1 = plain_shampoo(
        grad_three, w_rest[1], stat_mid[1], root_mid[1], stat_sq[2], root_sq[2], part, True
    )
    g_head, l_head, r_head, n_head = plain_shampoo(
        grad_head, w_head, stat_sq[3], head_root_rows, stat_hr, root_hr, part, False
    )
    new_m = beta_one * bias_m + (1.0 - beta_one) * grad_bias
    new_v = beta_two * bias_v + (1.0 - beta_two) * grad_bias * grad_bias
    m_hat = new_m / (1.0 - beta_one**STEP)
    v_hat = new_v / (1.0 - beta_two**STEP)
    new_b = biases - bias_rate * (m_hat / (jnp.sqrt(v_hat) + adam_eps) + weight_decay * biases)
    new_rest = jnp.stack([n_mid0, n_mid1])
    return (
        loss_sum,
        seed_total,
        grad_norm,
        g_first,
        jnp.stack([g_mid0, g_mid1]),
        g_head,
        new_m,
        new_v,
        l_first,
        jnp.stack([l_mid0, l_mid1]),
        jnp.stack([r_first, r_mid0, r_mid1, l_head]),
        r_head,
        n_first,
        new_rest,
        n_head,
        new_b,
        n_first.astype(jnp.bfloat16),
        new_rest.astype(jnp.bfloat16),
        n_head.astype(jnp.bfloat16),
    )


def solution(mesh):
    placed = (
        P("rep", "dom", None),
        P("rep", None, "dom", None),
        P("rep", None, "dom", None),
        P("rep", "dom", None, None),
        P("rep", "dom", None),
        P("rep", "dom"),
        P("rep", "dom"),
        P(), P(), P(), P(),
        P("rep", None),
        P("rep", None),
        P(None, "rep", None),
        P(None, "rep", None),
        P(None, "rep", None),
        P(), P(), P(), P(), P(),
    )
    small = mesh.shape["rep"] == 4 and mesh.shape["dom"] == 8
    return jax.shard_map(
        shards if small else plain_shards,
        mesh=mesh,
        in_specs=placed,
        out_specs=(
            P(), P(), P(),
            P("rep", None), P(None, "rep", None), P("rep", None),
            P(), P(),
            P("rep", None), P(None, "rep", None), P(None, "rep", None), P(),
            P("rep", None), P(None, "rep", None), P("rep", None), P(),
            P("rep", None), P(None, "rep", None), P("rep", None),
        ),
        check_vma=False,
    )
```
